32 devices in a mesh: seq: 8 (over y, x, core), dp: 4 (over z).
Axes of the slice: x: 2, y: 2, z: 4, core: 2. Of those that a mesh axis runs over, the one named last changes fastest.
Arguments:
- inputs: bfloat16 [2, 64, 512, 512], P(None, 'seq', 'dp'), may hold values from -6 to 6
- cotangent: bfloat16 [2, 64, 512, 512], P(None, 'seq', 'dp'), may hold values from -6 to 6
- lengths: int32 [2, 64], P(None, 'seq'), may hold values from 64 to 512, as said below
- weights: float32 [48, 256, 256], P('dp', 'seq'), may hold values from -0.3005204 to 0.3005204
- vectors: float32 [6144], replicated, may hold values from -0.35 to 1.3
- positions: float32 [512, 512], P('dp'), may hold values from -3 to 3
- left_stats: float32 [48, 256, 256], P('dp', 'seq'), may hold values from -4.8828125e-05 to 0.00390625
- right_stats: float32 [48, 256, 256], P('dp', 'seq'), may hold values from -4.8828125e-05 to 0.00390625
- left_roots: float32 [48, 256, 256], P('dp', 'seq'), may hold values from -1.13137085 to 11.313708
- right_roots: float32 [48, 256, 256], P('dp', 'seq'), may hold values from -1.13137085 to 11.313708
- vector_second: float32 [6144], replicated, may hold values from 3.8146973e-06 to 1.5258789e-05
- position_second: float32 [512, 512], P('dp'), may hold values from 7.450581e-09 to 2.9802322e-08
Outputs:
- layer_out: bfloat16 [2, 64, 512, 512], P(None, 'seq', 'dp')
- input_grad: float32 [2, 64, 512, 512], P(None, 'seq', 'dp')
- block_grads: float32 [48, 256, 256], P('dp', 'seq')
- left_new: float32 [48, 256, 256], P('dp', 'seq')
- right_new: float32 [48, 256, 256], P('dp', 'seq')
- weights_new: float32 [48, 256, 256], P('dp', 'seq')
- vector_grads: float32 [6144], replicated
- vector_second_new: float32 [6144], replicated
- vectors_new: float32 [6144], replicated
- position_grads: float32 [512, 512], P('dp')
- position_second_new: float32 [512, 512], P('dp')
- positions_new: float32 [512, 512], P('dp')
The draws below stay inside these ranges and needn't reach their ends.
Inputs may be any that keep to these rules, and one draw needn't show every extreme that they name: `lengths`: for every index of seq, one of its 2 x 8 windows holds exactly 512 valid characters.
All inputs are finite; a program needn't handle non-finite values.
Results may differ from the reference program's by a relative error of at most 0.02.
The reference program's roundings to bfloat16 on the way count: a program that leaves them out, or rounds other values in their place, can miss the bound.
Values may be sent and summed in bfloat16 or wider, within the bound.
No kernel may reach another device: no remote copies, remote signals or barrier semaphores. Data moves between devices by JAX's collectives and lax.ppermute only.
A program may use at most 256 MiB of HBM per device.

```python
import math
import jax
import jax.numpy as jnp
from jax import lax

D = 512
HEADS = 8
FF = 2048
WIN = 512
BLK = 256
WPD = 8
NMB = 2
NWIN = 64
TOKENS = 65536
VEC = 6144
NBLK = 48


def place_diagonal(off_part, diagonal):
    marker = jnp.eye(BLK, dtype=jnp.bool_)
    return jnp.where(marker[None], diagonal[:, :, None], off_part)


def draw_lengths(key, part):
    key = jax.random.fold_in(key, 11)
    base_key, micro_key, window_key = jax.random.split(key, 3)
    base_lengths = jax.random.randint(base_key, (NMB, NWIN), WIN // 8, WIN + 1)
    group_count = NWIN // WPD
    chosen_micro = jax.random.randint(micro_key, (group_count,), 0, NMB)
    chosen_window = jax.random.randint(window_key, (group_count,), 0, WPD)
    indices = jnp.arange(NWIN)
    owner = indices // WPD
    hit_rows = jnp.arange(NMB)[:, None] == chosen_micro[owner][None, :]
    hit_cols = indices % WPD == chosen_window[owner]
    return jnp.where(hit_rows & hit_cols[None, :], WIN, base_lengths).astype(jnp.int32)


def draw_weights(key, part):
    key = jax.random.fold_in(key, 23)
    square = (D // BLK) ** 2
    wide = D // BLK * (FF // BLK)
    indices = jnp.arange(NBLK)
    block_scale = jnp.where(indices < 3 * square, D ** (-0.5), jnp.where(indices < 4 * square, 4.0 * D ** (-0.5), jnp.where(indices < 4 * square + wide, D ** (-0.5), FF ** (-0.5))))
    uniform_draw = jax.random.uniform(key, (NBLK, BLK, BLK), jnp.float32, -1.0, 1.0)
    shaped = 1.7 * uniform_draw
    return (shaped * block_scale[:, None, None]).astype(jnp.float32)


def draw_vectors(key, part):
    key = jax.random.fold_in(key, 53)
    uniform_draw = jax.random.uniform(key, (VEC,), jnp.float32, -1.0, 1.0)
    indices = jnp.arange(VEC)
    offset_base = 4 * D + FF
    gain_mask = (indices >= offset_base) & (indices < offset_base + D) | (indices >= offset_base + 2 * D) & (indices < offset_base + 3 * D)
    return jnp.where(gain_mask, 1.0 + 0.3 * uniform_draw, 0.35 * uniform_draw).astype(jnp.float32)


def statistic_parts(key, level, low_log, high_log):
    diagonal_key, off_key = jax.random.split(key)
    diagonal = level * jnp.exp(jax.random.uniform(diagonal_key, (NBLK, BLK), jnp.float32, low_log, high_log))
    off_draw = jax.random.uniform(off_key, (NBLK, BLK, BLK), jnp.float32, -1.0, 1.0)
    return (off_draw, diagonal)


def draw_left_stats(key, part):
    key = jax.random.fold_in(key, 31)
    level = 0.25 * BLK / TOKENS
    off_draw, diagonal = statistic_parts(key, level, 0.0, math.log(4.0))
    return place_diagonal(0.0125 * level * off_draw, diagonal).astype(jnp.float32)


def draw_right_stats(key, part):
    key = jax.random.fold_in(key, 37)
    level = 0.25 * BLK / TOKENS
    off_draw, diagonal = statistic_parts(key, level, 0.0, math.log(4.0))
    return place_diagonal(0.0125 * level * off_draw, diagonal).astype(jnp.float32)


def draw_left_roots(key, part):
    key = jax.random.fold_in(key, 41)
    level = (0.25 * BLK / TOKENS) ** (-0.25)
    off_draw, diagonal = statistic_parts(key, level, math.log(0.5), math.log(2.0))
    return place_diagonal(0.87 * BLK ** (-0.5) * level * off_draw, diagonal).astype(jnp.float32)


def draw_right_roots(key, part):
    key = jax.random.fold_in(key, 43)
    level = (0.25 * BLK / TOKENS) ** (-0.25)
    off_draw, diagonal = statistic_parts(key, level, math.log(0.5), math.log(2.0))
    return place_diagonal(0.87 * BLK ** (-0.5) * level * off_draw, diagonal).astype(jnp.float32)


def shard_levels(stream_key, dims, cuts, low, high):
    def one(dim, parts):
        draws = jax.random.uniform(jax.random.fold_in(jax.random.fold_in(stream_key, 6), dim), (parts,), jnp.float32, low / len(cuts), high / len(cuts))
        return jnp.repeat(jnp.exp(draws), dims[dim] // parts).reshape((-1,) + (1,) * (len(dims) - dim - 1))

    level = one(*cuts[0])
    for cut in cuts[1:]:
        level = level * one(*cut)
    return level


def scatter_about(rng, extent, width, most, cuts=(), kind=jnp.bfloat16):
    values = width * jax.random.normal(rng, extent, jnp.float32)
    if cuts:
        values = values * shard_levels(rng, extent, cuts, -0.22, 0.18)
    return jnp.clip(values, -most, most).astype(kind)


def setup_inputs(seed: int = 0) -> dict:
    splits = jax.random.split(jax.random.key(seed), 13)
    inputs = scatter_about(splits[0], (NMB, NWIN, WIN, D), 1.0, 6.0, ((1, 8), (2, 4)))
    cotangent = scatter_about(splits[1], (NMB, NWIN, WIN, D), 1.0, 6.0, ((1, 8), (2, 4)))
    lengths = draw_lengths(jax.random.fold_in(splits[12], 71), 0)
    weights = draw_weights(jax.random.fold_in(splits[12], 71), 0)
    vectors = draw_vectors(jax.random.fold_in(splits[12], 71), 0)
    positions = scatter_about(splits[5], (WIN, D), 0.5, 3.0, ((0, 4),), jnp.float32)
    left_stats = draw_left_stats(jax.random.fold_in(splits[12], 71), 0)
    right_stats = draw_right_stats(jax.random.fold_in(splits[12], 71), 0)
    left_roots = draw_left_roots(jax.random.fold_in(splits[12], 71), 0)
    right_roots = draw_right_roots(jax.random.fold_in(splits[12], 71), 0)
    vector_second = jnp.clip(jnp.exp(jax.random.uniform(splits[10], (VEC,), jnp.float32, math.log(3.814697265625e-06), math.log(1.52587890625e-05))), 3.814697265625e-06, 1.52587890625e-05)
    position_second = jnp.clip(jnp.exp(math.log(2.9802322387695312e-08) - 1.3862944 * jax.random.uniform(splits[11], (WIN, D), jnp.float32) ** shard_levels(splits[11], (WIN, D), ((0, 4),), -0.2, 0.2)), 7.450580596923828e-09, 2.9802322387695312e-08)
    return dict(inputs=inputs, cotangent=cotangent, lengths=lengths, weights=weights, vectors=vectors, positions=positions, left_stats=left_stats, right_stats=right_stats, left_roots=left_roots, right_roots=right_roots, vector_second=vector_second, position_second=position_second)


NORM_EPS = 1e-05
ROOT_EPS = 1e-08
DECAY = 0.5
MATRIX_RATE = 0.5
VECTOR_RATE = 0.2
MASKED = -1e+30

@jax.custom_vjp
def low(v):
    return lax.optimization_barrier(v.astype(jnp.bfloat16)).astype(jnp.float32)

@jax.custom_vjp
def low_back(v):
    return v

def low_keep(v):
    return (low(v), None)

def low_pass(kept, grad):
    return (grad,)

def back_keep(v):
    return (v, None)

def back_low(kept, grad):
    return (low(grad),)
low.defvjp(low_keep, low_pass)
low_back.defvjp(back_keep, back_low)

def low_both(values):
    return low_back(low(values))

def layer_norm(values, gain, shift):
    centered = values - lax.optimization_barrier(jnp.mean(values, axis=-1, keepdims=True))
    spread = lax.optimization_barrier(jnp.mean(centered * centered, axis=-1, keepdims=True))
    return centered * lax.rsqrt(spread + NORM_EPS) * gain + shift

def to_blocks(matrix, block_size):
    rows, cols = matrix.shape
    grid = matrix.reshape(rows // block_size, block_size, cols // block_size, block_size)
    return grid.transpose(0, 2, 1, 3).reshape(-1, block_size, block_size)

def from_blocks(block_stack, rows, cols):
    block_size = block_stack.shape[-1]
    grid = block_stack.reshape(rows // block_size, cols // block_size, block_size, block_size)
    return grid.transpose(0, 2, 1, 3).reshape(rows, cols)

def project(values, matrix):
    return jnp.einsum('gpd,de->gpe', values, matrix, precision=lax.Precision.HIGHEST)

def window_forward(params, tokens_in, window_lengths):
    w_query, w_key, w_value, w_out, w_up, w_down, vector_pack, position_table = params
    model_width = w_query.shape[0]
    hidden = w_up.shape[1]
    head_dim = model_width // HEADS
    offset_base = 3 * model_width + hidden
    bias_query = vector_pack[0:model_width]
    bias_value = vector_pack[model_width:2 * model_width]
    bias_out = vector_pack[2 * model_width:3 * model_width]
    bias_up = vector_pack[3 * model_width:offset_base]
    bias_down = vector_pack[offset_base:offset_base + model_width]
    gain_one = vector_pack[offset_base + model_width:offset_base + 2 * model_width]
    shift_one = vector_pack[offset_base + 2 * model_width:offset_base + 3 * model_width]
    gain_two = vector_pack[offset_base + 3 * model_width:offset_base + 4 * model_width]
    shift_two = vector_pack[offset_base + 4 * model_width:offset_base + 5 * model_width]
    group_count = tokens_in.shape[0]
    window = tokens_in.shape[1]
    highest = lax.Precision.HIGHEST
    start_vals = tokens_in + position_table[None]
    start_low = low(start_vals)
    queries = low_both(project(start_low, low(w_query)) + bias_query).reshape(group_count, window, HEADS, head_dim)
    key_rows = low_both(project(start_low, low(w_key))).reshape(group_count, window, HEADS, head_dim)
    values = low_both(project(start_low, low(w_value)) + bias_value).reshape(group_count, window, HEADS, head_dim)
    scores = low_back(jnp.einsum('gqhd,gkhd->ghqk', queries, key_rows, precision=highest) * head_dim ** (-0.5))
    places = jnp.arange(window, dtype=jnp.int32)
    causal = places[None, :] <= places[:, None]
    allowed = causal[None, None] & (places[None, None, None, :] < window_lengths[:, None, None, None])
    masked = jnp.where(allowed, scores, MASKED)
    row_top = lax.optimization_barrier(jnp.max(masked, axis=-1, keepdims=True))
    expo_terms = jnp.exp(masked - row_top)
    attn_probs = expo_terms / lax.optimization_barrier(jnp.sum(expo_terms, axis=-1, keepdims=True))
    attended = jnp.einsum('ghqk,gkhd->gqhd', low(attn_probs), values, precision=highest)
    attended = low_both(attended.reshape(group_count, window, model_width))
    mixed_rows = start_vals + low_back(project(attended, low(w_out)) + bias_out)
    normed = layer_norm(mixed_rows, gain_one, shift_one)
    up_rows = low_back(project(low(normed), low(w_up)) + bias_up)
    activated = jax.nn.gelu(up_rows, approximate=False)
    summed = normed + low_back(project(low(activated), low(w_down)) + bias_down)
    return layer_norm(summed, gain_two, shift_two)

def reference(inputs, cotangent, lengths, weights, vectors, positions, left_stats, right_stats, left_roots, right_roots, vector_second, position_second):
    square = (D // BLK) ** 2
    wide = D // BLK * (FF // BLK)
    w_query = from_blocks(weights[0:square], D, D)
    w_key = from_blocks(weights[square:2 * square], D, D)
    w_value = from_blocks(weights[2 * square:3 * square], D, D)
    w_out = from_blocks(weights[3 * square:4 * square], D, D)
    w_up = from_blocks(weights[4 * square:4 * square + wide], D, FF)
    w_down = from_blocks(weights[4 * square + wide:], FF, D)
    params = (w_query, w_key, w_value, w_out, w_up, w_down, vectors, positions)
    group_size = math.gcd(NMB * NWIN, max(1, 4096 // WIN))
    step_count = NMB * NWIN // group_size
    token_groups = inputs.reshape(step_count, group_size, WIN, D)
    cot_groups = cotangent.reshape(step_count, group_size, WIN, D)
    length_groups = lengths.reshape(step_count, group_size)
    places = jnp.arange(WIN, dtype=jnp.int32)

    def visit(totals, item):
        token_rows, cot_rows, window_lengths = item

        def local_forward(params_in, tokens_in):
            return window_forward(params_in, tokens_in, window_lengths)
        result, pull_back = jax.vjp(local_forward, params, token_rows.astype(jnp.float32))
        valid = (places[None, :] < window_lengths[:, None]).astype(jnp.float32)
        seed_grad = cot_rows.astype(jnp.float32) * valid[:, :, None] / TOKENS
        grads, input_rows = pull_back(seed_grad)
        totals = jax.tree.map(lambda left_part, right_part: left_part + right_part, totals, grads)
        return (totals, (result.astype(jnp.bfloat16), input_rows))
    zero_grads = jax.tree.map(jnp.zeros_like, params)
    totals, (layer_rows, grad_rows) = lax.scan(visit, zero_grads, (token_groups, cot_groups, length_groups))
    grad_query, grad_key, grad_value, grad_out, grad_up, grad_down, grad_vectors, grad_positions = totals
    block_grads = jnp.concatenate([to_blocks(grad_query, BLK), to_blocks(grad_key, BLK), to_blocks(grad_value, BLK), to_blocks(grad_out, BLK), to_blocks(grad_up, BLK), to_blocks(grad_down, BLK)], axis=0)
    highest = lax.Precision.HIGHEST
    left_new = DECAY * left_stats + (1.0 - DECAY) * jnp.einsum('bij,bkj->bik', block_grads, block_grads, precision=highest)
    right_new = DECAY * right_stats + (1.0 - DECAY) * jnp.einsum('bki,bkj->bij', block_grads, block_grads, precision=highest)
    left_applied = jnp.einsum('bij,bjk->bik', left_roots, block_grads, precision=highest)
    step_blocks = jnp.einsum('bij,bjk->bik', left_applied, right_roots, precision=highest)
    weights_new = weights - MATRIX_RATE * step_blocks
    vector_second_new = DECAY * vector_second + (1.0 - DECAY) * grad_vectors * grad_vectors
    vectors_new = vectors - VECTOR_RATE * grad_vectors / (jnp.sqrt(vector_second_new) + ROOT_EPS)
    position_second_new = DECAY * position_second + (1.0 - DECAY) * grad_positions * grad_positions
    positions_new = positions - VECTOR_RATE * grad_positions / (jnp.sqrt(position_second_new) + ROOT_EPS)
    layer_out = layer_rows.reshape(NMB, NWIN, WIN, D)
    input_grad = grad_rows.reshape(NMB, NWIN, WIN, D)
    return (layer_out, input_grad, block_grads, left_new, right_new, weights_new, grad_vectors, vector_second_new, vectors_new, grad_positions, position_second_new, positions_new)
```

```python
import functools

import jax
import jax.numpy as jnp
from jax import lax
from jax.experimental import pallas as pl
from jax.experimental.pallas import tpu as pltpu
from jax.sharding import PartitionSpec as P

HEADS = 8
FF = 2048
WIN = 512
D = 512
BLK = 256
QKV_BLOCKS = 12
REST_BLOCKS = 36
HEAD_DIM = D // HEADS
PAIR = 2 * HEAD_DIM
PAIRS = HEADS // 2
FF_CHUNKS = FF // BLK
ROWS_VEC = 16

NORM_EPS = 1e-05
ROOT_EPS = 1e-08
DECAY = 0.5
MATRIX_RATE = 0.5
VECTOR_RATE = 0.2
MASKED = -1e30
SCALE = HEAD_DIM ** (-0.5)
ROOT_HALF = 0.7071067811865476
DENSITY = 0.3989422804014327

F32 = jnp.float32
BF16 = jnp.bfloat16


def dot_nn(left, right):
    return lax.dot_general(left, right, (((1,), (0,)), ((), ())), preferred_element_type=F32)


def dot_nt(left, right):
    return lax.dot_general(left, right, (((1,), (1,)), ((), ())), preferred_element_type=F32)


def load_segments(dst, lead, parts, me, seg):
    for s, part in enumerate(parts):
        rows = pl.ds(pl.multiple_of((me ^ s) * seg, seg), seg)
        if lead:
            dst[0, rows, :] = part[0]
        else:
            dst[rows, :] = part[0]


def fill_qkv_matrix(full, stack):
    side = D // BLK
    for b in range(QKV_BLOCKS):
        m, i, j = b // (side * side), (b // side) % side, b % side
        full[BLK * i : BLK * (i + 1), D * m + BLK * j : D * m + BLK * (j + 1)] = stack[b]


def fill_mask(mask, length):
    for i in range(WIN // BLK):
        keys = lax.broadcasted_iota(jnp.int32, (BLK, WIN), 0) + BLK * i
        queries = lax.broadcasted_iota(jnp.int32, (BLK, WIN), 1)
        keep = (keys <= queries) & (keys < length)
        mask[BLK * i : BLK * (i + 1), :] = jnp.where(keep, 0.0, MASKED).astype(F32)


def half_marks():
    lane = lax.broadcasted_iota(jnp.int32, (1, PAIR), 1)
    low = jnp.where(lane < HEAD_DIM, 1.0, 0.0)
    return (low.astype(BF16), (1.0 - low).astype(BF16))


def attention_kernel(dp, seg, meta, *refs):
    parts = refs[:dp]
    stack, bias, h_ref, qkv_ref, o_ref, lse_ref, full, mask = refs[dp:]
    step = pl.program_id(0)
    me = meta[0]

    @pl.when(step == 0)
    def _():
        fill_qkv_matrix(full, stack)

    load_segments(h_ref, True, parts, me, seg)
    hidden = h_ref[0]
    for m in range(3):
        cols = slice(D * m, D * (m + 1))
        rows = dot_nn(hidden, full[:, cols])
        if m != 1:
            rows = rows + bias[(m // 2) : (m // 2) + 1, :]
        qkv_ref[0, :, cols] = rows.astype(BF16)
    fill_mask(mask, meta[1 + step])
    marks = half_marks()
    for p in range(PAIRS):
        at = PAIR * p
        q8 = qkv_ref[0, :, at : at + PAIR] * jnp.asarray(SCALE, BF16)
        key = qkv_ref[0, :, D + at : D + at + PAIR]
        val_t = jnp.transpose(qkv_ref[0, :, 2 * D + at : 2 * D + at + PAIR])
        pieces = []
        for h in range(2):
            key_h = key * marks[h]
            row = 2 * p + h
            blocks = []
            for qb in range(WIN // BLK):
                cols = slice(BLK * qb, BLK * (qb + 1))
                span = BLK * (qb + 1)
                s_t = dot_nt(key_h[:span], q8[cols]) + mask[:span, cols]
                top = jnp.max(s_t, axis=0, keepdims=True)
                expo = jnp.exp(s_t - top)
                total = jnp.sum(expo, axis=0, keepdims=True)
                probs = (expo * (1.0 / total)).astype(BF16)
                lse_ref[0, row : row + 1, cols] = top + jnp.log(total)
                blocks.append(dot_nn(val_t[HEAD_DIM * h : HEAD_DIM * (h + 1), :span], probs))
            pieces.append(jnp.concatenate(blocks, axis=1))
        o_t = jnp.concatenate(pieces, axis=0)
        o_ref[0, :, at : at + PAIR] = jnp.transpose(o_t).astype(BF16)


def attention_back_kernel(dp, seg, first, meta, *refs):
    stack, h_ref, qkv_ref, do_ref, lse_ref, da_ref = refs[:6]
    refs = refs[6:]
    if not first:
        prev, refs = refs[0], refs[1:]
    dx_refs, refs = refs[:dp], refs[dp:]
    dw_ref, db_ref, full, mask, dqkv, acc, dx = refs
    step = pl.program_id(0)
    me = meta[0]
    side = D // BLK

    @pl.when(step == 0)
    def _():
        fill_qkv_matrix(full, stack)
        if first:
            acc[...] = jnp.zeros_like(acc)
        else:
            for b in range(QKV_BLOCKS):
                m, i, j = b // (side * side), (b // side) % side, b % side
                acc[BLK * i : BLK * (i + 1), D * m + BLK * j : D * m + BLK * (j + 1)] = prev[
                    b
                ].astype(F32)
        db_ref[...] = jnp.zeros_like(db_ref)

    fill_mask(mask, meta[1 + step])
    marks = half_marks()
    for p in range(PAIRS):
        at = PAIR * p
        q8 = qkv_ref[0, :, at : at + PAIR] * jnp.asarray(SCALE, BF16)
        key = qkv_ref[0, :, D + at : D + at + PAIR]
        val = qkv_ref[0, :, 2 * D + at : 2 * D + at + PAIR]
        d_o = do_ref[0, :, at : at + PAIR]
        key_t = jnp.transpose(key)
        dq_pieces, dk_pieces, dv_pieces = [], [], []
        for h in range(2):
            key_h = key * marks[h]
            val_h = val * marks[h]
            row = 2 * p + h
            dq_blocks = []
            dk_sum, dv_sum = None, None
            for qb in reversed(range(WIN // BLK)):
                cols = slice(BLK * qb, BLK * (qb + 1))
                span = BLK * (qb + 1)
                s_t = dot_nt(key_h[:span], q8[cols]) + mask[:span, cols]
                probs = jnp.exp(s_t - lse_ref[0, row : row + 1, cols])
                d_probs = dot_nt(val_h[:span], d_o[cols])
                delta = jnp.sum(probs * d_probs, axis=0, keepdims=True)
                d_s = (probs * (d_probs - delta)).astype(BF16)
                dv_part = dot_nn(probs.astype(BF16), d_o[cols])
                dk_part = dot_nn(d_s, q8[cols])
                dq_blocks.append(dot_nn(key_t[HEAD_DIM * h : HEAD_DIM * (h + 1), :span], d_s))
                if dv_sum is None:
                    dv_sum, dk_sum = dv_part, dk_part
                else:
                    dv_sum = jnp.concatenate([dv_sum[:span] + dv_part, dv_sum[span:]], axis=0)
                    dk_sum = jnp.concatenate([dk_sum[:span] + dk_part, dk_sum[span:]], axis=0)
            dq_pieces.append(jnp.concatenate(dq_blocks[::-1], axis=1))
            dk_pieces.append(dk_sum)
            dv_pieces.append(dv_sum)
        lane = lax.broadcasted_iota(jnp.int32, (WIN, PAIR), 1) < HEAD_DIM
        dq = jnp.transpose(jnp.concatenate(dq_pieces, axis=0)) * SCALE
        dk = jnp.where(lane, dk_pieces[0], dk_pieces[1])
        dv = jnp.where(lane, dv_pieces[0], dv_pieces[1])
        dqkv[:, at : at + PAIR] = dq.astype(BF16)
        dqkv[:, D + at : D + at + PAIR] = dk.astype(BF16)
        dqkv[:, 2 * D + at : 2 * D + at + PAIR] = dv.astype(BF16)
    h_t = jnp.transpose(h_ref[0])
    for m in range(3):
        cols = slice(D * m, D * (m + 1))
        rows = dqkv[:, cols]
        acc[:, cols] += dot_nn(h_t, rows)
        if m != 1:
            db_ref[(m // 2) : (m // 2) + 1, :] += jnp.sum(
                rows.astype(F32), axis=0, keepdims=True
            )
    total = da_ref[0]
    for m in range(3):
        cols = slice(D * m, D * (m + 1))
        total = total + dot_nt(dqkv[:, cols], full[:, cols])
    dx[...] = total.astype(BF16)
    for s in range(dp):
        dx_refs[s][0] = dx[pl.ds(pl.multiple_of((me ^ s) * seg, seg), seg), :]

    @pl.when(step == pl.num_programs(0) - 1)
    def _():
        for b in range(QKV_BLOCKS):
            m, i, j = b // (side * side), (b // side) % side, b % side
            dw_ref[b] = acc[
                BLK * i : BLK * (i + 1), D * m + BLK * j : D * m + BLK * (j + 1)
            ].astype(BF16)


def normal_parts(u):
    size = jnp.abs(u)
    t = 1.0 / (1.0 + (0.3275911 * ROOT_HALF) * size)
    expo = jnp.exp(-0.5 * (u * u))
    poly = t * (
        0.5 * 0.254829592
        + t
        * (
            -0.5 * 0.284496736
            + t * (0.5 * 1.421413741 + t * (-0.5 * 1.453152027 + t * (0.5 * 1.061405429)))
        )
    )
    tail = poly * expo
    return jnp.where(u >= 0.0, 1.0 - tail, tail), expo


def norm_stats(rows):
    mean = jnp.mean(rows, axis=1, keepdims=True)
    centered = rows - mean
    spread = jnp.mean(centered * centered, axis=1, keepdims=True)
    inverse = lax.rsqrt(spread + NORM_EPS)
    return centered * inverse, inverse


def norm_back(d_rows, normal, inverse):
    mean_d = jnp.mean(d_rows, axis=1, keepdims=True)
    mean_dn = jnp.mean(d_rows * normal, axis=1, keepdims=True)
    return inverse * (d_rows - mean_d - normal * mean_dn)


def ffn_kernel(dp, seg, tokens, first, meta, *refs):
    cots, refs = refs[:dp], refs[dp:]
    h_ref, o_ref, stack, vec = refs[:4]
    refs = refs[4:]
    if not first:
        prev, refs = refs[0], refs[1:]
    out_refs, refs = refs[:dp], refs[dp:]
    da_ref, do_ref, dw_ref, vg_ref, acc, z_ref, gp_ref, buf, w_out = refs
    step = pl.program_id(0)
    me = meta[0]
    length = meta[1 + step]
    side = D // BLK
    up_at = side * side
    down_at = up_at + side * FF_CHUNKS

    @pl.when(step == 0)
    def _():
        for b in range(side * side):
            i, j = b // side, b % side
            w_out[BLK * i : BLK * (i + 1), BLK * j : BLK * (j + 1)] = stack[b]
        for b in range(REST_BLOCKS):
            if first:
                acc[b] = jnp.zeros((BLK, BLK), F32)
            elif b >= down_at:
                acc[b] = jnp.transpose(prev[b].astype(F32))
            else:
                acc[b] = prev[b].astype(F32)
        vg_ref[...] = jnp.zeros_like(vg_ref)

    def add_row(row, values, at=0):
        vg_ref[row : row + 1, at : at + values.shape[1]] += jnp.sum(
            values.astype(F32), axis=0, keepdims=True
        )

    bias_out, bias_down = vec[2:3, :], vec[7:8, :]
    gain_one, shift_one = vec[8:9, :], vec[9:10, :]
    gain_two, shift_two = vec[10:11, :], vec[11:12, :]
    attended = o_ref[0]
    mixed = h_ref[0].astype(F32) + (dot_nn(attended, w_out[...]) + bias_out)
    n_one, inv_one = norm_stats(mixed)
    normed = n_one * gain_one + shift_one
    normed_low = normed.astype(BF16)
    summed = normed + bias_down
    left, right = normed_low[:, :BLK], normed_low[:, BLK:]
    f_parts = [summed[:, :BLK], summed[:, BLK:]]
    for c in range(FF_CHUNKS):
        cols = slice(BLK * c, BLK * (c + 1))
        bias_up = vec[3 + c // 2 : 4 + c // 2, BLK * (c % 2) : BLK * (c % 2) + BLK]
        u = dot_nn(left, stack[up_at + c]) + dot_nn(right, stack[up_at + FF_CHUNKS + c]) + bias_up
        phi, expo = normal_parts(u)
        z = (u * phi).astype(BF16)
        z_ref[:, cols] = z
        gp_ref[:, cols] = phi + (u * expo) * DENSITY
        for j in range(side):
            f_parts[j] = f_parts[j] + dot_nn(z, stack[down_at + side * c + j])
    n_two, inv_two = norm_stats(jnp.concatenate(f_parts, axis=1))
    buf[...] = (n_two * gain_two + shift_two).astype(BF16)
    for s in range(dp):
        out_refs[s][0] = buf[pl.ds(pl.multiple_of((me ^ s) * seg, seg), seg), :]

    load_segments(buf, False, cots, me, seg)
    places = lax.broadcasted_iota(jnp.int32, (WIN, 1), 0)
    valid = jnp.where(places < length, 1.0 / tokens, 0.0).astype(F32)
    seed = buf[...].astype(F32) * valid
    add_row(10, seed * n_two)
    add_row(11, seed)
    d_summed = norm_back(seed * gain_two, n_two, inv_two)
    d_ff = d_summed.astype(BF16)
    add_row(7, d_ff)
    d_ff_t = jnp.transpose(d_ff)
    normed_t = jnp.transpose(normed_low)
    d_left, d_right = d_ff[:, :BLK], d_ff[:, BLK:]
    d_normed = [d_summed[:, :BLK], d_summed[:, BLK:]]
    for c in range(FF_CHUNKS):
        cols = slice(BLK * c, BLK * (c + 1))
        d_z = dot_nt(d_left, stack[down_at + side * c]) + dot_nt(
            d_right, stack[down_at + side * c + 1]
        )
        d_u = (d_z * gp_ref[:, cols]).astype(BF16)
        add_row(3 + c // 2, d_u, BLK * (c % 2))
        z = z_ref[:, cols]
        for j in range(side):
            rows = slice(BLK * j, BLK * (j + 1))
            acc[down_at + side * c + j] += dot_nn(d_ff_t[rows], z)
            acc[up_at + FF_CHUNKS * j + c] += dot_nn(normed_t[rows], d_u)
            d_normed[j] = d_normed[j] + dot_nt(d_u, stack[up_at + FF_CHUNKS * j + c])
    d_norm_rows = jnp.concatenate(d_normed, axis=1)
    add_row(8, d_norm_rows * n_one)
    add_row(9, d_norm_rows)
    d_mixed = norm_back(d_norm_rows * gain_one, n_one, inv_one)
    da_ref[0] = d_mixed
    d_branch = d_mixed.astype(BF16)
    add_row(2, d_branch)
    o_t = jnp.transpose(attended)
    for i in range(side):
        for j in range(side):
            acc[side * i + j] += dot_nn(
                o_t[BLK * i : BLK * (i + 1)], d_branch[:, BLK * j : BLK * (j + 1)]
            )
    do_ref[0] = dot_nt(d_branch, w_out[...]).astype(BF16)

    @pl.when(step == pl.num_programs(0) - 1)
    def _():
        for b in range(REST_BLOCKS):
            block = acc[b]
            if b >= down_at:
                block = jnp.transpose(block)
            dw_ref[b] = block.astype(BF16)


def whole_spec(shape, single=True):
    zeros = (0,) * len(shape)
    if single:
        return pl.BlockSpec(shape, lambda w, m: zeros, pipeline_mode=pl.Buffered(1))
    return pl.BlockSpec(shape, lambda w, m: zeros)


def window_spec(*shape):
    zeros = (0,) * len(shape)
    return pl.BlockSpec((1,) + shape, lambda w, m: (w,) + zeros)


def run_kernel(kernel, wins, meta, ins, in_specs, out_shape, out_specs, scratch, flops, moved):
    return pl.pallas_call(
        kernel,
        grid_spec=pltpu.PrefetchScalarGridSpec(
            num_scalar_prefetch=1,
            grid=(wins,),
            in_specs=in_specs,
            out_specs=out_specs,
            scratch_shapes=scratch,
        ),
        out_shape=out_shape,
        compiler_params=pltpu.CompilerParams(
            dimension_semantics=("arbitrary",), vmem_limit_bytes=56 * 1024 * 1024
        ),
        cost_estimate=pl.CostEstimate(
            flops=flops, bytes_accessed=moved, transcendentals=wins * WIN * FF
        ),
    )(meta, *ins)


def call_attention(dp, seg, meta, parts, stack, bias):
    wins = parts[0].shape[0]
    shape = jax.ShapeDtypeStruct
    return run_kernel(
        functools.partial(attention_kernel, dp, seg),
        wins,
        meta,
        [*parts, stack, bias],
        [window_spec(seg, D)] * dp + [whole_spec(stack.shape), whole_spec(bias.shape)],
        [
            shape((wins, WIN, D), BF16),
            shape((wins, WIN, 3 * D), BF16),
            shape((wins, WIN, D), BF16),
            shape((wins, HEADS, WIN), F32),
        ],
        [
            window_spec(WIN, D),
            window_spec(WIN, 3 * D),
            window_spec(WIN, D),
            window_spec(HEADS, WIN),
        ],
        [pltpu.VMEM((D, 3 * D), BF16), pltpu.VMEM((WIN, WIN), F32)],
        wins * 4_000_000_000,
        wins * 4_000_000,
    )


def call_ffn(dp, seg, tokens, meta, cots, hidden, attended, stack, vec, prev):
    wins = hidden.shape[0]
    shape = jax.ShapeDtypeStruct
    first = prev is None
    ins = [*cots, hidden, attended, stack, vec]
    specs = [window_spec(seg, D)] * dp + [
        window_spec(WIN, D),
        window_spec(WIN, D),
        whole_spec(stack.shape),
        whole_spec(vec.shape),
    ]
    if not first:
        ins.append(prev)
        specs.append(whole_spec(prev.shape))
    return run_kernel(
        functools.partial(ffn_kernel, dp, seg, tokens, first),
        wins,
        meta,
        ins,
        specs,
        [shape((wins, seg, D), BF16)] * dp
        + [
            shape((wins, WIN, D), F32),
            shape((wins, WIN, D), BF16),
            shape((REST_BLOCKS, BLK, BLK), BF16),
            shape((ROWS_VEC, D), F32),
        ],
        [window_spec(seg, D)] * dp
        + [
            window_spec(WIN, D),
            window_spec(WIN, D),
            whole_spec((REST_BLOCKS, BLK, BLK), False),
            whole_spec((ROWS_VEC, D), False),
        ],
        [
            pltpu.VMEM((REST_BLOCKS, BLK, BLK), F32),
            pltpu.VMEM((WIN, FF), BF16),
            pltpu.VMEM((WIN, FF), F32),
            pltpu.VMEM((WIN, D), BF16),
            pltpu.VMEM((D, D), BF16),
        ],
        wins * 8_000_000_000,
        wins * 12_000_000,
    )


def call_attention_back(dp, seg, meta, stack, hidden, qkv, d_o, lse, d_mixed, prev):
    wins = hidden.shape[0]
    shape = jax.ShapeDtypeStruct
    first = prev is None
    ins = [stack, hidden, qkv, d_o, lse, d_mixed]
    specs = [
        whole_spec(stack.shape),
        window_spec(WIN, D),
        window_spec(WIN, 3 * D),
        window_spec(WIN, D),
        window_spec(HEADS, WIN),
        window_spec(WIN, D),
    ]
    if not first:
        ins.append(prev)
        specs.append(whole_spec(prev.shape))
    return run_kernel(
        functools.partial(attention_back_kernel, dp, seg, first),
        wins,
        meta,
        ins,
        specs,
        [shape((wins, seg, D), BF16)] * dp
        + [shape((QKV_BLOCKS, BLK, BLK), BF16), shape((8, D), F32)],
        [window_spec(seg, D)] * dp
        + [whole_spec((QKV_BLOCKS, BLK, BLK), False), whole_spec((8, D), False)],
        [
            pltpu.VMEM((D, 3 * D), BF16),
            pltpu.VMEM((WIN, WIN), F32),
            pltpu.VMEM((WIN, 3 * D), BF16),
            pltpu.VMEM((D, 3 * D), F32),
            pltpu.VMEM((WIN, D), BF16),
        ],
        wins * 5_000_000_000,
        wins * 8_000_000,
    )


def swap(values, axis, size, k):
    return lax.ppermute(values, axis, [(i, i ^ k) for i in range(size)])


def bits_of(size):
    return [1 << i for i in range(size.bit_length() - 1)]


def hop_orders(seq_count):
    high = [k for k in bits_of(seq_count) if k > 1]
    return (high, high[::-1])


def gather_rows(cur, order, seq_count, seq_index):
    blocks, rows, cols = cur.shape
    for k in order:
        got = swap(cur, "seq", seq_count, k)
        odd = (seq_index & k) != 0
        cur = jnp.stack([jnp.where(odd, got, cur), jnp.where(odd, cur, got)], axis=0)
    lead = list(order[::-1])
    count = len(lead)
    axes = [count] + [lead.index(k) for k in sorted(lead, reverse=True)] + [count + 1, count + 2]
    return cur.transpose(axes).reshape(blocks, rows * seq_count, cols)


def gather_split(cur, seq_count, seq_index):
    first, second = hop_orders(seq_count)
    half = cur.shape[0] // 2
    return jnp.concatenate(
        [
            gather_rows(cur[:half], first + [1], seq_count, seq_index),
            gather_rows(cur[half:], second + [1], seq_count, seq_index),
        ],
        axis=0,
    )


def scatter_rows(cur, order, seq_count, seq_index):
    blocks, height, cols = cur.shape
    left = sorted(bits_of(seq_count), reverse=True)
    cur = cur.reshape([blocks] + [2] * len(left) + [height // seq_count, cols])
    for k in order:
        axis = 1 + left.index(k)
        bit = (seq_index // k) % 2
        mine = lax.dynamic_index_in_dim(cur, bit, axis, keepdims=False)
        other = lax.dynamic_index_in_dim(cur, 1 - bit, axis, keepdims=False)
        got = swap(other, "seq", seq_count, k)
        cur = (mine.astype(F32) + got.astype(F32)).astype(BF16)
        left.remove(k)
    return cur


def scatter_split(cur, seq_count, seq_index):
    first, second = hop_orders(seq_count)
    half = cur.shape[0] // 2
    return jnp.concatenate(
        [
            scatter_rows(cur[:half], [1] + first, seq_count, seq_index),
            scatter_rows(cur[half:], [1] + second, seq_count, seq_index),
        ],
        axis=0,
    )


def scatter_parts(cur, parts, dp_count, dp_index):
    owned = cur.shape[0] // len(parts)
    cur = cur.reshape((len(parts), owned) + cur.shape[1:])

    def slab(target):
        at = jnp.clip(target - parts[0], 0, len(parts) - 1)
        return lax.dynamic_index_in_dim(cur, at, 0, keepdims=False)

    total = slab(dp_index).astype(F32)
    for s in range(1, dp_count):
        pairs = [(i, i ^ s) for i in range(dp_count) if (i ^ s) in parts]
        got = lax.ppermute(slab(dp_index ^ s), "dp", pairs)
        total = total + got.astype(F32)
    return total


def gather_parts(own, parts, dp_count, dp_index):
    got = [own]
    for s in range(1, dp_count):
        got.append(
            lax.ppermute(own, "dp", [(i, i ^ s) for i in range(dp_count) if i in parts])
        )
    return jnp.concatenate([lax.select_n(dp_index ^ j, *got) for j in parts], axis=0)


def after(values, *marks):
    return lax.optimization_barrier((values, marks))[0]


def body(
    inputs,
    cotangent,
    lengths,
    weights,
    vectors,
    positions,
    left_stats,
    right_stats,
    left_roots,
    right_roots,
    vector_second,
    position_second,
):
    seq_count = lax.axis_size("seq")
    dp_count = lax.axis_size("dp")
    seq_index = lax.axis_index("seq")
    dp_index = lax.axis_index("dp")
    micro, wins_dev, segment, model_width = inputs.shape
    wins = wins_dev // dp_count
    total_tokens = micro * wins_dev * seq_count * segment * dp_count
    owned, row_part, _ = weights.shape
    qkv_parts = list(range(QKV_BLOCKS // owned))
    rest_parts = list(range(QKV_BLOCKS // owned, dp_count))

    own = weights.astype(BF16)
    qkv_rows = gather_parts(own, qkv_parts, dp_count, dp_index)
    stack_qkv = gather_split(qkv_rows, seq_count, seq_index)
    rest_rows = gather_parts(after(own, qkv_rows), rest_parts, dp_count, dp_index)
    stack_rest = gather_split(rest_rows, seq_count, seq_index)
    roots_full = lax.all_gather(right_roots.astype(BF16), "seq", axis=1, tiled=True)

    vec = vectors.reshape(-1, D)
    bias_qv = jnp.concatenate([vec[0:2], jnp.zeros((6, D), F32)], axis=0)
    vec_pad = jnp.concatenate([vec, jnp.zeros((ROWS_VEC - vec.shape[0], D), F32)], axis=0)

    def exchange(pieces):
        return [pieces[0]] + [swap(pieces[s], "dp", dp_count, s) for s in range(1, dp_count)]

    def send_segments(rows, shift, mark):
        grouped = rows.reshape(dp_count, wins, segment, model_width)
        pieces = []
        for s in range(dp_count):
            piece = lax.dynamic_index_in_dim(grouped, dp_index ^ s, 0, keepdims=False)
            if shift is not None:
                piece = (piece.astype(F32) + shift[None]).astype(BF16)
            pieces.append(piece)
        if mark is not None:
            pieces = after(pieces, mark)
        return exchange(pieces)

    metas = []
    for i in range(micro):
        lens = lax.dynamic_index_in_dim(
            lengths[i].reshape(dp_count, wins), dp_index, 0, keepdims=False
        )
        metas.append(jnp.concatenate([dp_index[None].astype(jnp.int32), lens]))

    xs, cots = [], []
    marks = [qkv_rows, rest_rows]
    for i in range(micro):
        x = send_segments(inputs[i], positions, marks[-2])
        marks.append(x[-1])
        c = send_segments(cotangent[i], None, marks[-2])
        marks.append(c[-1])
        xs.append(x)
        cots.append(c)

    out_got, dx_got = [], []
    dw_rest, dw_qkv = None, None
    vec_grads = jnp.zeros((ROWS_VEC, D), F32)
    for i in range(micro):
        hidden, qkv, attended, lse = call_attention(
            dp_count, segment, metas[i], xs[i], stack_qkv, bias_qv
        )
        results = call_ffn(
            dp_count, segment, total_tokens, metas[i], cots[i], hidden, attended, stack_rest,
            vec_pad, dw_rest,
        )
        outs = results[:dp_count]
        d_mixed, d_o, dw_rest, vg = results[dp_count:]
        out_got.append(exchange(outs))
        results = call_attention_back(
            dp_count, segment, metas[i], stack_qkv, hidden, qkv, d_o, lse, d_mixed, dw_qkv
        )
        dxs = results[:dp_count]
        dw_qkv, db = results[dp_count:]
        dx_got.append(exchange(dxs))
        vec_grads = vec_grads + vg + jnp.concatenate(
            [db[0:2], jnp.zeros((ROWS_VEC - 2, D), F32)], axis=0
        )

    rest_sum = scatter_parts(
        scatter_split(dw_rest, seq_count, seq_index), rest_parts, dp_count, dp_index
    )
    qkv_sum = scatter_parts(
        scatter_split(dw_qkv, seq_count, seq_index), qkv_parts, dp_count, dp_index
    )
    grad_rows = jnp.where(dp_index < len(qkv_parts), qkv_sum, rest_sum)
    grad_low = grad_rows.astype(BF16)
    grad_full = gather_split(grad_low, seq_count, seq_index)

    row_start = seq_index * row_part

    def batched(spec, left, right):
        return jnp.einsum(spec, left, right, preferred_element_type=F32)

    left_new = DECAY * left_stats + (1.0 - DECAY) * batched("bij,bkj->bik", grad_low, grad_full)
    column_part = lax.dynamic_slice_in_dim(grad_full, row_start, row_part, 2)
    right_new = DECAY * right_stats + (1.0 - DECAY) * batched(
        "bki,bkj->bij", column_part, grad_full
    )
    left_applied = batched("bij,bjk->bik", left_roots.astype(BF16), grad_full)
    step_rows = batched("bij,bjk->bik", left_applied.astype(BF16), roots_full)
    weights_new = weights - MATRIX_RATE * step_rows

    sums = vec_grads
    for k in bits_of(seq_count):
        sums = sums + swap(sums, "seq", seq_count, k)
    for k in bits_of(dp_count):
        sums = sums + swap(sums, "dp", dp_count, k)
    vector_grads = sums[: vec.shape[0]].reshape(-1)
    vector_second_new = DECAY * vector_second + (1.0 - DECAY) * vector_grads * vector_grads
    vectors_new = vectors - VECTOR_RATE * vector_grads / (jnp.sqrt(vector_second_new) + ROOT_EPS)

    place_sum = jnp.zeros((segment, model_width), F32)
    layer_rows, input_rows = [], []
    for i in range(micro):
        for got in dx_got[i]:
            place_sum = place_sum + jnp.sum(got.astype(F32), axis=0)
        layer_rows.append(
            jnp.concatenate([lax.select_n(dp_index ^ e, *out_got[i]) for e in range(dp_count)])
        )
        input_rows.append(
            jnp.concatenate(
                [lax.select_n(dp_index ^ e, *dx_got[i]).astype(F32) for e in range(dp_count)]
            )
        )
    for k in bits_of(seq_count):
        low = place_sum.astype(BF16)
        place_sum = low.astype(F32) + swap(low, "seq", seq_count, k).astype(F32)
    position_grads = place_sum
    position_second_new = DECAY * position_second + (1.0 - DECAY) * position_grads * position_grads
    positions_new = positions - VECTOR_RATE * position_grads / (
        jnp.sqrt(position_second_new) + ROOT_EPS
    )
    return (
        jnp.stack(layer_rows, axis=0),
        jnp.stack(input_rows, axis=0),
        grad_rows,
        left_new,
        right_new,
        weights_new,
        vector_grads,
        vector_second_new,
        vectors_new,
        position_grads,
        position_second_new,
        positions_new,
    )


def solution(mesh):
    rows = P(None, "seq", "dp", None)
    blocks = P("dp", "seq", None)
    in_specs = (
        rows, rows, P(None, "seq"), blocks, P(), P("dp", None),
        blocks, blocks, blocks, blocks, P(), P("dp", None),
    )
    out_specs = (
        rows, rows, blocks, blocks, blocks, blocks,
        P(), P(), P(), P("dp", None), P("dp", None), P("dp", None),
    )
    return jax.shard_map(body, mesh=mesh, in_specs=in_specs, out_specs=out_specs, check_vma=False)
```

```python
import functools
import itertools

import jax
import jax.numpy as jnp
from jax import lax
from jax.experimental import pallas as pl
from jax.experimental.pallas import tpu as pltpu
from jax.sharding import PartitionSpec as P

HEADS = 8
FF = 2048
WIN = 512
D = 512
BLK = 256
QKV_BLOCKS = 12
REST_BLOCKS = 36
HEAD_DIM = D // HEADS
PAIR = 2 * HEAD_DIM
PAIRS = HEADS // 2
FF_CHUNKS = FF // BLK
ROWS_VEC = 16

NORM_EPS = 1e-05
ROOT_EPS = 1e-08
DECAY = 0.5
MATRIX_RATE = 0.5
VECTOR_RATE = 0.2
MASKED = -1e30
SCALE = HEAD_DIM ** (-0.5)
ROOT_HALF = 0.7071067811865476
DENSITY = 0.3989422804014327

F32 = jnp.float32
BF16 = jnp.bfloat16


def dot_nn(left, right):
    return lax.dot_general(left, right, (((1,), (0,)), ((), ())), preferred_element_type=F32)


def dot_nt(left, right):
    return lax.dot_general(left, right, (((1,), (1,)), ((), ())), preferred_element_type=F32)


def each_piece(packing, refs, core):
    if not packing:
        yield 0, 0, refs[0]
        return
    base = 0
    for side, bits in enumerate(packing):
        for which in range(2):
            ref = refs[2 * side + which]
            blocks, rows = ref.shape[len(bits)], ref.shape[len(bits) + 1]
            last = core if which == 0 else 1 - core
            for at in itertools.product(range(2), repeat=len(bits)):
                first = sum(k * v for k, v in zip(bits, at))
                yield base, pl.multiple_of((first + last) * rows, rows), ref.at[at]
        base += blocks


def fill_qkv_matrix(full, packing, refs, core):
    side = D // BLK
    for base, offset, ref in each_piece(packing, refs, core):
        blocks, rows = ref.shape[:2]
        for n in range(blocks):
            b = base + n
            m, i, j = b // (side * side), (b // side) % side, b % side
            cols = slice(D * m + BLK * j, D * m + BLK * (j + 1))
            full[pl.ds(BLK * i + offset, rows), cols] = ref[n]


def fill_stack(stack, packing, refs, core):
    for base, offset, ref in each_piece(packing, refs, core):
        blocks, rows = ref.shape[:2]
        for n in range(blocks):
            stack[base + n, pl.ds(offset, rows), :] = ref[n]


def write_gradient(block_at, blocks, rows, core, outs):
    for b in range(blocks):
        if len(outs) == 1:
            outs[0][b] = block_at(b, 0, BLK).astype(BF16)
            continue
        for which, out in enumerate(outs):
            last = core if which == 0 else 1 - core
            for n in range(BLK // (2 * rows)):
                offset = pl.multiple_of((2 * n + last) * rows, rows)
                out[b, n * rows : (n + 1) * rows, :] = block_at(b, offset, rows).astype(BF16)


def fill_mask(mask, length):
    for i in range(WIN // BLK):
        keys = lax.broadcasted_iota(jnp.int32, (BLK, WIN), 0) + BLK * i
        queries = lax.broadcasted_iota(jnp.int32, (BLK, WIN), 1)
        keep = (keys <= queries) & (keys < length)
        mask[BLK * i : BLK * (i + 1), :] = jnp.where(keep, 0.0, MASKED).astype(F32)


def half_marks():
    lane = lax.broadcasted_iota(jnp.int32, (1, PAIR), 1)
    low = jnp.where(lane < HEAD_DIM, 1.0, 0.0)
    return (low.astype(BF16), (1.0 - low).astype(BF16))


def attention_kernel(packing, wins, meta, x_ref, bias, *refs):
    weight_refs = refs[: 2 * len(packing) or 1]
    qkv_ref, o_ref, lse_ref, full, mask = refs[len(weight_refs) :]
    step = pl.program_id(0)

    @pl.when(step == 0)
    def _():
        fill_qkv_matrix(full, packing, weight_refs, meta[wins])

    hidden = x_ref[:, 0].reshape(WIN, D)
    for m in range(3):
        cols = slice(D * m, D * (m + 1))
        rows = dot_nn(hidden, full[:, cols])
        if m != 1:
            rows = rows + bias[(m // 2) : (m // 2) + 1, :]
        qkv_ref[0, :, cols] = rows.astype(BF16)
    fill_mask(mask, meta[step])
    marks = half_marks()
    for p in range(PAIRS):
        at = PAIR * p
        q8 = qkv_ref[0, :, at : at + PAIR] * jnp.asarray(SCALE, BF16)
        key = qkv_ref[0, :, D + at : D + at + PAIR]
        val_t = jnp.transpose(qkv_ref[0, :, 2 * D + at : 2 * D + at + PAIR])
        pieces = []
        for h in range(2):
            key_h = key * marks[h]
            row = 2 * p + h
            blocks = []
            for qb in range(WIN // BLK):
                cols = slice(BLK * qb, BLK * (qb + 1))
                span = BLK * (qb + 1)
                s_t = dot_nt(key_h[:span], q8[cols]) + mask[:span, cols]
                top = jnp.max(s_t, axis=0, keepdims=True)
                expo = jnp.exp(s_t - top)
                total = jnp.sum(expo, axis=0, keepdims=True)
                probs = (expo * (1.0 / total)).astype(BF16)
                lse_ref[0, row : row + 1, cols] = top + jnp.log(total)
                blocks.append(dot_nn(val_t[HEAD_DIM * h : HEAD_DIM * (h + 1), :span], probs))
            pieces.append(jnp.concatenate(blocks, axis=1))
        o_t = jnp.concatenate(pieces, axis=0)
        o_ref[0, :, at : at + PAIR] = jnp.transpose(o_t).astype(BF16)


def qkv_block(acc, b, offset, rows):
    side = D // BLK
    m, i, j = b // (side * side), (b // side) % side, b % side
    return acc[pl.ds(BLK * i + offset, rows), D * m + BLK * j : D * m + BLK * (j + 1)]


def attention_back_kernel(packing, wins, begin, part, first, joined, last, meta, *refs):
    x_ref, qkv_ref, do_ref, lse_ref, da_ref = refs[:5]
    weight_refs = refs[5 : 5 + (2 * len(packing) or 1)]
    refs = refs[5 + len(weight_refs) :]
    if not first:
        prev, refs = refs[0], refs[1:]
    if joined:
        refs = refs[1:]
    dx_ref, refs = refs[0], refs[1:]
    dw_refs, refs = refs[: 2 if last else 1], refs[2 if last else 1 :]
    db_ref, full, mask, dqkv, acc = refs
    step = pl.program_id(0)
    side = D // BLK

    @pl.when(step == 0)
    def _():
        fill_qkv_matrix(full, packing, weight_refs, meta[wins])
        if first:
            acc[...] = jnp.zeros_like(acc)
        else:
            for b in range(QKV_BLOCKS):
                m, i, j = b // (side * side), (b // side) % side, b % side
                acc[BLK * i : BLK * (i + 1), D * m + BLK * j : D * m + BLK * (j + 1)] = prev[
                    b
                ].astype(F32)
        db_ref[...] = jnp.zeros_like(db_ref)

    fill_mask(mask, meta[begin + step])
    marks = half_marks()
    for p in range(PAIRS):
        at = PAIR * p
        q8 = qkv_ref[0, :, at : at + PAIR] * jnp.asarray(SCALE, BF16)
        key = qkv_ref[0, :, D + at : D + at + PAIR]
        val = qkv_ref[0, :, 2 * D + at : 2 * D + at + PAIR]
        d_o = do_ref[0, :, at : at + PAIR]
        key_t = jnp.transpose(key)
        dq_pieces, dk_pieces, dv_pieces = [], [], []
        for h in range(2):
            key_h = key * marks[h]
            val_h = val * marks[h]
            row = 2 * p + h
            dq_blocks = []
            dk_sum, dv_sum = None, None
            for qb in reversed(range(WIN // BLK)):
                cols = slice(BLK * qb, BLK * (qb + 1))
                span = BLK * (qb + 1)
                s_t = dot_nt(key_h[:span], q8[cols]) + mask[:span, cols]
                probs = jnp.exp(s_t - lse_ref[0, row : row + 1, cols])
                d_probs = dot_nt(val_h[:span], d_o[cols])
                delta = jnp.sum(probs * d_probs, axis=0, keepdims=True)
                d_s = (probs * (d_probs - delta)).astype(BF16)
                dv_part = dot_nn(probs.astype(BF16), d_o[cols])
                dk_part = dot_nn(d_s, q8[cols])
                dq_blocks.append(dot_nn(key_t[HEAD_DIM * h : HEAD_DIM * (h + 1), :span], d_s))
                if dv_sum is None:
                    dv_sum, dk_sum = dv_part, dk_part
                else:
                    dv_sum = jnp.concatenate([dv_sum[:span] + dv_part, dv_sum[span:]], axis=0)
                    dk_sum = jnp.concatenate([dk_sum[:span] + dk_part, dk_sum[span:]], axis=0)
            dq_pieces.append(jnp.concatenate(dq_blocks[::-1], axis=1))
            dk_pieces.append(dk_sum)
            dv_pieces.append(dv_sum)
        lane = lax.broadcasted_iota(jnp.int32, (WIN, PAIR), 1) < HEAD_DIM
        dq = jnp.transpose(jnp.concatenate(dq_pieces, axis=0)) * SCALE
        dk = jnp.where(lane, dk_pieces[0], dk_pieces[1])
        dv = jnp.where(lane, dv_pieces[0], dv_pieces[1])
        dqkv[:, at : at + PAIR] = dq.astype(BF16)
        dqkv[:, D + at : D + at + PAIR] = dk.astype(BF16)
        dqkv[:, 2 * D + at : 2 * D + at + PAIR] = dv.astype(BF16)
    h_t = jnp.transpose(x_ref[:, 0].reshape(WIN, D))
    for m in range(3):
        cols = slice(D * m, D * (m + 1))
        rows = dqkv[:, cols]
        acc[:, cols] += dot_nn(h_t, rows)
        if m != 1:
            db_ref[(m // 2) : (m // 2) + 1, :] += jnp.sum(
                rows.astype(F32), axis=0, keepdims=True
            )
    total = da_ref[0]
    for m in range(3):
        cols = slice(D * m, D * (m + 1))
        total = total + dot_nt(dqkv[:, cols], full[:, cols])
    dx_ref[:, 0] = total.astype(BF16).reshape(dx_ref.shape[0], dx_ref.shape[2], D)

    @pl.when(step == pl.num_programs(0) - 1)
    def _():
        write_gradient(
            functools.partial(qkv_block, acc), QKV_BLOCKS, part, meta[wins], dw_refs
        )


def normal_parts(u):
    size = jnp.abs(u)
    t = 1.0 / (1.0 + (0.3275911 * ROOT_HALF) * size)
    expo = jnp.exp(-0.5 * (u * u))
    poly = t * (
        0.5 * 0.254829592
        + t
        * (
            -0.5 * 0.284496736
            + t * (0.5 * 1.421413741 + t * (-0.5 * 1.453152027 + t * (0.5 * 1.061405429)))
        )
    )
    tail = poly * expo
    return jnp.where(u >= 0.0, 1.0 - tail, tail), expo


def norm_stats(rows):
    mean = jnp.mean(rows, axis=1, keepdims=True)
    centered = rows - mean
    spread = jnp.mean(centered * centered, axis=1, keepdims=True)
    inverse = lax.rsqrt(spread + NORM_EPS)
    return centered * inverse, inverse


def norm_back(d_rows, normal, inverse):
    mean_d = jnp.mean(d_rows, axis=1, keepdims=True)
    mean_dn = jnp.mean(d_rows * normal, axis=1, keepdims=True)
    return inverse * (d_rows - mean_d - normal * mean_dn)


def fill_ffn_matrices(w_out, w_up, w_down, packing, refs, core):
    side = D // BLK
    for base, offset, ref in each_piece(packing, refs, core):
        blocks, rows = ref.shape[:2]
        for n in range(blocks):
            full, i, j = ffn_place(base + n, (w_out, w_up, w_down))
            full[pl.ds(BLK * i + offset, rows), BLK * j : BLK * (j + 1)] = ref[n]


def ffn_place(b, matrices):
    side = D // BLK
    if b < side * side:
        return matrices[0], b // side, b % side
    b -= side * side
    if b < side * FF_CHUNKS:
        return matrices[1], b // FF_CHUNKS, b % FF_CHUNKS
    b -= side * FF_CHUNKS
    return matrices[2], b // side, b % side


def ffn_kernel(packing, wins, tokens, part, first, last, split, meta, *refs):
    cot_ref, x_ref, o_ref, vec = refs[:4]
    weight_refs = refs[4 : 4 + (2 * len(packing) or 1)]
    refs = refs[4 + len(weight_refs) :]
    if not first:
        prev, refs = refs[0], refs[1:]
    out_ref, da_ref, do_ref = refs[:3]
    refs = refs[3:]
    dw_refs, refs = refs[: 2 if split else 1], refs[2 if split else 1 :]
    vg_ref, w_out, w_up, w_down, acc_out, acc_up, acc_down, z_ref, gp_ref, du_ref = refs
    step = pl.program_id(0)
    length = meta[step]
    accs = (acc_out, acc_up, acc_down)

    def acc_block(b, offset, rows):
        full, i, j = ffn_place(b, accs)
        if full is acc_down:
            i, j = j, i
        return full.at[pl.ds(BLK * i + offset, rows), BLK * j : BLK * (j + 1)]

    @pl.when(step == 0)
    def _():
        fill_ffn_matrices(w_out, w_up, w_down, packing, weight_refs, meta[wins])
        for b in range(REST_BLOCKS):
            acc_block(b, 0, BLK)[...] = (
                jnp.zeros((BLK, BLK), F32) if first else prev[b].astype(F32)
            )
        vg_ref[...] = jnp.zeros_like(vg_ref)

    def add_row(row, values, at=0):
        vg_ref[row : row + 1, at : at + values.shape[1]] += jnp.sum(
            values.astype(F32), axis=0, keepdims=True
        )

    bias_out, bias_down = vec[2:3, :], vec[7:8, :]
    gain_one, shift_one = vec[8:9, :], vec[9:10, :]
    gain_two, shift_two = vec[10:11, :], vec[11:12, :]
    attended = o_ref[0]
    mixed = x_ref[:, 0].reshape(WIN, D).astype(F32) + (dot_nn(attended, w_out[...]) + bias_out)
    n_one, inv_one = norm_stats(mixed)
    normed = n_one * gain_one + shift_one
    normed_low = normed.astype(BF16)
    for c in range(FF // D):
        cols = slice(D * c, D * (c + 1))
        u = dot_nn(normed_low, w_up[:, cols]) + vec[3 + c : 4 + c, :]
        phi, expo = normal_parts(u)
        z_ref[:, cols] = (u * phi).astype(BF16)
        gp_ref[:, cols] = phi + (u * expo) * DENSITY
    summed = normed + (dot_nn(z_ref[...], w_down[...]) + bias_down)
    n_two, inv_two = norm_stats(summed)
    result = (n_two * gain_two + shift_two).astype(BF16)
    out_ref[:, 0] = result.reshape(out_ref.shape[0], out_ref.shape[2], D)

    places = lax.broadcasted_iota(jnp.int32, (WIN, 1), 0)
    valid = jnp.where(places < length, 1.0 / tokens, 0.0).astype(F32)
    seed = cot_ref[:, 0].reshape(WIN, D).astype(F32) * valid
    add_row(10, seed * n_two)
    add_row(11, seed)
    d_summed = norm_back(seed * gain_two, n_two, inv_two)
    d_ff = d_summed.astype(BF16)
    add_row(7, d_ff)
    for c in range(FF // D):
        cols = slice(D * c, D * (c + 1))
        d_z = dot_nt(d_ff, w_down[cols, :])
        d_u = (d_z * gp_ref[:, cols]).astype(BF16)
        add_row(3 + c, d_u)
        du_ref[:, cols] = d_u
    d_ff_t = jnp.transpose(d_ff)
    normed_t = jnp.transpose(normed_low)
    for c in range(FF // D):
        cols = slice(D * c, D * (c + 1))
        acc_down[:, cols] += dot_nn(d_ff_t, z_ref[:, cols])
        acc_up[:, cols] += dot_nn(normed_t, du_ref[:, cols])
    d_normed = d_summed + dot_nt(du_ref[...], w_up[...])
    add_row(8, d_normed * n_one)
    add_row(9, d_normed)
    d_mixed = norm_back(d_normed * gain_one, n_one, inv_one)
    da_ref[0] = d_mixed
    d_branch = d_mixed.astype(BF16)
    add_row(2, d_branch)
    acc_out[...] += dot_nn(jnp.transpose(attended), d_branch)
    do_ref[0] = dot_nt(d_branch, w_out[...]).astype(BF16)

    @pl.when(step == pl.num_programs(0) - 1)
    def _():
        if last:
            for j in range(D // BLK):
                for i in range(FF_CHUNKS):
                    at = (slice(BLK * j, BLK * (j + 1)), slice(BLK * i, BLK * (i + 1)))
                    acc_down[at] = jnp.transpose(acc_down[at])
        write_gradient(
            lambda b, offset, rows: acc_block(b, offset, rows)[...],
            REST_BLOCKS, part, meta[wins], dw_refs,
        )


def whole_spec(shape):
    zeros = (0,) * len(shape)
    return pl.BlockSpec(shape, lambda w, m: zeros, pipeline_mode=pl.Buffered(1))


def total_spec(shape):
    zeros = (0,) * len(shape)
    return pl.BlockSpec(shape, lambda w, m: zeros)


def window_spec(begin, *shape):
    zeros = (0,) * len(shape)
    return pl.BlockSpec((1,) + shape, lambda w, m: (begin + w,) + zeros)


def segment_spec(dp, seg, begin=0):
    return pl.BlockSpec((dp, 1, seg, D), lambda w, m: (0, begin + w, 0, 0))


def gradient_outs(blocks, last, part):
    if not last:
        return [jax.ShapeDtypeStruct((blocks, BLK, BLK), BF16)]
    return [jax.ShapeDtypeStruct((blocks, BLK // 2, BLK), BF16)] * 2


def run_kernel(kernel, wins, meta, ins, outs, scratch, flops, moved, aliases=None):
    return pl.pallas_call(
        kernel,
        grid_spec=pltpu.PrefetchScalarGridSpec(
            num_scalar_prefetch=1,
            grid=(wins,),
            in_specs=[spec for _, spec in ins],
            out_specs=[spec for _, spec in outs],
            scratch_shapes=scratch,
        ),
        out_shape=[shape for shape, _ in outs],
        input_output_aliases=aliases or {},
        compiler_params=pltpu.CompilerParams(
            dimension_semantics=("arbitrary",), vmem_limit_bytes=56 * 1024 * 1024
        ),
        cost_estimate=pl.CostEstimate(
            flops=flops, bytes_accessed=moved, transcendentals=wins * WIN * FF
        ),
    )(meta, *[values for values, _ in ins])


def call_attention(meta, x, packing, weight_parts, bias):
    dp, wins, seg, _ = x.shape
    shape = jax.ShapeDtypeStruct
    return run_kernel(
        functools.partial(attention_kernel, packing, wins),
        wins,
        meta,
        [(x, segment_spec(dp, seg)), (bias, whole_spec(bias.shape))]
        + [(part, whole_spec(part.shape)) for part in weight_parts],
        [
            (shape((wins, WIN, 3 * D), BF16), window_spec(0, WIN, 3 * D)),
            (shape((wins, WIN, D), BF16), window_spec(0, WIN, D)),
            (shape((wins, HEADS, WIN), F32), window_spec(0, HEADS, WIN)),
        ],
        [pltpu.VMEM((D, 3 * D), BF16), pltpu.VMEM((WIN, WIN), F32)],
        wins * 8_500_000_000,
        wins * 4_000_000,
    )


def call_ffn(tokens, part, last, meta, cot, x, attended, packing, weight_parts, vec, prev):
    dp, wins, seg, _ = x.shape
    shape = jax.ShapeDtypeStruct
    first = prev is None
    ins = [
        (cot, segment_spec(dp, seg)),
        (x, segment_spec(dp, seg)),
        (attended, window_spec(0, WIN, D)),
        (vec, whole_spec(vec.shape)),
    ] + [(piece, whole_spec(piece.shape)) for piece in weight_parts]
    if not first:
        ins.append((prev, whole_spec(prev.shape)))
    split = last and part % 16 == 0
    return run_kernel(
        functools.partial(ffn_kernel, packing, wins, tokens, part, first, last, split),
        wins,
        meta,
        ins,
        [
            (shape((dp, wins, seg, D), BF16), segment_spec(dp, seg)),
            (shape((wins, WIN, D), F32), window_spec(0, WIN, D)),
            (shape((wins, WIN, D), BF16), window_spec(0, WIN, D)),
        ]
        + [(out, total_spec(out.shape)) for out in gradient_outs(REST_BLOCKS, split, part)]
        + [(shape((ROWS_VEC, D), F32), total_spec((ROWS_VEC, D)))],
        [
            pltpu.VMEM((D, D), BF16),
            pltpu.VMEM((D, FF), BF16),
            pltpu.VMEM((FF, D), BF16),
            pltpu.VMEM((D, D), F32),
            pltpu.VMEM((D, FF), F32),
            pltpu.VMEM((D, FF), F32),
            pltpu.VMEM((WIN, FF), BF16),
            pltpu.VMEM((WIN, FF), F32),
            pltpu.VMEM((WIN, FF), BF16),
        ],
        wins * 18_000_000_000,
        wins * 12_000_000,
    )


def call_attention_back(
    begin, count, part, last, meta, packing, weight_parts, x, qkv, d_o, lse, d_mixed, prev, dx
):
    dp, wins, seg, _ = x.shape
    shape = jax.ShapeDtypeStruct
    first = prev is None
    ins = [
        (x, segment_spec(dp, seg, begin)),
        (qkv, window_spec(begin, WIN, 3 * D)),
        (d_o, window_spec(begin, WIN, D)),
        (lse, window_spec(begin, HEADS, WIN)),
        (d_mixed, window_spec(begin, WIN, D)),
    ] + [(piece, whole_spec(piece.shape)) for piece in weight_parts]
    if not first:
        ins.append((prev, whole_spec(prev.shape)))
    aliases = {}
    if dx is not None:
        ins.append((dx, pl.BlockSpec(memory_space=pl.ANY)))
        aliases = {len(ins): 0}
    split = last and part % 16 == 0
    return run_kernel(
        functools.partial(
            attention_back_kernel, packing, wins, begin, part, first, dx is not None, split
        ),
        count,
        meta,
        ins,
        [(shape((dp, wins, seg, D), BF16), segment_spec(dp, seg, begin))]
        + [(out, total_spec(out.shape)) for out in gradient_outs(QKV_BLOCKS, split, part)]
        + [(shape((8, D), F32), total_spec((8, D)))],
        [
            pltpu.VMEM((D, 3 * D), BF16),
            pltpu.VMEM((WIN, WIN), F32),
            pltpu.VMEM((WIN, 3 * D), BF16),
            pltpu.VMEM((D, 3 * D), F32),
        ],
        count * 12_500_000_000,
        count * 8_000_000,
        aliases,
    )


def swap(values, axis, size, k):
    return lax.ppermute(values, axis, [(i, i ^ k) for i in range(size)])


def bits_of(size):
    return [1 << i for i in range(size.bit_length() - 1)]


def hop_orders(seq_count):
    high = [k for k in bits_of(seq_count) if k > 1]
    return (high, high[::-1])


def gather_hop(state, k, seq_count, seq_index, *marks):
    cur, lead = state
    got = after(swap(cur, "seq", seq_count, k), *marks)
    odd = (seq_index & k) != 0
    cur = jnp.stack([jnp.where(odd, got, cur), jnp.where(odd, cur, got)], axis=0)
    return cur, [k] + lead


def gather_end(state):
    cur, lead = state
    count = len(lead)
    blocks, rows, cols = cur.shape[count:]
    axes = [count] + [lead.index(k) for k in sorted(lead, reverse=True)] + [count + 1, count + 2]
    return cur.transpose(axes).reshape(blocks, rows << count, cols)


def halves(cur):
    half = cur.shape[0] // 2
    return [cur[:half], cur[half:]]


def gather_split(cur, seq_count, seq_index):
    done = []
    for part, order in zip(halves(cur), hop_orders(seq_count)):
        state = (part, [])
        for k in order + [1]:
            state = gather_hop(state, k, seq_count, seq_index)
        done.append(gather_end(state))
    return jnp.concatenate(done, axis=0)


def pack_rows(states, row_part, seq_count, seq_index, *marks):
    if row_part % 16:
        states = [gather_hop(state, 1, seq_count, seq_index) for state in states]
        return (), [jnp.concatenate([gather_end(state) for state in states], axis=0)]
    parts = []
    for cur, _ in states:
        parts += [cur, after(swap(cur, "seq", seq_count, 1), *marks)]
    return tuple(tuple(lead) for _, lead in states), parts


def scatter_first(parts, seq_count, seq_index, *marks):
    left = sorted(bits_of(seq_count), reverse=True)
    blocks, height, cols = parts[0].shape
    if len(parts) == 2:
        mine, other = parts
        rows = 2 * height // seq_count
    else:
        rows = height // seq_count
        cur = parts[0].reshape(blocks, seq_count // 2, 2, rows, cols)
        mine, other = [
            lax.dynamic_index_in_dim(cur, bit, 2, keepdims=False)
            for bit in (seq_index % 2, 1 - seq_index % 2)
        ]
    got = after(swap(other, "seq", seq_count, 1), *marks).reshape(mine.shape)
    cur = mine.astype(F32) + got.astype(F32)
    left.remove(1)
    cur = cur.astype(BF16).reshape([blocks] + [2] * len(left) + [rows, cols])
    return [(half, left) for half in halves(cur)]


def scatter_hop(state, k, seq_count, seq_index, *marks):
    cur, left = state
    axis = 1 + left.index(k)
    bit = (seq_index // k) % 2
    mine = lax.dynamic_index_in_dim(cur, bit, axis, keepdims=False)
    other = lax.dynamic_index_in_dim(cur, 1 - bit, axis, keepdims=False)
    got = after(swap(other, "seq", seq_count, k), *marks)
    cur = (mine.astype(F32) + got.astype(F32)).astype(BF16)
    return cur, [b for b in left if b != k]


def scatter_parts(cur, parts, dp_count, dp_index, *marks):
    owned = cur.shape[0] // len(parts)
    cur = cur.reshape((len(parts), owned) + cur.shape[1:])

    def slab(target):
        at = jnp.clip(target - parts[0], 0, len(parts) - 1)
        return lax.dynamic_index_in_dim(cur, at, 0, keepdims=False)

    total = slab(dp_index).astype(F32)
    for s in range(1, dp_count):
        pairs = [(i, i ^ s) for i in range(dp_count) if (i ^ s) in parts]
        got = after(lax.ppermute(slab(dp_index ^ s), "dp", pairs), *marks)
        total = total + got.astype(F32)
    return total


def gather_parts(own, parts, dp_count, dp_index):
    got = [own]
    for s in range(1, dp_count):
        got.append(
            lax.ppermute(own, "dp", [(i, i ^ s) for i in range(dp_count) if i in parts])
        )
    return jnp.concatenate([lax.select_n(dp_index ^ j, *got) for j in parts], axis=0)


def after(values, *marks):
    if not marks:
        return values
    return lax.optimization_barrier((values, marks))[0]


def body(
    inputs,
    cotangent,
    lengths,
    weights,
    vectors,
    positions,
    left_stats,
    right_stats,
    left_roots,
    right_roots,
    vector_second,
    position_second,
):
    seq_count = lax.axis_size("seq")
    dp_count = lax.axis_size("dp")
    seq_index = lax.axis_index("seq")
    dp_index = lax.axis_index("dp")
    micro, wins_dev, segment, model_width = inputs.shape
    wins = wins_dev // dp_count
    total_tokens = micro * wins_dev * seq_count * segment * dp_count
    owned, row_part, _ = weights.shape
    qkv_parts = list(range(QKV_BLOCKS // owned))
    rest_parts = list(range(QKV_BLOCKS // owned, dp_count))

    def exchange(rows):
        return lax.all_to_all(rows, "dp", 0, 0, tiled=True)

    grouped = (dp_count, wins, segment, model_width)
    xs = [
        exchange((inputs[0].astype(F32) + positions[None]).astype(BF16).reshape(grouped))
    ]

    own = weights.astype(BF16)
    orders = hop_orders(seq_count)
    hops = len(orders[0])

    def gather_both(states, step, *marks):
        return [
            gather_hop(state, order[step], seq_count, seq_index, *marks)
            for state, order in zip(states, orders)
        ]

    def after_both(states, *marks):
        return [(after(cur, *marks), lead) for cur, lead in states]

    def scatter_both(states, step, *marks):
        return [
            scatter_hop(state, order[step], seq_count, seq_index, *marks)
            for state, order in zip(states, orders)
        ]

    qkv_rows = gather_parts(own, qkv_parts, dp_count, dp_index)
    states = [(part, []) for part in halves(qkv_rows)]
    states = gather_both(states, 0)
    rest_own = after(own, states[0][0], states[1][0])
    for step in range(1, hops):
        states = gather_both(states, step)
    packing_qkv, parts_qkv = pack_rows(
        after_both(states, xs[0]), row_part, seq_count, seq_index
    )
    rest_rows = gather_parts(rest_own, rest_parts, dp_count, dp_index)
    rest = [(part, []) for part in halves(after(rest_rows, parts_qkv))]
    roots_full = lax.all_gather(right_roots.astype(BF16), "seq", axis=1, tiled=True)

    vec = vectors.reshape(-1, D)
    bias_qv = jnp.concatenate([vec[0:2], jnp.zeros((6, D), F32)], axis=0)
    vec_pad = jnp.concatenate([vec, jnp.zeros((ROWS_VEC - vec.shape[0], D), F32)], axis=0)

    metas = [
        lax.dynamic_index_in_dim(
            lengths[i].reshape(dp_count, wins), dp_index, 0, keepdims=False
        )
        for i in range(micro)
    ]
    metas = [jnp.concatenate([lens, (seq_index % 2)[None]]) for lens in metas]
    for i in range(1, micro):
        rows = (inputs[i].astype(F32) + positions[None]).astype(BF16).reshape(grouped)
        xs.append(exchange(after(rows, xs[-1])))
    cots = []
    for i in range(micro):
        cots.append(
            exchange(after(cotangent[i].reshape(grouped), cots[-1] if i else xs[-1]))
        )

    forward, ffn, out_got, dx_got = [], [], [], []
    rest = gather_both(rest, 0)
    mark = (rest[0][0], rest[1][0])
    for i in range(micro):
        forward.append(
            call_attention(after(metas[i], mark), xs[i], packing_qkv, parts_qkv, bias_qv)
        )
        mark = forward[-1][2]
        if i + 1 < hops:
            rest = gather_both(rest, i + 1, mark)
            mark = (mark, rest[0][0], rest[1][0])
    for step in range(micro + 1, hops):
        rest = gather_both(rest, step)
    mark = forward[-1][2]
    packing_rest, parts_rest = pack_rows(rest, row_part, seq_count, seq_index, mark)
    dw_rest = [None]
    vec_sums = jnp.zeros((ROWS_VEC, D), F32)
    for i in range(micro):
        qkv, attended, lse = forward[i]
        out, d_mixed, d_o, *dw_rest, vg = call_ffn(
            total_tokens, row_part, i == micro - 1, after(metas[i], mark), cots[i], xs[i],
            attended, packing_rest, parts_rest, vec_pad, dw_rest[0],
        )
        out_got.append(exchange(out))
        ffn.append((d_mixed, d_o))
        vec_sums = vec_sums + vg
        mark = vg

    def rest_step(state, step, *marks):
        if step == 0:
            return scatter_first(dw_rest, seq_count, seq_index, *marks)
        return scatter_both(state, step - 1, *marks)

    rest, rest_done = None, 0
    dw_qkv = [None]
    gates = (mark, out_got[0])
    for i in range(micro):
        qkv, attended, lse = forward[i]
        last = i == micro - 1
        if i == 1:
            gates = gates + (out_got[1],)
        dx, *dw_qkv, db = call_attention_back(
            0, wins, row_part, last, after(metas[i], gates), packing_qkv, parts_qkv, xs[i],
            qkv, ffn[i][1], lse, ffn[i][0], dw_qkv[0], None,
        )
        vec_sums = vec_sums + jnp.concatenate([db, jnp.zeros_like(db)], axis=0)
        rest = rest_step(rest, rest_done, db)
        rest_done += 1
        gates = (db, rest[0][0], rest[1][0])
        dx_got.append(exchange(after(dx, *dx_got[-1:])))

    states = scatter_first(
        after(dw_qkv, dx_got[0]) if micro > 1 else dw_qkv, seq_count, seq_index
    )
    while rest_done <= hops:
        rest = rest_step(rest, rest_done)
        rest_done += 1
    quiet = []
    for step in range(hops):
        states = scatter_both(states, step)
        quiet.append((states[0][0], states[1][0]))
    grad_rows = scatter_parts(
        jnp.concatenate([cur for cur, _ in states + rest], axis=0),
        qkv_parts + rest_parts, dp_count, dp_index,
    )
    grad_low = grad_rows.astype(BF16)
    grad_full = gather_split(grad_low, seq_count, seq_index)

    row_start = seq_index * row_part

    def batched(spec, left, right):
        return jnp.einsum(spec, left, right, preferred_element_type=F32)

    left_new = DECAY * left_stats + (1.0 - DECAY) * batched("bij,bkj->bik", grad_low, grad_full)
    column_part = lax.dynamic_slice_in_dim(grad_full, row_start, row_part, 2)
    right_new = DECAY * right_stats + (1.0 - DECAY) * batched(
        "bki,bkj->bij", column_part, grad_full
    )
    left_applied = batched("bij,bjk->bik", left_roots.astype(BF16), grad_full)
    step_rows = batched("bij,bjk->bik", left_applied.astype(BF16), roots_full)
    weights_new = weights - MATRIX_RATE * step_rows

    vec_sums = after(vec_sums, quiet[0])
    for k in bits_of(dp_count):
        vec_sums = vec_sums + swap(vec_sums, "dp", dp_count, k)
    place_sum = sum(jnp.sum(got.astype(F32), axis=(0, 1)) for got in dx_got)
    whole = (wins_dev, segment, model_width)
    layer_rows = [got.reshape(whole) for got in after(out_got, dx_got[-1])]
    input_rows = [got.astype(F32).reshape(whole) for got in dx_got]
    place_sum = jnp.concatenate([place_sum, vec_sums], axis=0)
    for k in bits_of(seq_count):
        low = place_sum.astype(BF16)
        place_sum = low.astype(F32) + swap(low, "seq", seq_count, k).astype(F32)
    vector_grads = place_sum[segment : segment + vec.shape[0]].reshape(-1)
    place_sum = place_sum[:segment]
    vector_second_new = DECAY * vector_second + (1.0 - DECAY) * vector_grads * vector_grads
    vectors_new = vectors - VECTOR_RATE * vector_grads / (jnp.sqrt(vector_second_new) + ROOT_EPS)
    position_grads = place_sum
    position_second_new = DECAY * position_second + (1.0 - DECAY) * position_grads * position_grads
    positions_new = positions - VECTOR_RATE * position_grads / (
        jnp.sqrt(position_second_new) + ROOT_EPS
    )
    return (
        jnp.stack(layer_rows, axis=0),
        jnp.stack(input_rows, axis=0),
        grad_rows,
        left_new,
        right_new,
        weights_new,
        vector_grads,
        vector_second_new,
        vectors_new,
        position_grads,
        position_second_new,
        positions_new,
    )


def solution(mesh):
    rows = P(None, "seq", "dp", None)
    blocks = P("dp", "seq", None)
    in_specs = (
        rows, rows, P(None, "seq"), blocks, P(), P("dp", None),
        blocks, blocks, blocks, blocks, P(), P("dp", None),
    )
    out_specs = (
        rows, rows, blocks, blocks, blocks, blocks,
        P(), P(), P(), P("dp", None), P("dp", None), P("dp", None),
    )
    return jax.shard_map(body, mesh=mesh, in_specs=in_specs, out_specs=out_specs, check_vma=False)
```

```python
import functools
import itertools

import jax
import jax.numpy as jnp
from jax import lax
from jax.experimental import pallas as pl
from jax.experimental.pallas import tpu as pltpu
from jax.sharding import PartitionSpec as P

HEADS = 8
FF = 2048
WIN = 512
D = 512
BLK = 256
QKV_BLOCKS = 12
REST_BLOCKS = 36
HEAD_DIM = D // HEADS
PAIR = 2 * HEAD_DIM
PAIRS = HEADS // 2
FF_CHUNKS = FF // BLK
ROWS_VEC = 16

NORM_EPS = 1e-05
ROOT_EPS = 1e-08
DECAY = 0.5
MATRIX_RATE = 0.5
VECTOR_RATE = 0.2
MASKED = -1e30
SCALE = HEAD_DIM ** (-0.5)
ROOT_HALF = 0.7071067811865476
DENSITY = 0.3989422804014327

F32 = jnp.float32
BF16 = jnp.bfloat16


def dot_nn(left, right):
    return lax.dot_general(left, right, (((1,), (0,)), ((), ())), preferred_element_type=F32)


def dot_nt(left, right):
    return lax.dot_general(left, right, (((1,), (1,)), ((), ())), preferred_element_type=F32)


def each_piece(packing, refs, core):
    if not packing:
        yield 0, 0, refs[0]
        return
    base = 0
    for side, bits in enumerate(packing):
        for which in range(2):
            ref = refs[2 * side + which]
            blocks, rows = ref.shape[len(bits)], ref.shape[len(bits) + 1]
            last = core if which == 0 else 1 - core
            for at in itertools.product(range(2), repeat=len(bits)):
                first = sum(k * v for k, v in zip(bits, at))
                yield base, pl.multiple_of((first + last) * rows, rows), ref.at[at]
        base += blocks


def fill_qkv_matrix(full, packing, refs, core):
    side = D // BLK
    for base, offset, ref in each_piece(packing, refs, core):
        blocks, rows = ref.shape[:2]
        for n in range(blocks):
            b = base + n
            m, i, j = b // (side * side), (b // side) % side, b % side
            cols = slice(D * m + BLK * j, D * m + BLK * (j + 1))
            full[pl.ds(BLK * i + offset, rows), cols] = ref[n]


def fill_stack(stack, packing, refs, core):
    for base, offset, ref in each_piece(packing, refs, core):
        blocks, rows = ref.shape[:2]
        for n in range(blocks):
            stack[base + n, pl.ds(offset, rows), :] = ref[n]


def write_gradient(block_at, blocks, rows, core, outs):
    for b in range(blocks):
        if len(outs) == 1:
            outs[0][b] = block_at(b, 0, BLK).astype(BF16)
            continue
        for which, out in enumerate(outs):
            last = core if which == 0 else 1 - core
            for n in range(BLK // (2 * rows)):
                offset = pl.multiple_of((2 * n + last) * rows, rows)
                out[b, n * rows : (n + 1) * rows, :] = block_at(b, offset, rows).astype(BF16)


def fill_mask(mask, length):
    for i in range(WIN // BLK):
        keys = lax.broadcasted_iota(jnp.int32, (BLK, WIN), 0) + BLK * i
        queries = lax.broadcasted_iota(jnp.int32, (BLK, WIN), 1)
        keep = (keys <= queries) & (keys < length)
        mask[BLK * i : BLK * (i + 1), :] = jnp.where(keep, 0.0, MASKED).astype(F32)


def half_marks():
    lane = lax.broadcasted_iota(jnp.int32, (1, PAIR), 1)
    low = jnp.where(lane < HEAD_DIM, 1.0, 0.0)
    return (low.astype(BF16), (1.0 - low).astype(BF16))


def attention_kernel(packing, wins, meta, x_ref, bias, *refs):
    weight_refs = refs[: 2 * len(packing) or 1]
    qkv_ref, o_ref, lse_ref, full, mask = refs[len(weight_refs) :]
    step = pl.program_id(0)

    @pl.when(step == 0)
    def _():
        fill_qkv_matrix(full, packing, weight_refs, meta[wins])

    hidden = x_ref[:, 0, 0].reshape(WIN, D)
    for m in range(3):
        cols = slice(D * m, D * (m + 1))
        rows = dot_nn(hidden, full[:, cols])
        if m != 1:
            rows = rows + bias[(m // 2) : (m // 2) + 1, :]
        qkv_ref[0, :, cols] = rows.astype(BF16)
    fill_mask(mask, meta[step])
    marks = half_marks()
    for p in range(PAIRS):
        at = PAIR * p
        q8 = qkv_ref[0, :, at : at + PAIR] * jnp.asarray(SCALE, BF16)
        key = qkv_ref[0, :, D + at : D + at + PAIR]
        val_t = jnp.transpose(qkv_ref[0, :, 2 * D + at : 2 * D + at + PAIR])
        pieces = []
        for h in range(2):
            key_h = key * marks[h]
            row = 2 * p + h
            blocks = []
            for qb in range(WIN // BLK):
                cols = slice(BLK * qb, BLK * (qb + 1))
                span = BLK * (qb + 1)
                s_t = dot_nt(key_h[:span], q8[cols]) + mask[:span, cols]
                top = jnp.max(s_t, axis=0, keepdims=True)
                expo = jnp.exp(s_t - top)
                total = jnp.sum(expo, axis=0, keepdims=True)
                probs = (expo * (1.0 / total)).astype(BF16)
                lse_ref[0, row : row + 1, cols] = top + jnp.log(total)
                blocks.append(dot_nn(val_t[HEAD_DIM * h : HEAD_DIM * (h + 1), :span], probs))
            pieces.append(jnp.concatenate(blocks, axis=1))
        o_t = jnp.concatenate(pieces, axis=0)
        o_ref[0, :, at : at + PAIR] = jnp.transpose(o_t).astype(BF16)


def qkv_block(acc, b, offset, rows):
    side = D // BLK
    m, i, j = b // (side * side), (b // side) % side, b % side
    return acc[pl.ds(BLK * i + offset, rows), D * m + BLK * j : D * m + BLK * (j + 1)]


def attention_back_kernel(packing, wins, begin, part, first, joined, last, meta, *refs):
    x_ref, qkv_ref, do_ref, lse_ref, da_ref = refs[:5]
    weight_refs = refs[5 : 5 + (2 * len(packing) or 1)]
    refs = refs[5 + len(weight_refs) :]
    if not first:
        prev, refs = refs[0], refs[1:]
    if joined:
        refs = refs[1:]
    dx_ref, refs = refs[0], refs[1:]
    dw_refs, refs = refs[: 2 if last else 1], refs[2 if last else 1 :]
    db_ref, full, mask, dqkv, acc = refs
    step = pl.program_id(0)
    side = D // BLK

    @pl.when(step == 0)
    def _():
        fill_qkv_matrix(full, packing, weight_refs, meta[wins])
        if first:
            acc[...] = jnp.zeros_like(acc)
        else:
            for b in range(QKV_BLOCKS):
                m, i, j = b // (side * side), (b // side) % side, b % side
                acc[BLK * i : BLK * (i + 1), D * m + BLK * j : D * m + BLK * (j + 1)] = prev[
                    b
                ].astype(F32)
        db_ref[...] = jnp.zeros_like(db_ref)

    fill_mask(mask, meta[begin + step])
    marks = half_marks()
    for p in range(PAIRS):
        at = PAIR * p
        q8 = qkv_ref[0, :, at : at + PAIR] * jnp.asarray(SCALE, BF16)
        key = qkv_ref[0, :, D + at : D + at + PAIR]
        val = qkv_ref[0, :, 2 * D + at : 2 * D + at + PAIR]
        d_o = do_ref[0, :, at : at + PAIR]
        key_t = jnp.transpose(key)
        dq_pieces, dk_pieces, dv_pieces = [], [], []
        for h in range(2):
            key_h = key * marks[h]
            val_h = val * marks[h]
            row = 2 * p + h
            dq_blocks = []
            dk_sum, dv_sum = None, None
            for qb in reversed(range(WIN // BLK)):
                cols = slice(BLK * qb, BLK * (qb + 1))
                span = BLK * (qb + 1)
                s_t = dot_nt(key_h[:span], q8[cols]) + mask[:span, cols]
                probs = jnp.exp(s_t - lse_ref[0, row : row + 1, cols])
                d_probs = dot_nt(val_h[:span], d_o[cols])
                delta = jnp.sum(probs * d_probs, axis=0, keepdims=True)
                d_s = (probs * (d_probs - delta)).astype(BF16)
                dv_part = dot_nn(probs.astype(BF16), d_o[cols])
                dk_part = dot_nn(d_s, q8[cols])
                dq_blocks.append(dot_nn(key_t[HEAD_DIM * h : HEAD_DIM * (h + 1), :span], d_s))
                if dv_sum is None:
                    dv_sum, dk_sum = dv_part, dk_part
                else:
                    dv_sum = jnp.concatenate([dv_sum[:span] + dv_part, dv_sum[span:]], axis=0)
                    dk_sum = jnp.concatenate([dk_sum[:span] + dk_part, dk_sum[span:]], axis=0)
            dq_pieces.append(jnp.concatenate(dq_blocks[::-1], axis=1))
            dk_pieces.append(dk_sum)
            dv_pieces.append(dv_sum)
        lane = lax.broadcasted_iota(jnp.int32, (WIN, PAIR), 1) < HEAD_DIM
        dq = jnp.transpose(jnp.concatenate(dq_pieces, axis=0)) * SCALE
        dk = jnp.where(lane, dk_pieces[0], dk_pieces[1])
        dv = jnp.where(lane, dv_pieces[0], dv_pieces[1])
        dqkv[:, at : at + PAIR] = dq.astype(BF16)
        dqkv[:, D + at : D + at + PAIR] = dk.astype(BF16)
        dqkv[:, 2 * D + at : 2 * D + at + PAIR] = dv.astype(BF16)
    h_t = jnp.transpose(x_ref[:, 0, 0].reshape(WIN, D))
    for m in range(3):
        cols = slice(D * m, D * (m + 1))
        rows = dqkv[:, cols]
        acc[:, cols] += dot_nn(h_t, rows)
        if m != 1:
            db_ref[(m // 2) : (m // 2) + 1, :] += jnp.sum(
                rows.astype(F32), axis=0, keepdims=True
            )
    total = da_ref[0]
    for m in range(3):
        cols = slice(D * m, D * (m + 1))
        total = total + dot_nt(dqkv[:, cols], full[:, cols])
    dx_ref[:, 0] = total.astype(BF16).reshape(dx_ref.shape[0], dx_ref.shape[2], D)

    @pl.when(step == pl.num_programs(0) - 1)
    def _():
        write_gradient(
            functools.partial(qkv_block, acc), QKV_BLOCKS, part, meta[wins], dw_refs
        )


def normal_parts(u):
    size = jnp.abs(u)
    t = 1.0 / (1.0 + (0.3275911 * ROOT_HALF) * size)
    expo = jnp.exp(-0.5 * (u * u))
    poly = t * (
        0.5 * 0.254829592
        + t
        * (
            -0.5 * 0.284496736
            + t * (0.5 * 1.421413741 + t * (-0.5 * 1.453152027 + t * (0.5 * 1.061405429)))
        )
    )
    tail = poly * expo
    return jnp.where(u >= 0.0, 1.0 - tail, tail), expo


def norm_stats(rows):
    mean = jnp.mean(rows, axis=1, keepdims=True)
    centered = rows - mean
    spread = jnp.mean(centered * centered, axis=1, keepdims=True)
    inverse = lax.rsqrt(spread + NORM_EPS)
    return centered * inverse, inverse


def norm_back(d_rows, normal, inverse):
    mean_d = jnp.mean(d_rows, axis=1, keepdims=True)
    mean_dn = jnp.mean(d_rows * normal, axis=1, keepdims=True)
    return inverse * (d_rows - mean_d - normal * mean_dn)


def fill_ffn_matrices(w_out, w_up, w_down, packing, refs, core):
    side = D // BLK
    for base, offset, ref in each_piece(packing, refs, core):
        blocks, rows = ref.shape[:2]
        for n in range(blocks):
            full, i, j = ffn_place(base + n, (w_out, w_up, w_down))
            full[pl.ds(BLK * i + offset, rows), BLK * j : BLK * (j + 1)] = ref[n]


def ffn_place(b, matrices):
    side = D // BLK
    if b < side * side:
        return matrices[0], b // side, b % side
    b -= side * side
    if b < side * FF_CHUNKS:
        return matrices[1], b // FF_CHUNKS, b % FF_CHUNKS
    b -= side * FF_CHUNKS
    return matrices[2], b // side, b % side


def ffn_kernel(packing, wins, tokens, part, first, last, split, meta, *refs):
    cot_ref, x_ref, o_ref, vec = refs[:4]
    weight_refs = refs[4 : 4 + (2 * len(packing) or 1)]
    refs = refs[4 + len(weight_refs) :]
    if not first:
        prev, refs = refs[0], refs[1:]
    out_ref, da_ref, do_ref = refs[:3]
    refs = refs[3:]
    dw_refs, refs = refs[: 2 if split else 1], refs[2 if split else 1 :]
    vg_ref, w_out, w_up, w_down, acc_out, acc_up, acc_down, z_ref, gp_ref, du_ref = refs
    step = pl.program_id(0)
    length = meta[step]
    accs = (acc_out, acc_up, acc_down)

    def acc_block(b, offset, rows):
        full, i, j = ffn_place(b, accs)
        if full is acc_down:
            i, j = j, i
        return full.at[pl.ds(BLK * i + offset, rows), BLK * j : BLK * (j + 1)]

    @pl.when(step == 0)
    def _():
        fill_ffn_matrices(w_out, w_up, w_down, packing, weight_refs, meta[wins])
        for b in range(REST_BLOCKS):
            acc_block(b, 0, BLK)[...] = (
                jnp.zeros((BLK, BLK), F32) if first else prev[b].astype(F32)
            )
        vg_ref[...] = jnp.zeros_like(vg_ref)

    def add_row(row, values, at=0):
        vg_ref[row : row + 1, at : at + values.shape[1]] += jnp.sum(
            values.astype(F32), axis=0, keepdims=True
        )

    bias_out, bias_down = vec[2:3, :], vec[7:8, :]
    gain_one, shift_one = vec[8:9, :], vec[9:10, :]
    gain_two, shift_two = vec[10:11, :], vec[11:12, :]
    attended = o_ref[0]
    mixed = x_ref[:, 0, 0].reshape(WIN, D).astype(F32) + (dot_nn(attended, w_out[...]) + bias_out)
    n_one, inv_one = norm_stats(mixed)
    normed = n_one * gain_one + shift_one
    normed_low = normed.astype(BF16)
    for c in range(FF // D):
        cols = slice(D * c, D * (c + 1))
        u = dot_nn(normed_low, w_up[:, cols]) + vec[3 + c : 4 + c, :]
        phi, expo = normal_parts(u)
        z_ref[:, cols] = (u * phi).astype(BF16)
        gp_ref[:, cols] = phi + (u * expo) * DENSITY
    summed = normed + (dot_nn(z_ref[...], w_down[...]) + bias_down)
    n_two, inv_two = norm_stats(summed)
    result = (n_two * gain_two + shift_two).astype(BF16)
    out_ref[:, 0] = result.reshape(out_ref.shape[0], out_ref.shape[2], D)

    places = lax.broadcasted_iota(jnp.int32, (WIN, 1), 0)
    valid = jnp.where(places < length, 1.0 / tokens, 0.0).astype(F32)
    seed = cot_ref[:, 0].reshape(WIN, D).astype(F32) * valid
    add_row(10, seed * n_two)
    add_row(11, seed)
    d_summed = norm_back(seed * gain_two, n_two, inv_two)
    d_ff = d_summed.astype(BF16)
    add_row(7, d_ff)
    for c in range(FF // D):
        cols = slice(D * c, D * (c + 1))
        d_z = dot_nt(d_ff, w_down[cols, :])
        d_u = (d_z * gp_ref[:, cols]).astype(BF16)
        add_row(3 + c, d_u)
        du_ref[:, cols] = d_u
    d_ff_t = jnp.transpose(d_ff)
    normed_t = jnp.transpose(normed_low)
    for c in range(FF // D):
        cols = slice(D * c, D * (c + 1))
        acc_down[:, cols] += dot_nn(d_ff_t, z_ref[:, cols])
        acc_up[:, cols] += dot_nn(normed_t, du_ref[:, cols])
    d_normed = d_summed + dot_nt(du_ref[...], w_up[...])
    add_row(8, d_normed * n_one)
    add_row(9, d_normed)
    d_mixed = norm_back(d_normed * gain_one, n_one, inv_one)
    da_ref[0] = d_mixed
    d_branch = d_mixed.astype(BF16)
    add_row(2, d_branch)
    acc_out[...] += dot_nn(jnp.transpose(attended), d_branch)
    do_ref[0] = dot_nt(d_branch, w_out[...]).astype(BF16)

    @pl.when(step == pl.num_programs(0) - 1)
    def _():
        if last:
            for j in range(D // BLK):
                for i in range(FF_CHUNKS):
                    at = (slice(BLK * j, BLK * (j + 1)), slice(BLK * i, BLK * (i + 1)))
                    acc_down[at] = jnp.transpose(acc_down[at])
        write_gradient(
            lambda b, offset, rows: acc_block(b, offset, rows)[...],
            REST_BLOCKS, part, meta[wins], dw_refs,
        )


def whole_spec(shape):
    zeros = (0,) * len(shape)
    return pl.BlockSpec(shape, lambda w, m: zeros, pipeline_mode=pl.Buffered(1))


def total_spec(shape):
    zeros = (0,) * len(shape)
    return pl.BlockSpec(shape, lambda w, m: zeros)


def window_spec(begin, *shape):
    zeros = (0,) * len(shape)
    return pl.BlockSpec((1,) + shape, lambda w, m: (begin + w,) + zeros)


def segment_spec(dp, seg, begin=0):
    return pl.BlockSpec((dp, 1, seg, D), lambda w, m: (0, begin + w, 0, 0))


def input_spec(dp, seg, step, begin=0):
    return pl.BlockSpec((dp, 1, 1, seg, D), lambda w, m: (0, step, begin + w, 0, 0))


def gradient_outs(blocks, last, part):
    if not last:
        return [jax.ShapeDtypeStruct((blocks, BLK, BLK), BF16)]
    return [jax.ShapeDtypeStruct((blocks, BLK // 2, BLK), BF16)] * 2


def run_kernel(kernel, wins, meta, ins, outs, scratch, flops, moved, aliases=None):
    return pl.pallas_call(
        kernel,
        grid_spec=pltpu.PrefetchScalarGridSpec(
            num_scalar_prefetch=1,
            grid=(wins,),
            in_specs=[spec for _, spec in ins],
            out_specs=[spec for _, spec in outs],
            scratch_shapes=scratch,
        ),
        out_shape=[shape for shape, _ in outs],
        input_output_aliases=aliases or {},
        compiler_params=pltpu.CompilerParams(
            dimension_semantics=("arbitrary",), vmem_limit_bytes=56 * 1024 * 1024
        ),
        cost_estimate=pl.CostEstimate(
            flops=flops, bytes_accessed=moved, transcendentals=wins * WIN * FF
        ),
    )(meta, *[values for values, _ in ins])


def call_attention(i, meta, x, packing, weight_parts, bias):
    dp, _, wins, seg, _ = x.shape
    shape = jax.ShapeDtypeStruct
    return run_kernel(
        functools.partial(attention_kernel, packing, wins),
        wins,
        meta,
        [(x, input_spec(dp, seg, i)), (bias, whole_spec(bias.shape))]
        + [(piece, whole_spec(piece.shape)) for piece in weight_parts],
        [
            (shape((wins, WIN, 3 * D), BF16), window_spec(0, WIN, 3 * D)),
            (shape((wins, WIN, D), BF16), window_spec(0, WIN, D)),
            (shape((wins, HEADS, WIN), F32), window_spec(0, HEADS, WIN)),
        ],
        [pltpu.VMEM((D, 3 * D), BF16), pltpu.VMEM((WIN, WIN), F32)],
        wins * 3_000_000_000,
        wins * 1_000_000,
    )


def call_ffn(i, tokens, part, last, meta, cot, x, attended, packing, weight_parts, vec, prev):
    dp, _, wins, seg, _ = x.shape
    shape = jax.ShapeDtypeStruct
    first = prev is None
    ins = [
        (cot, segment_spec(dp, seg)),
        (x, input_spec(dp, seg, i)),
        (attended, window_spec(0, WIN, D)),
        (vec, whole_spec(vec.shape)),
    ] + [(piece, whole_spec(piece.shape)) for piece in weight_parts]
    if not first:
        ins.append((prev, whole_spec(prev.shape)))
    split = last and part % 16 == 0
    return run_kernel(
        functools.partial(ffn_kernel, packing, wins, tokens, part, first, last, split),
        wins,
        meta,
        ins,
        [
            (shape((dp, wins, seg, D), BF16), segment_spec(dp, seg)),
            (shape((wins, WIN, D), F32), window_spec(0, WIN, D)),
            (shape((wins, WIN, D), BF16), window_spec(0, WIN, D)),
        ]
        + [(out, total_spec(out.shape)) for out in gradient_outs(REST_BLOCKS, split, part)]
        + [(shape((ROWS_VEC, D), F32), total_spec((ROWS_VEC, D)))],
        [
            pltpu.VMEM((D, D), BF16),
            pltpu.VMEM((D, FF), BF16),
            pltpu.VMEM((FF, D), BF16),
            pltpu.VMEM((D, D), F32),
            pltpu.VMEM((D, FF), F32),
            pltpu.VMEM((D, FF), F32),
            pltpu.VMEM((WIN, FF), BF16),
            pltpu.VMEM((WIN, FF), F32),
            pltpu.VMEM((WIN, FF), BF16),
        ],
        wins * 18_000_000_000,
        wins * 12_000_000,
    )


def call_attention_back(
    i, begin, count, part, last, meta, packing, weight_parts, x, qkv, d_o, lse, d_mixed, prev, dx
):
    dp, _, wins, seg, _ = x.shape
    shape = jax.ShapeDtypeStruct
    first = prev is None
    ins = [
        (x, input_spec(dp, seg, i, begin)),
        (qkv, window_spec(begin, WIN, 3 * D)),
        (d_o, window_spec(begin, WIN, D)),
        (lse, window_spec(begin, HEADS, WIN)),
        (d_mixed, window_spec(begin, WIN, D)),
    ] + [(piece, whole_spec(piece.shape)) for piece in weight_parts]
    if not first:
        ins.append((prev, whole_spec(prev.shape)))
    aliases = {}
    if dx is not None:
        ins.append((dx, pl.BlockSpec(memory_space=pl.ANY)))
        aliases = {len(ins): 0}
    split = last and part % 16 == 0
    return run_kernel(
        functools.partial(
            attention_back_kernel, packing, wins, begin, part, first, dx is not None, split
        ),
        count,
        meta,
        ins,
        [(shape((dp, wins, seg, D), BF16), segment_spec(dp, seg, begin))]
        + [(out, total_spec(out.shape)) for out in gradient_outs(QKV_BLOCKS, split, part)]
        + [(shape((8, D), F32), total_spec((8, D)))],
        [
            pltpu.VMEM((D, 3 * D), BF16),
            pltpu.VMEM((WIN, WIN), F32),
            pltpu.VMEM((WIN, 3 * D), BF16),
            pltpu.VMEM((D, 3 * D), F32),
        ],
        count * 12_500_000_000,
        count * 8_000_000,
        aliases,
    )


def split_first_kernel(bits, keep, got, *outs):
    for y in range(2):
        for which in range(2):
            at = 2 * y + (bits[0] if which == 0 else 1 - bits[0])
            outs[which][:, y] = (keep[0, :, at].astype(F32) + got[0, :, at].astype(F32)).astype(
                BF16
            )
    for x in range(2):
        for which in range(2):
            at = 2 * (bits[1] if which == 0 else 1 - bits[1]) + x
            outs[2 + which][:, x] = (
                keep[1, :, at].astype(F32) + got[1, :, at].astype(F32)
            ).astype(BF16)


def split_second_kernel(bits, *refs):
    for side in range(2):
        mine, got = refs[2 * side : 2 * side + 2]
        for which in range(2):
            bit = bits[1 - side]
            at = bit if which == 0 else 1 - bit
            refs[4 + 2 * side + which][...] = (
                mine[:, at].astype(F32) + got[:, at].astype(F32)
            ).astype(BF16)


def slabs_kernel(dp, me_ref, *refs):
    pairs, outs, total = refs[: len(refs) - dp - 1], refs[-dp - 1 : -1], refs[-1]
    base = 0
    for n in range(0, len(pairs), 2):
        blocks = pairs[n].shape[0]
        total[base : base + blocks] = pairs[n][...].astype(F32) + pairs[n + 1][...].astype(F32)
        base += blocks
    owned = outs[0].shape[0]
    for s in range(dp):
        outs[s][...] = total[pl.ds((me_ref[0] ^ s) * owned, owned)].astype(outs[s].dtype)


def call_small(kernel, steps, scalars, ins, outs, scratch=()):
    def spec(shape, axis):
        block = tuple(n // steps if d == axis else n for d, n in enumerate(shape))
        return pl.BlockSpec(block, lambda g, m: tuple(g if d == axis else 0 for d in range(len(shape))))

    return pl.pallas_call(
        kernel,
        grid_spec=pltpu.PrefetchScalarGridSpec(
            num_scalar_prefetch=1,
            grid=(steps,),
            in_specs=[spec(values.shape, axis) for values, axis in ins],
            out_specs=[spec(shape.shape, axis) for shape, axis in outs],
            scratch_shapes=list(scratch),
        ),
        out_shape=[shape for shape, _ in outs],
        compiler_params=pltpu.CompilerParams(
            dimension_semantics=("arbitrary",), vmem_limit_bytes=32 * 1024 * 1024
        ),
    )(scalars, *[values for values, _ in ins])


def split_first(bits, keep, got):
    blocks, height, cols = keep.shape
    half = blocks // 2
    view = (2, half, 4, height // 4, cols)
    out = jax.ShapeDtypeStruct((half, 2, height // 4, cols), BF16)
    return call_small(
        split_first_kernel,
        max(half // 6, 1),
        bits,
        [(keep.reshape(view), 1), (got.reshape(view), 1)],
        [(out, 0)] * 4,
    )


def split_second(bits, *parts):
    half, _, rows, cols = parts[0].shape
    out = jax.ShapeDtypeStruct((half, rows, cols), BF16)
    return call_small(
        split_second_kernel, 1, bits, [(part, 0) for part in parts], [(out, 0)] * 4
    )


def make_slabs(dp, me, parts):
    _, rows, cols = parts[0].shape
    blocks = sum(part.shape[0] for part in parts) // 2
    shape = (blocks // dp, rows, cols)
    return call_small(
        functools.partial(slabs_kernel, dp),
        1,
        me,
        [(part, None) for part in parts],
        [(jax.ShapeDtypeStruct(shape, F32 if s == 0 else BF16), None) for s in range(dp)],
        [pltpu.VMEM((blocks, rows, cols), F32)],
    )


def swap(values, axis, size, k):
    return lax.ppermute(values, axis, [(i, i ^ k) for i in range(size)])


def bits_of(size):
    return [1 << i for i in range(size.bit_length() - 1)]


def hop_orders(seq_count):
    high = [k for k in bits_of(seq_count) if k > 1]
    return (high, high[::-1])


def gather_hop(state, k, seq_count, seq_index, *marks):
    cur, lead = state
    got = after(swap(cur, "seq", seq_count, k), *marks)
    odd = (seq_index & k) != 0
    cur = jnp.stack([jnp.where(odd, got, cur), jnp.where(odd, cur, got)], axis=0)
    return cur, [k] + lead


def gather_end(state):
    cur, lead = state
    count = len(lead)
    blocks, rows, cols = cur.shape[count:]
    axes = [count] + [lead.index(k) for k in sorted(lead, reverse=True)] + [count + 1, count + 2]
    return cur.transpose(axes).reshape(blocks, rows << count, cols)


def halves(cur):
    half = cur.shape[0] // 2
    return [cur[:half], cur[half:]]


def gather_split(cur, seq_count, seq_index):
    done = []
    for part, order in zip(halves(cur), hop_orders(seq_count)):
        state = (part, [])
        for k in order + [1]:
            state = gather_hop(state, k, seq_count, seq_index)
        done.append(gather_end(state))
    return jnp.concatenate(done, axis=0)


def pack_weights(rows, orders, seq_count, seq_index):
    states = [(part, []) for part in halves(rows)]
    for step in range(len(orders[0])):
        states = [
            gather_hop(state, order[step], seq_count, seq_index)
            for state, order in zip(states, orders)
        ]
        if step == 0:
            cur, lead = states[0]
            axis = len(lead)
            states = [
                (lax.slice_in_dim(cur, 0, QKV_BLOCKS, axis=axis), lead),
                (lax.slice_in_dim(cur, QKV_BLOCKS, cur.shape[axis], axis=axis), lead),
                states[1],
            ]
            orders = (orders[0], orders[0], orders[1])
    return states


def join_cores(states, seq_count, seq_index, *marks):
    if states[0][0].shape[-2] % 16:
        states = [gather_hop(state, 1, seq_count, seq_index) for state in states]
        return (), [jnp.concatenate([gather_end(state) for state in states], axis=0)]
    parts = []
    for cur, _ in states:
        parts += [cur, after(swap(cur, "seq", seq_count, 1), *marks)]
    return tuple(tuple(lead) for _, lead in states), parts


def scatter_first(parts, seq_count, seq_index, *marks):
    left = sorted(bits_of(seq_count), reverse=True)
    blocks, height, cols = parts[0].shape
    if len(parts) == 2:
        mine, other = parts
        rows = 2 * height // seq_count
    else:
        rows = height // seq_count
        cur = parts[0].reshape(blocks, seq_count // 2, 2, rows, cols)
        mine, other = [
            lax.dynamic_index_in_dim(cur, bit, 2, keepdims=False)
            for bit in (seq_index % 2, 1 - seq_index % 2)
        ]
    got = after(swap(other, "seq", seq_count, 1), *marks).reshape(mine.shape)
    cur = mine.astype(F32) + got.astype(F32)
    left.remove(1)
    cur = cur.astype(BF16).reshape([blocks] + [2] * len(left) + [rows, cols])
    return [(half, left) for half in halves(cur)]


def scatter_hop(state, k, seq_count, seq_index, *marks):
    cur, left = state
    axis = 1 + left.index(k)
    bit = (seq_index // k) % 2
    mine = lax.dynamic_index_in_dim(cur, bit, axis, keepdims=False)
    other = lax.dynamic_index_in_dim(cur, 1 - bit, axis, keepdims=False)
    got = after(swap(other, "seq", seq_count, k), *marks)
    cur = (mine.astype(F32) + got.astype(F32)).astype(BF16)
    return cur, [b for b in left if b != k]


def after(values, *marks):
    if not marks:
        return values
    return lax.optimization_barrier((values, marks))[0]


def body(
    inputs,
    cotangent,
    lengths,
    weights,
    vectors,
    positions,
    left_stats,
    right_stats,
    left_roots,
    right_roots,
    vector_second,
    position_second,
):
    seq_count = lax.axis_size("seq")
    dp_count = lax.axis_size("dp")
    seq_index = lax.axis_index("seq")
    dp_index = lax.axis_index("dp")
    micro, wins_dev, segment, model_width = inputs.shape
    wins = wins_dev // dp_count
    total_tokens = micro * wins_dev * seq_count * segment * dp_count
    owned, row_part, _ = weights.shape
    def exchange(rows):
        return lax.all_to_all(rows, "dp", 0, 0, tiled=True)

    grouped = (dp_count, wins, segment, model_width)
    own = weights.astype(BF16)
    orders = hop_orders(seq_count)
    hops = len(orders[0])

    def scatter_both(states, step, *marks):
        return [
            scatter_hop(state, order[step], seq_count, seq_index, *marks)
            for state, order in zip(states, orders)
        ]

    shards = [own] + [swap(own, "dp", dp_count, s) for s in range(1, dp_count)]
    weight_rows = jnp.concatenate(
        [lax.select_n(dp_index ^ j, *shards) for j in range(dp_count)], axis=0
    )
    hidden = (inputs.astype(F32) + positions[None, None]).astype(BF16)
    hidden = jnp.swapaxes(hidden.reshape((micro,) + grouped), 0, 1)
    x = exchange(after(hidden, shards[1]) if dp_count > 1 else hidden)
    groups = pack_weights(weight_rows, orders, seq_count, seq_index)
    packing_qkv, parts_qkv = join_cores(groups[:1], seq_count, seq_index)
    roots_full = lax.all_gather(right_roots.astype(BF16), "seq", axis=1, tiled=True)

    vec = vectors.reshape(-1, D)
    bias_qv = jnp.concatenate([vec[0:2], jnp.zeros((6, D), F32)], axis=0)
    vec_pad = jnp.concatenate([vec, jnp.zeros((ROWS_VEC - vec.shape[0], D), F32)], axis=0)

    metas = [
        lax.dynamic_index_in_dim(
            lengths[i].reshape(dp_count, wins), dp_index, 0, keepdims=False
        )
        for i in range(micro)
    ]
    metas = [jnp.concatenate([lens, (seq_index % 2)[None]]) for lens in metas]
    cots = []
    for i in range(micro):
        cots.append(exchange(after(cotangent[i].reshape(grouped), cots[-1] if i else x)))

    forward, ffn, out_got, dx_got = [], [], [], []
    mark = ()
    for i in range(micro):
        forward.append(
            call_attention(i, after(metas[i], *mark), x, packing_qkv, parts_qkv, bias_qv)
        )
        mark = (forward[-1][2],)
    packing_rest, parts_rest = join_cores(groups[1:], seq_count, seq_index, forward[0][2])
    dw_rest = [None]
    vec_sums = jnp.zeros((ROWS_VEC, D), F32)
    for i in range(micro):
        qkv, attended, lse = forward[i]
        out, d_mixed, d_o, *dw_rest, vg = call_ffn(
            i, total_tokens, row_part, i == micro - 1, after(metas[i], *mark), cots[i], x,
            attended, packing_rest, parts_rest, vec_pad, dw_rest[0],
        )
        out_got.append(exchange(out))
        ffn.append((d_mixed, d_o))
        vec_sums = vec_sums + vg
        mark = (vg,)

    fast = seq_count == 8 and row_part % 16 == 0
    bits = jnp.stack([(seq_index // 2) % 2, (seq_index // 4) % 2]).astype(jnp.int32)

    def split_hops(parts, count, *marks):
        mine_a, send_a, mine_b, send_b = parts
        k_a, k_b = (2, 4) if count == 0 else (4, 2)
        got_a = after(swap(send_a, "seq", seq_count, k_a), *marks)
        got_b = after(swap(send_b, "seq", seq_count, k_b), *marks)
        if count == 0:
            return split_second(bits, mine_a, got_a, mine_b, got_b)
        return [mine_a, got_a, mine_b, got_b]

    def rest_step(state, step, *marks):
        if fast:
            if step == 0:
                got = after(swap(dw_rest[1], "seq", seq_count, 1), *marks)
                return split_first(bits, dw_rest[0], got)
            return split_hops(state, step - 1, *marks)
        if step == 0:
            return scatter_first(dw_rest, seq_count, seq_index, *marks)
        return scatter_both(state, step - 1, *marks)

    rest, rest_done = None, 0
    dw_qkv = [None]
    gates = mark + (out_got[0],)
    for i in range(micro):
        qkv, attended, lse = forward[i]
        last = i == micro - 1
        if i == 1:
            gates = gates + (out_got[1],)
        dx, *dw_qkv, db = call_attention_back(
            i, 0, wins, row_part, last, after(metas[i], gates), packing_qkv, parts_qkv, x,
            qkv, ffn[i][1], lse, ffn[i][0], dw_qkv[0], None,
        )
        vec_sums = vec_sums + jnp.concatenate([db, jnp.zeros_like(db)], axis=0)
        rest = rest_step(rest, rest_done, db)
        rest_done += 1
        gates = (db,) + (tuple(rest) if fast else (rest[0][0], rest[1][0]))
        dx_got.append(exchange(after(dx, *dx_got[-1:])))

    dw_qkv = after(dw_qkv, dx_got[0]) if micro > 1 else dw_qkv
    if fast:
        got = swap(dw_qkv[1], "seq", seq_count, 1)
        states = split_first(bits, dw_qkv[0], got)
        while rest_done <= hops:
            rest = rest_step(rest, rest_done)
            rest_done += 1
        for step in range(hops):
            states = split_hops(states, step)
        slabs = make_slabs(
            dp_count, after(dp_index[None].astype(jnp.int32), dx_got[-1]), states + rest
        )
    else:
        states = scatter_first(dw_qkv, seq_count, seq_index)
        while rest_done <= hops:
            rest = rest_step(rest, rest_done)
            rest_done += 1
        for step in range(hops):
            states = scatter_both(states, step)
        joined = jnp.concatenate([cur for cur, _ in states + rest], axis=0)
        joined = joined.reshape((dp_count, owned) + joined.shape[1:])
        slabs = [
            lax.dynamic_index_in_dim(joined, dp_index ^ s, 0, keepdims=False)
            for s in range(dp_count)
        ]
    grad_rows = slabs[0].astype(F32)
    for s in range(1, dp_count):
        grad_rows = grad_rows + swap(slabs[s], "dp", dp_count, s).astype(F32)
    grad_low = grad_rows.astype(BF16)
    grad_full = gather_split(grad_low, seq_count, seq_index)

    row_start = seq_index * row_part

    def batched(spec, left, right):
        return jnp.einsum(spec, left, right, preferred_element_type=F32)

    left_new = DECAY * left_stats + (1.0 - DECAY) * batched("bij,bkj->bik", grad_low, grad_full)
    column_part = lax.dynamic_slice_in_dim(grad_full, row_start, row_part, 2)
    right_new = DECAY * right_stats + (1.0 - DECAY) * batched(
        "bki,bkj->bij", column_part, grad_full
    )
    left_applied = batched("bij,bjk->bik", left_roots.astype(BF16), grad_full)
    step_rows = batched("bij,bjk->bik", left_applied.astype(BF16), roots_full)
    weights_new = weights - MATRIX_RATE * step_rows

    place_sum = sum(jnp.sum(got.astype(F32), axis=(0, 1)) for got in dx_got)
    whole = (wins_dev, segment, model_width)
    layer_rows = [got.reshape(whole) for got in after(out_got, dx_got[-1])]
    input_rows = [got.astype(F32).reshape(whole) for got in after(dx_got, dx_got[-1])]
    place_sum = jnp.concatenate([place_sum, vec_sums], axis=0)
    for k in bits_of(seq_count):
        low = place_sum.astype(BF16)
        place_sum = low.astype(F32) + swap(low, "seq", seq_count, k).astype(F32)
    vec_sums = place_sum[segment:]
    place_sum = place_sum[:segment]
    for k in bits_of(dp_count):
        vec_sums = vec_sums + swap(vec_sums, "dp", dp_count, k)
    vector_grads = vec_sums[: vec.shape[0]].reshape(-1)
    vector_second_new = DECAY * vector_second + (1.0 - DECAY) * vector_grads * vector_grads
    vectors_new = vectors - VECTOR_RATE * vector_grads / (jnp.sqrt(vector_second_new) + ROOT_EPS)
    position_grads = place_sum
    position_second_new = DECAY * position_second + (1.0 - DECAY) * position_grads * position_grads
    positions_new = positions - VECTOR_RATE * position_grads / (
        jnp.sqrt(position_second_new) + ROOT_EPS
    )
    return (
        jnp.stack(layer_rows, axis=0),
        jnp.stack(input_rows, axis=0),
        grad_rows,
        left_new,
        right_new,
        weights_new,
        vector_grads,
        vector_second_new,
        vectors_new,
        position_grads,
        position_second_new,
        positions_new,
    )


def solution(mesh):
    rows = P(None, "seq", "dp", None)
    blocks = P("dp", "seq", None)
    in_specs = (
        rows, rows, P(None, "seq"), blocks, P(), P("dp", None),
        blocks, blocks, blocks, blocks, P(), P("dp", None),
    )
    out_specs = (
        rows, rows, blocks, blocks, blocks, blocks,
        P(), P(), P(), P("dp", None), P("dp", None), P("dp", None),
    )
    return jax.shard_map(body, mesh=mesh, in_specs=in_specs, out_specs=out_specs, check_vma=False)
```

```python
import functools
import itertools

import jax
import jax.numpy as jnp
from jax import lax
from jax.experimental import pallas as pl
from jax.experimental.pallas import tpu as pltpu
from jax.sharding import PartitionSpec as P

HEADS = 8
FF = 2048
WIN = 512
D = 512
BLK = 256
QKV_BLOCKS = 12
REST_BLOCKS = 36
HEAD_DIM = D // HEADS
PAIR = 2 * HEAD_DIM
PAIRS = HEADS // 2
FF_CHUNKS = FF // BLK
ROWS_VEC = 16

NORM_EPS = 1e-05
ROOT_EPS = 1e-08
DECAY = 0.5
MATRIX_RATE = 0.5
VECTOR_RATE = 0.2
MASKED = -1e30
SCALE = HEAD_DIM ** (-0.5)
ROOT_HALF = 0.7071067811865476
DENSITY = 0.3989422804014327

F32 = jnp.float32
BF16 = jnp.bfloat16


def dot_nn(left, right):
    return lax.dot_general(left, right, (((1,), (0,)), ((), ())), preferred_element_type=F32)


def dot_nt(left, right):
    return lax.dot_general(left, right, (((1,), (1,)), ((), ())), preferred_element_type=F32)


def each_piece(packing, refs, core):
    if not packing:
        yield 0, 0, refs[0]
        return
    base = 0
    for side, bits in enumerate(packing):
        for which in range(2):
            ref = refs[2 * side + which]
            blocks, rows = ref.shape[len(bits)], ref.shape[len(bits) + 1]
            last = core if which == 0 else 1 - core
            for at in itertools.product(range(2), repeat=len(bits)):
                first = sum(k * v for k, v in zip(bits, at))
                yield base, pl.multiple_of((first + last) * rows, rows), ref.at[at]
        base += blocks


def fill_qkv_matrix(full, packing, refs, core):
    side = D // BLK
    for base, offset, ref in each_piece(packing, refs, core):
        blocks, rows = ref.shape[:2]
        for n in range(blocks):
            b = base + n
            m, i, j = b // (side * side), (b // side) % side, b % side
            cols = slice(D * m + BLK * j, D * m + BLK * (j + 1))
            full[pl.ds(BLK * i + offset, rows), cols] = ref[n]


def fill_stack(stack, packing, refs, core):
    for base, offset, ref in each_piece(packing, refs, core):
        blocks, rows = ref.shape[:2]
        for n in range(blocks):
            stack[base + n, pl.ds(offset, rows), :] = ref[n]


def write_gradient(block_at, blocks, rows, core, outs):
    for b in range(blocks):
        if len(outs) == 1:
            outs[0][b] = block_at(b, 0, BLK).astype(BF16)
            continue
        for which, out in enumerate(outs):
            last = core if which == 0 else 1 - core
            for n in range(BLK // (2 * rows)):
                offset = pl.multiple_of((2 * n + last) * rows, rows)
                out[b, n * rows : (n + 1) * rows, :] = block_at(b, offset, rows).astype(BF16)


def fill_mask(mask, length):
    for i in range(WIN // BLK):
        keys = lax.broadcasted_iota(jnp.int32, (BLK, WIN), 0) + BLK * i
        queries = lax.broadcasted_iota(jnp.int32, (BLK, WIN), 1)
        keep = (keys <= queries) & (keys < length)
        mask[BLK * i : BLK * (i + 1), :] = jnp.where(keep, 0.0, MASKED).astype(F32)


def half_marks():
    lane = lax.broadcasted_iota(jnp.int32, (1, PAIR), 1)
    low = jnp.where(lane < HEAD_DIM, 1.0, 0.0)
    return (low.astype(BF16), (1.0 - low).astype(BF16))


def attention_kernel(packing, wins, meta, x_ref, bias, *refs):
    weight_refs = refs[: 2 * len(packing) or 1]
    qkv_ref, o_ref, lse_ref, full, mask = refs[len(weight_refs) :]
    step = pl.program_id(0)

    @pl.when(step == 0)
    def _():
        fill_qkv_matrix(full, packing, weight_refs, meta[wins])

    hidden = x_ref[:, 0].reshape(WIN, D)
    for m in range(3):
        cols = slice(D * m, D * (m + 1))
        rows = dot_nn(hidden, full[:, cols])
        if m != 1:
            rows = rows + bias[(m // 2) : (m // 2) + 1, :]
        qkv_ref[0, :, cols] = rows.astype(BF16)
    fill_mask(mask, meta[step])
    marks = half_marks()
    for p in range(PAIRS):
        at = PAIR * p
        q8 = qkv_ref[0, :, at : at + PAIR] * jnp.asarray(SCALE, BF16)
        key = qkv_ref[0, :, D + at : D + at + PAIR]
        val_t = jnp.transpose(qkv_ref[0, :, 2 * D + at : 2 * D + at + PAIR])
        pieces = []
        for h in range(2):
            key_h = key * marks[h]
            row = 2 * p + h
            blocks = []
            for qb in range(WIN // BLK):
                cols = slice(BLK * qb, BLK * (qb + 1))
                span = BLK * (qb + 1)
                s_t = dot_nt(key_h[:span], q8[cols]) + mask[:span, cols]
                top = jnp.max(s_t, axis=0, keepdims=True)
                expo = jnp.exp(s_t - top)
                total = jnp.sum(expo, axis=0, keepdims=True)
                probs = (expo * (1.0 / total)).astype(BF16)
                lse_ref[0, row : row + 1, cols] = top + jnp.log(total)
                blocks.append(dot_nn(val_t[HEAD_DIM * h : HEAD_DIM * (h + 1), :span], probs))
            pieces.append(jnp.concatenate(blocks, axis=1))
        o_t = jnp.concatenate(pieces, axis=0)
        o_ref[0, :, at : at + PAIR] = jnp.transpose(o_t).astype(BF16)


def qkv_block(acc, b, offset, rows):
    side = D // BLK
    m, i, j = b // (side * side), (b // side) % side, b % side
    return acc[pl.ds(BLK * i + offset, rows), D * m + BLK * j : D * m + BLK * (j + 1)]


def attention_back_kernel(packing, wins, part, split, meta, *refs):
    x_ref, qkv_ref, do_ref, lse_ref, da_ref = refs[:5]
    weight_refs = refs[5 : 5 + (2 * len(packing) or 1)]
    refs = refs[5 + len(weight_refs) :]
    dx_ref, refs = refs[0], refs[1:]
    dw_refs, refs = refs[: 2 if split else 1], refs[2 if split else 1 :]
    db_ref, full, mask, dqkv, acc = refs
    step = pl.program_id(0)

    @pl.when(step == 0)
    def _():
        fill_qkv_matrix(full, packing, weight_refs, meta[wins])
        acc[...] = jnp.zeros_like(acc)
        db_ref[...] = jnp.zeros_like(db_ref)

    fill_mask(mask, meta[step])
    marks = half_marks()
    for p in range(PAIRS):
        at = PAIR * p
        q8 = qkv_ref[0, :, at : at + PAIR] * jnp.asarray(SCALE, BF16)
        key = qkv_ref[0, :, D + at : D + at + PAIR]
        val = qkv_ref[0, :, 2 * D + at : 2 * D + at + PAIR]
        d_o = do_ref[0, :, at : at + PAIR]
        key_t = jnp.transpose(key)
        dq_pieces, dk_pieces, dv_pieces = [], [], []
        for h in range(2):
            key_h = key * marks[h]
            val_h = val * marks[h]
            row = 2 * p + h
            dq_blocks = []
            dk_sum, dv_sum = None, None
            for qb in reversed(range(WIN // BLK)):
                cols = slice(BLK * qb, BLK * (qb + 1))
                span = BLK * (qb + 1)
                s_t = dot_nt(key_h[:span], q8[cols]) + mask[:span, cols]
                probs = jnp.exp(s_t - lse_ref[0, row : row + 1, cols])
                d_probs = dot_nt(val_h[:span], d_o[cols])
                delta = jnp.sum(probs * d_probs, axis=0, keepdims=True)
                d_s = (probs * (d_probs - delta)).astype(BF16)
                dv_part = dot_nn(probs.astype(BF16), d_o[cols])
                dk_part = dot_nn(d_s, q8[cols])
                dq_blocks.append(dot_nn(key_t[HEAD_DIM * h : HEAD_DIM * (h + 1), :span], d_s))
                if dv_sum is None:
                    dv_sum, dk_sum = dv_part, dk_part
                else:
                    dv_sum = jnp.concatenate([dv_sum[:span] + dv_part, dv_sum[span:]], axis=0)
                    dk_sum = jnp.concatenate([dk_sum[:span] + dk_part, dk_sum[span:]], axis=0)
            dq_pieces.append(jnp.concatenate(dq_blocks[::-1], axis=1))
            dk_pieces.append(dk_sum)
            dv_pieces.append(dv_sum)
        lane = lax.broadcasted_iota(jnp.int32, (WIN, PAIR), 1) < HEAD_DIM
        dq = jnp.transpose(jnp.concatenate(dq_pieces, axis=0)) * SCALE
        dk = jnp.where(lane, dk_pieces[0], dk_pieces[1])
        dv = jnp.where(lane, dv_pieces[0], dv_pieces[1])
        dqkv[:, at : at + PAIR] = dq.astype(BF16)
        dqkv[:, D + at : D + at + PAIR] = dk.astype(BF16)
        dqkv[:, 2 * D + at : 2 * D + at + PAIR] = dv.astype(BF16)
    h_t = jnp.transpose(x_ref[:, 0].reshape(WIN, D))
    for m in range(3):
        cols = slice(D * m, D * (m + 1))
        rows = dqkv[:, cols]
        acc[:, cols] += dot_nn(h_t, rows)
        if m != 1:
            db_ref[(m // 2) : (m // 2) + 1, :] += jnp.sum(
                rows.astype(F32), axis=0, keepdims=True
            )
    total = da_ref[0]
    for m in range(3):
        cols = slice(D * m, D * (m + 1))
        total = total + dot_nt(dqkv[:, cols], full[:, cols])
    dx_ref[:, 0] = total.astype(BF16).reshape(dx_ref.shape[0], dx_ref.shape[2], D)

    @pl.when(step == pl.num_programs(0) - 1)
    def _():
        write_gradient(
            functools.partial(qkv_block, acc), QKV_BLOCKS, part, meta[wins], dw_refs
        )


def normal_parts(u):
    size = jnp.abs(u)
    t = 1.0 / (1.0 + (0.3275911 * ROOT_HALF) * size)
    expo = jnp.exp(-0.5 * (u * u))
    poly = t * (
        0.5 * 0.254829592
        + t
        * (
            -0.5 * 0.284496736
            + t * (0.5 * 1.421413741 + t * (-0.5 * 1.453152027 + t * (0.5 * 1.061405429)))
        )
    )
    tail = poly * expo
    return jnp.where(u >= 0.0, 1.0 - tail, tail), expo


def norm_stats(rows):
    mean = jnp.mean(rows, axis=1, keepdims=True)
    centered = rows - mean
    spread = jnp.mean(centered * centered, axis=1, keepdims=True)
    inverse = lax.rsqrt(spread + NORM_EPS)
    return centered * inverse, inverse


def norm_back(d_rows, normal, inverse):
    mean_d = jnp.mean(d_rows, axis=1, keepdims=True)
    mean_dn = jnp.mean(d_rows * normal, axis=1, keepdims=True)
    return inverse * (d_rows - mean_d - normal * mean_dn)


def fill_ffn_matrices(w_out, w_up, w_down, packing, refs, core):
    side = D // BLK
    for base, offset, ref in each_piece(packing, refs, core):
        blocks, rows = ref.shape[:2]
        for n in range(blocks):
            full, i, j = ffn_place(base + n, (w_out, w_up, w_down))
            full[pl.ds(BLK * i + offset, rows), BLK * j : BLK * (j + 1)] = ref[n]


def ffn_place(b, matrices):
    side = D // BLK
    if b < side * side:
        return matrices[0], b // side, b % side
    b -= side * side
    if b < side * FF_CHUNKS:
        return matrices[1], b // FF_CHUNKS, b % FF_CHUNKS
    b -= side * FF_CHUNKS
    return matrices[2], b // side, b % side


def ffn_kernel(packing, wins, tokens, part, split, meta, *refs):
    cot_ref, x_ref, o_ref, vec = refs[:4]
    weight_refs = refs[4 : 4 + (2 * len(packing) or 1)]
    refs = refs[4 + len(weight_refs) :]
    out_ref, da_ref, do_ref = refs[:3]
    refs = refs[3:]
    dw_refs, refs = refs[: 2 if split else 1], refs[2 if split else 1 :]
    vg_ref, w_out, w_up, w_down, acc_out, acc_up, acc_down, z_ref, gp_ref, du_ref = refs
    step = pl.program_id(0)
    length = meta[step]
    accs = (acc_out, acc_up, acc_down)

    def acc_block(b, offset, rows):
        full, i, j = ffn_place(b, accs)
        if full is acc_down:
            i, j = j, i
        return full.at[pl.ds(BLK * i + offset, rows), BLK * j : BLK * (j + 1)]

    @pl.when(step == 0)
    def _():
        fill_ffn_matrices(w_out, w_up, w_down, packing, weight_refs, meta[wins])
        for acc in accs:
            acc[...] = jnp.zeros_like(acc)
        vg_ref[...] = jnp.zeros_like(vg_ref)

    def add_row(row, values, at=0):
        vg_ref[row : row + 1, at : at + values.shape[1]] += jnp.sum(
            values.astype(F32), axis=0, keepdims=True
        )

    bias_out, bias_down = vec[2:3, :], vec[7:8, :]
    gain_one, shift_one = vec[8:9, :], vec[9:10, :]
    gain_two, shift_two = vec[10:11, :], vec[11:12, :]
    attended = o_ref[0]
    mixed = x_ref[:, 0].reshape(WIN, D).astype(F32) + (dot_nn(attended, w_out[...]) + bias_out)
    n_one, inv_one = norm_stats(mixed)
    normed = n_one * gain_one + shift_one
    normed_low = normed.astype(BF16)
    for c in range(FF // D):
        cols = slice(D * c, D * (c + 1))
        u = dot_nn(normed_low, w_up[:, cols]) + vec[3 + c : 4 + c, :]
        phi, expo = normal_parts(u)
        z_ref[:, cols] = (u * phi).astype(BF16)
        gp_ref[:, cols] = phi + (u * expo) * DENSITY
    summed = normed + (dot_nn(z_ref[...], w_down[...]) + bias_down)
    n_two, inv_two = norm_stats(summed)
    result = (n_two * gain_two + shift_two).astype(BF16)
    out_ref[:, 0] = result.reshape(out_ref.shape[0], out_ref.shape[2], D)

    places = lax.broadcasted_iota(jnp.int32, (WIN, 1), 0)
    valid = jnp.where(places < length, 1.0 / tokens, 0.0).astype(F32)
    seed = cot_ref[:, 0].reshape(WIN, D).astype(F32) * valid
    add_row(10, seed * n_two)
    add_row(11, seed)
    d_summed = norm_back(seed * gain_two, n_two, inv_two)
    d_ff = d_summed.astype(BF16)
    add_row(7, d_ff)
    for c in range(FF // D):
        cols = slice(D * c, D * (c + 1))
        d_z = dot_nt(d_ff, w_down[cols, :])
        d_u = (d_z * gp_ref[:, cols]).astype(BF16)
        add_row(3 + c, d_u)
        du_ref[:, cols] = d_u
    d_ff_t = jnp.transpose(d_ff)
    normed_t = jnp.transpose(normed_low)
    for c in range(FF // D):
        cols = slice(D * c, D * (c + 1))
        acc_down[:, cols] += dot_nn(d_ff_t, z_ref[:, cols])
        acc_up[:, cols] += dot_nn(normed_t, du_ref[:, cols])
    d_normed = d_summed + dot_nt(du_ref[...], w_up[...])
    add_row(8, d_normed * n_one)
    add_row(9, d_normed)
    d_mixed = norm_back(d_normed * gain_one, n_one, inv_one)
    da_ref[0] = d_mixed
    d_branch = d_mixed.astype(BF16)
    add_row(2, d_branch)
    acc_out[...] += dot_nn(jnp.transpose(attended), d_branch)
    do_ref[0] = dot_nt(d_branch, w_out[...]).astype(BF16)

    @pl.when(step == pl.num_programs(0) - 1)
    def _():
        for j in range(D // BLK):
            for i in range(FF_CHUNKS):
                at = (slice(BLK * j, BLK * (j + 1)), slice(BLK * i, BLK * (i + 1)))
                acc_down[at] = jnp.transpose(acc_down[at])
        write_gradient(
            lambda b, offset, rows: acc_block(b, offset, rows)[...],
            REST_BLOCKS, part, meta[wins], dw_refs,
        )


def whole_spec(shape):
    zeros = (0,) * len(shape)
    return pl.BlockSpec(shape, lambda w, m: zeros, pipeline_mode=pl.Buffered(1))


def blocks_spec(part, count, at):
    lead = part.ndim - 3
    shape = part.shape[:lead] + (count,) + part.shape[lead + 1 :]
    return pl.BlockSpec(
        shape, lambda w, m: (0,) * lead + (at, 0, 0), pipeline_mode=pl.Buffered(1)
    )


def total_spec(shape):
    zeros = (0,) * len(shape)
    return pl.BlockSpec(shape, lambda w, m: zeros)


def window_spec(begin, *shape):
    zeros = (0,) * len(shape)
    return pl.BlockSpec((1,) + shape, lambda w, m: (begin + w,) + zeros)


def segment_spec(dp, seg):
    return pl.BlockSpec((dp, 1, seg, D), lambda w, m: (0, w, 0, 0))


def input_spec(dp, seg, begin):
    return pl.BlockSpec((dp, 1, seg, D), lambda w, m: (0, begin + w, 0, 0))


def gradient_outs(blocks, part):
    if part % 16:
        return [jax.ShapeDtypeStruct((blocks, BLK, BLK), BF16)]
    return [jax.ShapeDtypeStruct((blocks, BLK // 2, BLK), BF16)] * 2


def run_kernel(kernel, wins, meta, ins, outs, scratch, flops, moved):
    return pl.pallas_call(
        kernel,
        grid_spec=pltpu.PrefetchScalarGridSpec(
            num_scalar_prefetch=1,
            grid=(wins,),
            in_specs=[spec for _, spec in ins],
            out_specs=[spec for _, spec in outs],
            scratch_shapes=scratch,
        ),
        out_shape=[shape for shape, _ in outs],
        compiler_params=pltpu.CompilerParams(
            dimension_semantics=("arbitrary",), vmem_limit_bytes=56 * 1024 * 1024
        ),
        cost_estimate=pl.CostEstimate(
            flops=flops, bytes_accessed=moved, transcendentals=wins * WIN * FF
        ),
    )(meta, *[values for values, _ in ins])


def call_attention(meta, x, packing, weight_parts, bias):
    dp, wins, seg, _ = x.shape
    shape = jax.ShapeDtypeStruct
    return run_kernel(
        functools.partial(attention_kernel, packing, wins),
        wins,
        meta,
        [(x, input_spec(dp, seg, 0)), (bias, whole_spec(bias.shape))]
        + [(piece, whole_spec(piece.shape)) for piece in weight_parts],
        [
            (shape((wins, WIN, 3 * D), BF16), window_spec(0, WIN, 3 * D)),
            (shape((wins, WIN, D), BF16), window_spec(0, WIN, D)),
            (shape((wins, HEADS, WIN), F32), window_spec(0, HEADS, WIN)),
        ],
        [pltpu.VMEM((D, 3 * D), BF16), pltpu.VMEM((WIN, WIN), F32)],
        wins * 3_000_000_000,
        wins * 1_000_000,
    )


def call_ffn(begin, tokens, part, meta, cot, x, attended, packing, weight_parts, vec):
    dp, wins, seg, _ = cot.shape
    shape = jax.ShapeDtypeStruct
    counts = (QKV_BLOCKS, QKV_BLOCKS, 2 * QKV_BLOCKS, 2 * QKV_BLOCKS)
    ins = [
        (cot, segment_spec(dp, seg)),
        (x, input_spec(dp, seg, begin)),
        (attended, window_spec(begin, WIN, D)),
        (vec, whole_spec(vec.shape)),
    ] + [
        (piece, blocks_spec(piece, count, 0) if packing else whole_spec(piece.shape))
        for piece, count in zip(weight_parts, counts)
    ]
    return run_kernel(
        functools.partial(ffn_kernel, packing, wins, tokens, part, part % 16 == 0),
        wins,
        meta,
        ins,
        [
            (shape((dp, wins, seg, D), BF16), segment_spec(dp, seg)),
            (shape((wins, WIN, D), F32), window_spec(0, WIN, D)),
            (shape((wins, WIN, D), BF16), window_spec(0, WIN, D)),
        ]
        + [(out, total_spec(out.shape)) for out in gradient_outs(REST_BLOCKS, part)]
        + [(shape((ROWS_VEC, D), F32), total_spec((ROWS_VEC, D)))],
        [
            pltpu.VMEM((D, D), BF16),
            pltpu.VMEM((D, FF), BF16),
            pltpu.VMEM((FF, D), BF16),
            pltpu.VMEM((D, D), F32),
            pltpu.VMEM((D, FF), F32),
            pltpu.VMEM((D, FF), F32),
            pltpu.VMEM((WIN, FF), BF16),
            pltpu.VMEM((WIN, FF), F32),
            pltpu.VMEM((WIN, FF), BF16),
        ],
        wins * 18_000_000_000,
        wins * 12_000_000,
    )


def call_attention_back(
    begin, part, meta, packing, weight_parts, x, qkv, d_o, lse, d_mixed
):
    dp, _, seg, _ = x.shape
    wins = d_o.shape[0]
    shape = jax.ShapeDtypeStruct
    return run_kernel(
        functools.partial(attention_back_kernel, packing, wins, part, part % 16 == 0),
        wins,
        meta,
        [
            (x, input_spec(dp, seg, begin)),
            (qkv, window_spec(begin, WIN, 3 * D)),
            (d_o, window_spec(0, WIN, D)),
            (lse, window_spec(begin, HEADS, WIN)),
            (d_mixed, window_spec(0, WIN, D)),
        ]
        + [(piece, whole_spec(piece.shape)) for piece in weight_parts],
        [(shape((dp, wins, seg, D), BF16), segment_spec(dp, seg))]
        + [(out, total_spec(out.shape)) for out in gradient_outs(QKV_BLOCKS, part)]
        + [(shape((8, D), F32), total_spec((8, D)))],
        [
            pltpu.VMEM((D, 3 * D), BF16),
            pltpu.VMEM((WIN, WIN), F32),
            pltpu.VMEM((WIN, 3 * D), BF16),
            pltpu.VMEM((D, 3 * D), F32),
        ],
        wins * 12_500_000_000,
        wins * 8_000_000,
    )


def split_first_kernel(terms, bits, *refs):
    ins, outs = refs[:terms], refs[terms:]

    def total(side, at):
        return sum(ref[side, :, at].astype(F32) for ref in ins).astype(BF16)

    for y in range(2):
        for which in range(2):
            outs[which][:, y] = total(0, 2 * y + (bits[0] if which == 0 else 1 - bits[0]))
    for x in range(2):
        for which in range(2):
            outs[2 + which][:, x] = total(1, 2 * (bits[1] if which == 0 else 1 - bits[1]) + x)


def split_second_kernel(bits, *refs):
    for side in range(2):
        mine, got = refs[2 * side : 2 * side + 2]
        for which in range(2):
            bit = bits[1 - side]
            at = bit if which == 0 else 1 - bit
            refs[4 + 2 * side + which][...] = (
                mine[:, at].astype(F32) + got[:, at].astype(F32)
            ).astype(BF16)


def slabs_kernel(dp, me_ref, *refs):
    pairs, vec, outs, total = refs[: len(refs) - dp - 2], refs[-dp - 2], refs[-dp - 1 : -1], refs[-1]
    base = 0
    for n in range(0, len(pairs), 2):
        blocks = pairs[n].shape[0]
        total[base : base + blocks] = pairs[n][...].astype(F32) + pairs[n + 1][...].astype(F32)
        base += blocks
    owned = outs[0].shape[0] - 1
    for s in range(dp):
        slab = total[pl.ds((me_ref[0] ^ s) * owned, owned)]
        outs[s][:owned] = slab.astype(outs[s].dtype)
        outs[s][owned] = vec[...].astype(BF16).astype(outs[s].dtype)


def update_kernel(packing, scalars, *refs):
    count = 2 * len(packing)
    parts, root_parts, refs = refs[:count], refs[count : 2 * count], refs[2 * count :]
    own, left_stats, right_stats, left_roots, weights = refs[:5]
    left_new, right_new, weights_new, full, roots = refs[5:]
    fill_stack(full, packing, parts, scalars[0])
    fill_stack(roots, packing, root_parts, scalars[0])
    blocks, rows, _ = own.shape
    at = scalars[1] * rows
    lane = lax.broadcasted_iota(jnp.int32, (rows, BLK), 1)
    line = lax.broadcasted_iota(jnp.int32, (rows, BLK), 0)
    pick = jnp.where(lane == line + at, 1.0, 0.0).astype(BF16)
    for b in range(blocks):
        whole = full[b]
        crossed = dot_nt(jnp.concatenate([own[b], pick], axis=0), whole)
        left_new[b] = DECAY * left_stats[b] + (1.0 - DECAY) * crossed[:rows]
        turned = jnp.concatenate([left_roots[b].astype(BF16), crossed[rows:].astype(BF16)], axis=0)
        passed = dot_nn(turned, whole)
        right_new[b] = DECAY * right_stats[b] + (1.0 - DECAY) * passed[rows:]
        step = dot_nn(passed[:rows].astype(BF16), roots[b])
        weights_new[b] = weights[b] - MATRIX_RATE * step


def call_small(kernel, steps, scalars, ins, outs, scratch=()):
    def spec(shape, axis):
        if isinstance(axis, pl.BlockSpec):
            return axis
        block = tuple(n // steps if d == axis else n for d, n in enumerate(shape))
        return pl.BlockSpec(block, lambda g, m: tuple(g if d == axis else 0 for d in range(len(shape))))

    return pl.pallas_call(
        kernel,
        grid_spec=pltpu.PrefetchScalarGridSpec(
            num_scalar_prefetch=1,
            grid=(steps,),
            in_specs=[spec(values.shape, axis) for values, axis in ins],
            out_specs=[spec(shape.shape, axis) for shape, axis in outs],
            scratch_shapes=list(scratch),
        ),
        out_shape=[shape for shape, _ in outs],
        compiler_params=pltpu.CompilerParams(
            dimension_semantics=("arbitrary",), vmem_limit_bytes=32 * 1024 * 1024
        ),
    )(scalars, *[values for values, _ in ins])


def update_blocks(scalars, packing, parts, root_parts, own, *shards):
    blocks = own.shape[0]
    out = jax.ShapeDtypeStruct(own.shape, F32)
    share = blocks // 2
    ats = (QKV_BLOCKS // share, QKV_BLOCKS // share, 2 * QKV_BLOCKS // share, 2 * QKV_BLOCKS // share)
    return call_small(
        functools.partial(update_kernel, packing),
        1,
        scalars,
        [(part, None) for part in parts]
        + [(part, blocks_spec(part, share, at)) for part, at in zip(root_parts, ats)]
        + [(values, None) for values in (own, *shards)],
        [(out, None)] * 3,
        [pltpu.VMEM((blocks, BLK, BLK), BF16)] * 2,
    )


def split_first(bits, *terms):
    blocks, height, cols = terms[0].shape
    half = blocks // 2
    view = (2, half, 4, height // 4, cols)
    out = jax.ShapeDtypeStruct((half, 2, height // 4, cols), BF16)
    return call_small(
        functools.partial(split_first_kernel, len(terms)),
        max(half // 6, 1),
        bits,
        [(term.reshape(view), 1) for term in terms],
        [(out, 0)] * 4,
    )


def split_second(bits, *parts):
    half, _, rows, cols = parts[0].shape
    out = jax.ShapeDtypeStruct((half, rows, cols), BF16)
    return call_small(
        split_second_kernel, 1, bits, [(part, 0) for part in parts], [(out, 0)] * 4
    )


def make_slabs(dp, me, parts, vec):
    _, rows, cols = parts[0].shape
    blocks = sum(part.shape[0] for part in parts) // 2
    shape = (blocks // dp + 1, rows, cols)
    return call_small(
        functools.partial(slabs_kernel, dp),
        1,
        me,
        [(part, None) for part in [*parts, vec]],
        [(jax.ShapeDtypeStruct(shape, F32 if s == 0 else BF16), None) for s in range(dp)],
        [pltpu.VMEM((blocks, rows, cols), F32)],
    )


def swap(values, axis, size, k):
    return lax.ppermute(values, axis, [(i, i ^ k) for i in range(size)])


def bits_of(size):
    return [1 << i for i in range(size.bit_length() - 1)]


def hop_orders(seq_count):
    high = [k for k in bits_of(seq_count) if k > 1]
    return (high, high[::-1])


def gather_hop(state, k, seq_count, seq_index, *marks):
    cur, lead = state
    got = after(swap(cur, "seq", seq_count, k), *marks)
    odd = (seq_index & k) != 0
    cur = jnp.stack([jnp.where(odd, got, cur), jnp.where(odd, cur, got)], axis=0)
    return cur, [k] + lead


def gather_end(state):
    cur, lead = state
    count = len(lead)
    blocks, rows, cols = cur.shape[count:]
    axes = [count] + [lead.index(k) for k in sorted(lead, reverse=True)] + [count + 1, count + 2]
    return cur.transpose(axes).reshape(blocks, rows << count, cols)


def halves(cur):
    half = cur.shape[0] // 2
    return [cur[:half], cur[half:]]


def gather_split(cur, seq_count, seq_index):
    done = []
    for part, order in zip(halves(cur), hop_orders(seq_count)):
        state = (part, [])
        for k in order + [1]:
            state = gather_hop(state, k, seq_count, seq_index)
        done.append(gather_end(state))
    return jnp.concatenate(done, axis=0)


def pack_weights(rows, roots, orders, seq_count, seq_index):
    states = [
        (jnp.concatenate(pair, axis=0), []) for pair in zip(halves(rows), halves(roots))
    ]
    for step in range(len(orders[0])):
        states = [
            gather_hop(state, order[step], seq_count, seq_index)
            for state, order in zip(states, orders)
        ]
        if step == 0:
            cur, lead = states[0]
            axis = len(lead)
            states = [
                (lax.slice_in_dim(cur, 0, QKV_BLOCKS, axis=axis), lead),
                (lax.slice_in_dim(cur, QKV_BLOCKS, cur.shape[axis], axis=axis), lead),
                states[1],
            ]
            orders = (orders[0], orders[0], orders[1])
    return states


def join_cores(states, seq_count, seq_index, *marks):
    if states[0][0].shape[-2] % 16:
        states = [gather_hop(state, 1, seq_count, seq_index) for state in states]
        return (), [jnp.concatenate([gather_end(state) for state in states], axis=0)]
    parts = []
    for cur, _ in states:
        parts += [cur, after(swap(cur, "seq", seq_count, 1), *marks)]
    return tuple(tuple(lead) for _, lead in states), parts


def scatter_first(whole, seq_count, seq_index):
    left = sorted(bits_of(seq_count), reverse=True)
    blocks, height, cols = whole.shape
    rows = height // seq_count
    cur = whole.reshape(blocks, seq_count // 2, 2, rows, cols)
    mine, other = [
        lax.dynamic_index_in_dim(cur, bit, 2, keepdims=False)
        for bit in (seq_index % 2, 1 - seq_index % 2)
    ]
    cur = mine.astype(F32) + swap(other, "seq", seq_count, 1).astype(F32)
    left.remove(1)
    cur = cur.astype(BF16).reshape([blocks] + [2] * len(left) + [rows, cols])
    return [(half, left) for half in halves(cur)]


def scatter_hop(state, k, seq_count, seq_index, *marks):
    cur, left = state
    axis = 1 + left.index(k)
    bit = (seq_index // k) % 2
    mine = lax.dynamic_index_in_dim(cur, bit, axis, keepdims=False)
    other = lax.dynamic_index_in_dim(cur, 1 - bit, axis, keepdims=False)
    got = after(swap(other, "seq", seq_count, k), *marks)
    cur = (mine.astype(F32) + got.astype(F32)).astype(BF16)
    return cur, [b for b in left if b != k]


def after(values, *marks):
    if not marks:
        return values
    return lax.optimization_barrier((values, marks))[0]


def body(
    inputs,
    cotangent,
    lengths,
    weights,
    vectors,
    positions,
    left_stats,
    right_stats,
    left_roots,
    right_roots,
    vector_second,
    position_second,
):
    seq_count = lax.axis_size("seq")
    dp_count = lax.axis_size("dp")
    seq_index = lax.axis_index("seq")
    dp_index = lax.axis_index("dp")
    micro, wins_dev, segment, model_width = inputs.shape
    wins = wins_dev // dp_count
    total_tokens = micro * wins_dev * seq_count * segment * dp_count
    owned, row_part, _ = weights.shape
    def exchange(rows):
        return lax.all_to_all(rows, "dp", 0, 0, tiled=True)

    grouped = (dp_count, wins, segment, model_width)
    own = weights.astype(BF16)
    orders = hop_orders(seq_count)
    hops = len(orders[0])

    def scatter_both(states, step, *marks):
        return [
            scatter_hop(state, order[step], seq_count, seq_index, *marks)
            for state, order in zip(states, orders)
        ]

    vec = vectors.reshape(-1, D)
    bias_qv = jnp.concatenate([vec[0:2], jnp.zeros((6, D), F32)], axis=0)
    vec_pad = jnp.concatenate([vec, jnp.zeros((ROWS_VEC - vec.shape[0], D), F32)], axis=0)

    metas = [
        lax.dynamic_index_in_dim(
            lengths[i].reshape(dp_count, wins), dp_index, 0, keepdims=False
        )
        for i in range(micro)
    ]
    metas = [jnp.concatenate([lens, (seq_index % 2)[None]]) for lens in metas]
    shards = [own] + [swap(own, "dp", dp_count, s) for s in range(1, dp_count)]
    weight_rows = jnp.concatenate(
        [lax.select_n(dp_index ^ j, *shards) for j in range(dp_count)], axis=0
    )
    hidden = (inputs.astype(F32) + positions[None, None]).astype(BF16)
    hidden = jnp.swapaxes(hidden.reshape((micro,) + grouped), 0, 1).reshape(
        dp_count, micro * wins, segment, model_width
    )
    x = exchange(after(hidden, *shards[1:]))
    roots_low = right_roots.astype(BF16)
    groups = pack_weights(weight_rows, roots_low, orders, seq_count, seq_index)
    cur, lead = groups[0]
    groups[0] = (after(cur, vec_pad, bias_qv, roots_low, *metas), lead)
    packing_qkv, parts_qkv = join_cores(groups[:1], seq_count, seq_index)
    cots = []
    for i in range(micro):
        cots.append(exchange(after(cotangent[i].reshape(grouped), cots[-1] if i else x)))

    ffn, out_got, dx_got = [], [], []
    qkv, attended, lse = call_attention(
        jnp.concatenate([lens[:-1] for lens in metas] + [metas[0][-1:]]), x, packing_qkv,
        parts_qkv, bias_qv,
    )
    mark = (lse,)
    packing_rest, parts_rest = join_cores(groups[1:], seq_count, seq_index, lse)
    share = owned // 2
    if not packing_rest:
        (stack,) = parts_rest
        middle = QKV_BLOCKS + share
        roots_full = jnp.concatenate([stack[QKV_BLOCKS:middle], stack[-share:]], axis=0)
        parts_rest = [jnp.concatenate([stack[:QKV_BLOCKS], stack[middle:-share]], axis=0)]
    fast = seq_count == 8 and row_part % 16 == 0
    bits = jnp.stack([(seq_index // 2) % 2, (seq_index // 4) % 2]).astype(jnp.int32)

    def over_cores(parts, *marks):
        keep, send = parts
        return [keep, after(swap(send, "seq", seq_count, 1), *marks)]

    def hop(parts, count, *marks):
        mine_a, send_a, mine_b, send_b = parts
        k_a, k_b = (2, 4) if count == 0 else (4, 2)
        got_a = after(swap(send_a, "seq", seq_count, k_a), *marks)
        got_b = after(swap(send_b, "seq", seq_count, k_b), *marks)
        return [mine_a, got_a, mine_b, got_b]

    vec_sums = jnp.zeros((ROWS_VEC, D), F32)
    dw_rest, dw_qkv = [], []
    for i in range(micro):
        out, d_mixed, d_o, *dw, vg = call_ffn(
            i * wins, total_tokens, row_part, after(metas[i], *mark), cots[i], x, attended,
            packing_rest, parts_rest, vec_pad,
        )
        out_got.append(exchange(out))
        ffn.append((d_mixed, d_o))
        vec_sums = vec_sums + vg
        mark = (vg,)
        dw_rest.append(dw)
    gates = mark + (out_got[0],)
    rest_core, qkv_core = [], []
    for i in range(micro):
        dx, *dw, db = call_attention_back(
            i * wins, row_part, after(metas[i], gates), packing_qkv, parts_qkv, x, qkv, ffn[i][1], lse,
            ffn[i][0],
        )
        vec_sums = vec_sums + jnp.concatenate([db, jnp.zeros_like(db)], axis=0)
        dw_qkv.append(dw)
        gates = (db,) + tuple(out_got[1:])
        if fast and i == 0:
            for n in range(micro):
                rest_core += over_cores(dw_rest[n], *(mark[:1] if n == 0 else (db,)))
            rest = split_first(bits, *rest_core)
            gates = gates + tuple(rest)
        if fast and i == micro - 1:
            rest = hop(rest, 0, db)
            qkv_core += over_cores(dw_qkv[0], db)
            dx = after(dx, *rest)
        dx_got.append(exchange(after(dx, *dx_got[-1:])))

    whole = (wins_dev, segment, model_width)
    layer_out = jnp.stack([got.reshape(whole) for got in out_got], axis=0)

    for k in bits_of(seq_count):
        vec_sums = vec_sums + swap(vec_sums, "seq", seq_count, k)
    if fast:
        qkv_core += over_cores(dw_qkv[1])
        states = split_first(bits, *qkv_core)
        rest = hop(split_second(bits, *rest), 1)
        states = hop(split_second(bits, *hop(states, 0)), 1)
        slabs = make_slabs(
            dp_count, after(dp_index[None].astype(jnp.int32), dx_got[-1], layer_out), states + rest,
            vec_sums.reshape(row_part, BLK),
        )
    else:
        states = []
        for parts in (dw_qkv, dw_rest):
            total = sum(part[0].astype(F32) for part in parts).astype(BF16)
            group = scatter_first(total, seq_count, seq_index)
            for step in range(hops):
                group = scatter_both(group, step)
            states += group
        joined = jnp.concatenate([cur for cur, _ in states], axis=0)
        joined = joined.reshape((dp_count, owned) + joined.shape[1:])
        vec_rows = vec_sums.astype(BF16).reshape(-1, row_part, BLK)
        slabs = [
            jnp.concatenate(
                [lax.dynamic_index_in_dim(joined, dp_index ^ s, 0, keepdims=False), vec_rows]
            )
            for s in range(dp_count)
        ]
    slabs = [slabs[0].astype(F32)] + [
        swap(slabs[s], "dp", dp_count, s).astype(F32) for s in range(1, dp_count)
    ]
    grad_rows = sum(slab[:owned] for slab in slabs)
    vec_sums = sum(lax.select_n(dp_index ^ j, *[slab[owned:] for slab in slabs]) for j in range(dp_count))
    vec_sums = vec_sums.reshape(ROWS_VEC, D)
    grad_low = grad_rows.astype(BF16)
    if fast:
        states = [(part, []) for part in halves(grad_low)]
        for step in range(hops):
            states = [
                gather_hop(state, order[step], seq_count, seq_index)
                for state, order in zip(states, orders)
            ]
        packing, parts = join_cores(states, seq_count, seq_index)
        left_new, right_new, weights_new = update_blocks(
            jnp.stack([seq_index % 2, seq_index]).astype(jnp.int32), packing, parts, parts_rest,
            grad_low, left_stats, right_stats, left_roots, weights,
        )
    else:
        grad_full = gather_split(grad_low, seq_count, seq_index)
        row_start = seq_index * row_part

        def batched(spec, left, right):
            return jnp.einsum(spec, left, right, preferred_element_type=F32)

        left_new = DECAY * left_stats + (1.0 - DECAY) * batched("bij,bkj->bik", grad_low, grad_full)
        column_part = lax.dynamic_slice_in_dim(grad_full, row_start, row_part, 2)
        right_new = DECAY * right_stats + (1.0 - DECAY) * batched(
            "bki,bkj->bij", column_part, grad_full
        )
        left_applied = batched("bij,bjk->bik", left_roots.astype(BF16), grad_full)
        step_rows = batched("bij,bjk->bik", left_applied.astype(BF16), roots_full)
        weights_new = weights - MATRIX_RATE * step_rows

    place_sum = sum(jnp.sum(got.astype(F32), axis=(0, 1)) for got in dx_got)
    for k in bits_of(seq_count):
        low = place_sum.astype(BF16)
        place_sum = low.astype(F32) + swap(low, "seq", seq_count, k).astype(F32)
    vector_grads = vec_sums[: vec.shape[0]].reshape(-1)
    vector_second_new = DECAY * vector_second + (1.0 - DECAY) * vector_grads * vector_grads
    vectors_new = vectors - VECTOR_RATE * vector_grads / (jnp.sqrt(vector_second_new) + ROOT_EPS)
    position_grads = place_sum
    position_second_new = DECAY * position_second + (1.0 - DECAY) * position_grads * position_grads
    positions_new = positions - VECTOR_RATE * position_grads / (
        jnp.sqrt(position_second_new) + ROOT_EPS
    )
    return (
        layer_out,
        jnp.stack([got.astype(F32).reshape(whole) for got in dx_got], axis=0),
        grad_rows,
        left_new,
        right_new,
        weights_new,
        vector_grads,
        vector_second_new,
        vectors_new,
        position_grads,
        position_second_new,
        positions_new,
    )


def solution(mesh):
    rows = P(None, "seq", "dp", None)
    blocks = P("dp", "seq", None)
    in_specs = (
        rows, rows, P(None, "seq"), blocks, P(), P("dp", None),
        blocks, blocks, blocks, blocks, P(), P("dp", None),
    )
    out_specs = (
        rows, rows, blocks, blocks, blocks, blocks,
        P(), P(), P(), P("dp", None), P("dp", None), P("dp", None),
    )
    return jax.shard_map(body, mesh=mesh, in_specs=in_specs, out_specs=out_specs, check_vma=False)
```

```python
import functools
import itertools

import jax
import jax.numpy as jnp
from jax import lax
from jax.experimental import pallas as pl
from jax.experimental.pallas import tpu as pltpu
from jax.sharding import PartitionSpec as P

HEADS = 8
FF = 2048
WIN = 512
D = 512
BLK = 256
QKV_BLOCKS = 12
REST_BLOCKS = 36
HEAD_DIM = D // HEADS
PAIR = 2 * HEAD_DIM
PAIRS = HEADS // 2
FF_CHUNKS = FF // BLK
ROWS_VEC = 16
GROUP = 2

NORM_EPS = 1e-05
ROOT_EPS = 1e-08
DECAY = 0.5
MATRIX_RATE = 0.5
VECTOR_RATE = 0.2
MASKED = -1e30
SCALE = HEAD_DIM ** (-0.5)
ROOT_HALF = 0.7071067811865476
DENSITY = 0.3989422804014327

F32 = jnp.float32
BF16 = jnp.bfloat16


def dot_nn(left, right):
    return lax.dot_general(left, right, (((1,), (0,)), ((), ())), preferred_element_type=F32)


def dot_nt(left, right):
    return lax.dot_general(left, right, (((1,), (1,)), ((), ())), preferred_element_type=F32)


def each_piece(packing, refs, core):
    if not packing:
        yield 0, 0, refs[0]
        return
    base = 0
    for side, bits in enumerate(packing):
        for which in range(2):
            ref = refs[2 * side + which]
            blocks, rows = ref.shape[len(bits)], ref.shape[len(bits) + 1]
            last = core if which == 0 else 1 - core
            for at in itertools.product(range(2), repeat=len(bits)):
                first = sum(k * v for k, v in zip(bits, at))
                yield base, pl.multiple_of((first + last) * rows, rows), ref.at[at]
        base += blocks


def fill_qkv_matrix(full, packing, refs, core):
    side = D // BLK
    for base, offset, ref in each_piece(packing, refs, core):
        blocks, rows = ref.shape[:2]
        for n in range(blocks):
            b = base + n
            m, i, j = b // (side * side), (b // side) % side, b % side
            cols = slice(D * m + BLK * j, D * m + BLK * (j + 1))
            full[pl.ds(BLK * i + offset, rows), cols] = ref[n]


def fill_stack(stack, packing, refs, core):
    for base, offset, ref in each_piece(packing, refs, core):
        blocks, rows = ref.shape[:2]
        for n in range(blocks):
            stack[base + n, pl.ds(offset, rows), :] = ref[n]


def write_gradient(block_at, blocks, rows, core, outs):
    for b in range(blocks):
        if len(outs) == 1:
            outs[0][b] = block_at(b, 0, BLK).astype(BF16)
            continue
        for which, out in enumerate(outs):
            last = core if which == 0 else 1 - core
            for n in range(BLK // (2 * rows)):
                offset = pl.multiple_of((2 * n + last) * rows, rows)
                out[b, n * rows : (n + 1) * rows, :] = block_at(b, offset, rows).astype(BF16)


def fill_mask(mask, length):
    for i in range(WIN // BLK):
        keys = lax.broadcasted_iota(jnp.int32, (BLK, WIN), 0) + BLK * i
        queries = lax.broadcasted_iota(jnp.int32, (BLK, WIN), 1)
        keep = (keys <= queries) & (keys < length)
        mask[BLK * i : BLK * (i + 1), :] = jnp.where(keep, 0.0, MASKED).astype(F32)


def half_marks():
    lane = lax.broadcasted_iota(jnp.int32, (1, PAIR), 1)
    low = jnp.where(lane < HEAD_DIM, 1.0, 0.0)
    return (low.astype(BF16), (1.0 - low).astype(BF16))


def attention_kernel(packing, wins, meta, x_ref, bias, *refs):
    weight_refs = refs[: 2 * len(packing) or 1]
    qkv_ref, o_ref, lse_ref, full, mask = refs[len(weight_refs) :]
    step = pl.program_id(0)

    @pl.when(step == 0)
    def _():
        fill_qkv_matrix(full, packing, weight_refs, meta[wins])

    hidden = x_ref[:, 0].reshape(WIN, D)
    for m in range(3):
        cols = slice(D * m, D * (m + 1))
        rows = dot_nn(hidden, full[:, cols])
        if m != 1:
            rows = rows + bias[(m // 2) : (m // 2) + 1, :]
        qkv_ref[0, :, cols] = rows.astype(BF16)
    fill_mask(mask, meta[step])
    marks = half_marks()
    half = WIN // BLK
    for group in range(0, PAIRS, GROUP):
        cases, scores, probs = [], [], []
        for p in range(group, group + GROUP):
            at = PAIR * p
            q8 = qkv_ref[0, :, at : at + PAIR] * jnp.asarray(SCALE, BF16)
            key = qkv_ref[0, :, D + at : D + at + PAIR]
            for h in range(2):
                key_h = key * marks[h]
                for qb in range(half):
                    cols, span = slice(BLK * qb, BLK * (qb + 1)), BLK * (qb + 1)
                    cases.append((2 * p + h, qb))
                    scores.append(dot_nt(key_h[:span], q8[cols]) + mask[:span, cols])
        for (row, qb), s_t in zip(cases, scores):
            cols = slice(BLK * qb, BLK * (qb + 1))
            top = jnp.max(s_t, axis=0, keepdims=True)
            expo = jnp.exp(s_t - top)
            total = jnp.sum(expo, axis=0, keepdims=True)
            probs.append((expo * (1.0 / total)).astype(BF16))
            lse_ref[0, row : row + 1, cols] = top + jnp.log(total)
        for n, p in enumerate(range(group, group + GROUP)):
            at = PAIR * p
            val_t = jnp.transpose(qkv_ref[0, :, 2 * D + at : 2 * D + at + PAIR])
            pieces = []
            for h in range(2):
                rows = slice(HEAD_DIM * h, HEAD_DIM * (h + 1))
                first = (2 * n + h) * half
                pieces.append(
                    jnp.concatenate(
                        [
                            dot_nn(val_t[rows, : BLK * (qb + 1)], probs[first + qb])
                            for qb in range(half)
                        ],
                        axis=1,
                    )
                )
            o_ref[0, :, at : at + PAIR] = jnp.transpose(
                jnp.concatenate(pieces, axis=0)
            ).astype(BF16)


def qkv_block(acc, b, offset, rows):
    side = D // BLK
    m, i, j = b // (side * side), (b // side) % side, b % side
    return acc[pl.ds(BLK * i + offset, rows), D * m + BLK * j : D * m + BLK * (j + 1)]


def attention_back_kernel(packing, wins, part, split, meta, *refs):
    x_ref, qkv_ref, do_ref, lse_ref, da_ref = refs[:5]
    weight_refs = refs[5 : 5 + (2 * len(packing) or 1)]
    refs = refs[5 + len(weight_refs) :]
    dx_ref, refs = refs[0], refs[1:]
    dw_refs, refs = refs[: 2 if split else 1], refs[2 if split else 1 :]
    db_ref, full, mask, dqkv, acc = refs
    step = pl.program_id(0)

    @pl.when(step == 0)
    def _():
        fill_qkv_matrix(full, packing, weight_refs, meta[wins])
        acc[...] = jnp.zeros_like(acc)
        db_ref[...] = jnp.zeros_like(db_ref)

    fill_mask(mask, meta[step])
    marks = half_marks()
    for p in range(PAIRS):
        at = PAIR * p
        q8 = qkv_ref[0, :, at : at + PAIR] * jnp.asarray(SCALE, BF16)
        key = qkv_ref[0, :, D + at : D + at + PAIR]
        val = qkv_ref[0, :, 2 * D + at : 2 * D + at + PAIR]
        d_o = do_ref[0, :, at : at + PAIR]
        key_t = jnp.transpose(key)
        both = [(BLK * (qb + 1), slice(BLK * qb, BLK * (qb + 1))) for qb in range(WIN // BLK)]
        scores, grads = [], []
        for h in range(2):
            key_h, val_h = key * marks[h], val * marks[h]
            scores.append([dot_nt(key_h[:span], q8[cols]) + mask[:span, cols] for span, cols in both])
            grads.append([dot_nt(val_h[:span], d_o[cols]) for span, cols in both])
        lows, d_lows = [], []
        for h in range(2):
            row = 2 * p + h
            lows.append([])
            d_lows.append([])
            for (span, cols), s_t, d_probs in zip(both, scores[h], grads[h]):
                probs = jnp.exp(s_t - lse_ref[0, row : row + 1, cols])
                delta = jnp.sum(probs * d_probs, axis=0, keepdims=True)
                d_lows[h].append((probs * (d_probs - delta)).astype(BF16))
                lows[h].append(probs.astype(BF16))
        dq_pieces, dk_pieces, dv_pieces = [], [], []
        for h in range(2):
            rows = slice(HEAD_DIM * h, HEAD_DIM * (h + 1))
            dv_sum = dot_nn(lows[h][-1], d_o[both[-1][1]])
            dk_sum = dot_nn(d_lows[h][-1], q8[both[-1][1]])
            for (span, cols), low, d_low in list(zip(both, lows[h], d_lows[h]))[:-1]:
                dv_part, dk_part = dot_nn(low, d_o[cols]), dot_nn(d_low, q8[cols])
                dv_sum = jnp.concatenate([dv_sum[:span] + dv_part, dv_sum[span:]], axis=0)
                dk_sum = jnp.concatenate([dk_sum[:span] + dk_part, dk_sum[span:]], axis=0)
            dq_pieces.append(
                jnp.concatenate(
                    [dot_nn(key_t[rows, :span], d_low) for (span, _), d_low in zip(both, d_lows[h])],
                    axis=1,
                )
            )
            dk_pieces.append(dk_sum)
            dv_pieces.append(dv_sum)
        lane = lax.broadcasted_iota(jnp.int32, (WIN, PAIR), 1) < HEAD_DIM
        dq = jnp.transpose(jnp.concatenate(dq_pieces, axis=0)) * SCALE
        dk = jnp.where(lane, dk_pieces[0], dk_pieces[1])
        dv = jnp.where(lane, dv_pieces[0], dv_pieces[1])
        dqkv[:, at : at + PAIR] = dq.astype(BF16)
        dqkv[:, D + at : D + at + PAIR] = dk.astype(BF16)
        dqkv[:, 2 * D + at : 2 * D + at + PAIR] = dv.astype(BF16)
    h_t = jnp.transpose(x_ref[:, 0].reshape(WIN, D))
    for m in range(3):
        cols = slice(D * m, D * (m + 1))
        rows = dqkv[:, cols]
        acc[:, cols] += dot_nn(h_t, rows)
        if m != 1:
            db_ref[(m // 2) : (m // 2) + 1, :] += jnp.sum(
                rows.astype(F32), axis=0, keepdims=True
            )
    total = da_ref[0]
    for m in range(3):
        cols = slice(D * m, D * (m + 1))
        total = total + dot_nt(dqkv[:, cols], full[:, cols])
    dx_ref[:, 0] = total.astype(BF16).reshape(dx_ref.shape[0], dx_ref.shape[2], D)

    @pl.when(step == pl.num_programs(0) - 1)
    def _():
        write_gradient(
            functools.partial(qkv_block, acc), QKV_BLOCKS, part, meta[wins], dw_refs
        )


def normal_parts(u):
    size = jnp.abs(u)
    t = 1.0 / (1.0 + (0.3275911 * ROOT_HALF) * size)
    expo = jnp.exp(-0.5 * (u * u))
    poly = t * (
        0.5 * 0.254829592
        + t
        * (
            -0.5 * 0.284496736
            + t * (0.5 * 1.421413741 + t * (-0.5 * 1.453152027 + t * (0.5 * 1.061405429)))
        )
    )
    tail = poly * expo
    return jnp.where(u >= 0.0, 1.0 - tail, tail), expo


def norm_stats(rows):
    mean = jnp.mean(rows, axis=1, keepdims=True)
    centered = rows - mean
    spread = jnp.mean(centered * centered, axis=1, keepdims=True)
    inverse = lax.rsqrt(spread + NORM_EPS)
    return centered * inverse, inverse


def norm_back(d_rows, normal, inverse):
    mean_d = jnp.mean(d_rows, axis=1, keepdims=True)
    mean_dn = jnp.mean(d_rows * normal, axis=1, keepdims=True)
    return inverse * (d_rows - mean_d - normal * mean_dn)


def fill_ffn_matrices(w_out, w_up, w_down, packing, refs, core):
    side = D // BLK
    for base, offset, ref in each_piece(packing, refs, core):
        blocks, rows = ref.shape[:2]
        for n in range(blocks):
            full, i, j = ffn_place(base + n, (w_out, w_up, w_down))
            full[pl.ds(BLK * i + offset, rows), BLK * j : BLK * (j + 1)] = ref[n]


def ffn_place(b, matrices):
    side = D // BLK
    if b < side * side:
        return matrices[0], b // side, b % side
    b -= side * side
    if b < side * FF_CHUNKS:
        return matrices[1], b // FF_CHUNKS, b % FF_CHUNKS
    b -= side * FF_CHUNKS
    return matrices[2], b // side, b % side


def ffn_kernel(packing, wins, tokens, part, split, pieces, meta, *refs):
    cot_ref, x_ref, o_ref, vec = refs[:4]
    weight_refs = refs[4 : 4 + (2 * len(packing) or 1)]
    refs = refs[4 + len(weight_refs) :]
    out_refs, refs = refs[:pieces], refs[pieces:]
    da_ref, do_ref = refs[:2]
    refs = refs[2:]
    dw_refs, refs = refs[: 2 if split else 1], refs[2 if split else 1 :]
    vg_ref, w_out, w_up, w_down, acc_out, acc_up, acc_down, z_ref, gp_ref, du_ref, buf = refs
    step = pl.program_id(0)
    length = meta[step]
    accs = (acc_out, acc_up, acc_down)

    def acc_block(b, offset, rows):
        full, i, j = ffn_place(b, accs)
        if full is acc_down:
            i, j = j, i
        return full.at[pl.ds(BLK * i + offset, rows), BLK * j : BLK * (j + 1)]

    @pl.when(step == 0)
    def _():
        fill_ffn_matrices(w_out, w_up, w_down, packing, weight_refs, meta[wins])
        for acc in accs:
            acc[...] = jnp.zeros_like(acc)
        vg_ref[...] = jnp.zeros_like(vg_ref)

    def add_row(row, values, at=0):
        vg_ref[row : row + 1, at : at + values.shape[1]] += jnp.sum(
            values.astype(F32), axis=0, keepdims=True
        )

    bias_out, bias_down = vec[2:3, :], vec[7:8, :]
    gain_one, shift_one = vec[8:9, :], vec[9:10, :]
    gain_two, shift_two = vec[10:11, :], vec[11:12, :]
    attended = o_ref[0]
    mixed = x_ref[:, 0].reshape(WIN, D).astype(F32) + (dot_nn(attended, w_out[...]) + bias_out)
    n_one, inv_one = norm_stats(mixed)
    normed = n_one * gain_one + shift_one
    normed_low = normed.astype(BF16)
    for c in range(FF // D):
        cols = slice(D * c, D * (c + 1))
        u = dot_nn(normed_low, w_up[:, cols]) + vec[3 + c : 4 + c, :]
        phi, expo = normal_parts(u)
        z_ref[:, cols] = (u * phi).astype(BF16)
        gp_ref[:, cols] = phi + (u * expo) * DENSITY
    summed = normed + (dot_nn(z_ref[...], w_down[...]) + bias_down)
    n_two, inv_two = norm_stats(summed)
    result = (n_two * gain_two + shift_two).astype(BF16)
    if pieces == 1:
        out_ref = out_refs[0]
        out_ref[:, 0] = result.reshape(out_ref.shape[0], out_ref.shape[2], D)
    else:
        buf[...] = result
        for s, out_ref in enumerate(out_refs):
            rows = out_ref.shape[1]
            at = pl.multiple_of((meta[wins + 1] ^ s) * rows, rows)
            out_ref[0] = buf[pl.ds(at, rows), :]

    places = lax.broadcasted_iota(jnp.int32, (WIN, 1), 0)
    valid = jnp.where(places < length, 1.0 / tokens, 0.0).astype(F32)
    seed = cot_ref[:, 0].reshape(WIN, D).astype(F32) * valid
    add_row(10, seed * n_two)
    add_row(11, seed)
    d_summed = norm_back(seed * gain_two, n_two, inv_two)
    d_ff = d_summed.astype(BF16)
    add_row(7, d_ff)
    for c in range(FF // D):
        cols = slice(D * c, D * (c + 1))
        d_z = dot_nt(d_ff, w_down[cols, :])
        d_u = (d_z * gp_ref[:, cols]).astype(BF16)
        add_row(3 + c, d_u)
        du_ref[:, cols] = d_u
    d_ff_t = jnp.transpose(d_ff)
    normed_t = jnp.transpose(normed_low)
    for c in range(FF // D):
        cols = slice(D * c, D * (c + 1))
        acc_down[:, cols] += dot_nn(d_ff_t, z_ref[:, cols])
        acc_up[:, cols] += dot_nn(normed_t, du_ref[:, cols])
    d_normed = d_summed + dot_nt(du_ref[...], w_up[...])
    add_row(8, d_normed * n_one)
    add_row(9, d_normed)
    d_mixed = norm_back(d_normed * gain_one, n_one, inv_one)
    da_ref[0] = d_mixed
    d_branch = d_mixed.astype(BF16)
    add_row(2, d_branch)
    acc_out[...] += dot_nn(jnp.transpose(attended), d_branch)
    do_ref[0] = dot_nt(d_branch, w_out[...]).astype(BF16)

    @pl.when(step == pl.num_programs(0) - 1)
    def _():
        for j in range(D // BLK):
            for i in range(FF_CHUNKS):
                at = (slice(BLK * j, BLK * (j + 1)), slice(BLK * i, BLK * (i + 1)))
                acc_down[at] = jnp.transpose(acc_down[at])
        write_gradient(
            lambda b, offset, rows: acc_block(b, offset, rows)[...],
            REST_BLOCKS, part, meta[wins], dw_refs,
        )


def whole_spec(shape):
    zeros = (0,) * len(shape)
    return pl.BlockSpec(shape, lambda w, m: zeros, pipeline_mode=pl.Buffered(1))


def blocks_spec(part, count, at):
    lead = part.ndim - 3
    shape = part.shape[:lead] + (count,) + part.shape[lead + 1 :]
    return pl.BlockSpec(
        shape, lambda w, m: (0,) * lead + (at, 0, 0), pipeline_mode=pl.Buffered(1)
    )


def total_spec(shape):
    zeros = (0,) * len(shape)
    return pl.BlockSpec(shape, lambda w, m: zeros)


def window_spec(begin, *shape):
    zeros = (0,) * len(shape)
    return pl.BlockSpec((1,) + shape, lambda w, m: (begin + w,) + zeros)


def segment_spec(dp, seg):
    return pl.BlockSpec((dp, 1, seg, D), lambda w, m: (0, w, 0, 0))


def input_spec(dp, seg, begin):
    return pl.BlockSpec((dp, 1, seg, D), lambda w, m: (0, begin + w, 0, 0))


def gradient_outs(blocks, part):
    if part % 16:
        return [jax.ShapeDtypeStruct((blocks, BLK, BLK), BF16)]
    return [jax.ShapeDtypeStruct((blocks, BLK // 2, BLK), BF16)] * 2


def run_kernel(kernel, wins, meta, ins, outs, scratch, flops, moved):
    return pl.pallas_call(
        kernel,
        grid_spec=pltpu.PrefetchScalarGridSpec(
            num_scalar_prefetch=1,
            grid=(wins,),
            in_specs=[spec for _, spec in ins],
            out_specs=[spec for _, spec in outs],
            scratch_shapes=scratch,
        ),
        out_shape=[shape for shape, _ in outs],
        compiler_params=pltpu.CompilerParams(
            dimension_semantics=("arbitrary",), vmem_limit_bytes=56 * 1024 * 1024
        ),
        cost_estimate=pl.CostEstimate(
            flops=flops, bytes_accessed=moved, transcendentals=wins * WIN * FF
        ),
    )(meta, *[values for values, _ in ins])


def call_attention(meta, x, packing, weight_parts, bias):
    dp, wins, seg, _ = x.shape
    shape = jax.ShapeDtypeStruct
    return run_kernel(
        functools.partial(attention_kernel, packing, wins),
        wins,
        meta,
        [(x, input_spec(dp, seg, 0)), (bias, whole_spec(bias.shape))]
        + [(piece, whole_spec(piece.shape)) for piece in weight_parts],
        [
            (shape((wins, WIN, 3 * D), BF16), window_spec(0, WIN, 3 * D)),
            (shape((wins, WIN, D), BF16), window_spec(0, WIN, D)),
            (shape((wins, HEADS, WIN), F32), window_spec(0, HEADS, WIN)),
        ],
        [pltpu.VMEM((D, 3 * D), BF16), pltpu.VMEM((WIN, WIN), F32)],
        wins * 3_000_000_000,
        wins * 1_000_000,
    )


def call_ffn(begin, tokens, part, apart, meta, cot, x, attended, packing, weight_parts, vec):
    dp, wins, seg, _ = cot.shape
    shape = jax.ShapeDtypeStruct
    counts = (QKV_BLOCKS, QKV_BLOCKS, 2 * QKV_BLOCKS, 2 * QKV_BLOCKS)
    ins = [
        (cot, segment_spec(dp, seg)),
        (x, input_spec(dp, seg, begin)),
        (attended, window_spec(begin, WIN, D)),
        (vec, whole_spec(vec.shape)),
    ] + [
        (piece, blocks_spec(piece, count, 0) if packing else whole_spec(piece.shape))
        for piece, count in zip(weight_parts, counts)
    ]
    outs = [(shape((dp, wins, seg, D), BF16), segment_spec(dp, seg))]
    if apart:
        outs = [(shape((wins, seg, D), BF16), window_spec(0, seg, D))] * dp
    return run_kernel(
        functools.partial(ffn_kernel, packing, wins, tokens, part, part % 16 == 0, dp if apart else 1),
        wins,
        meta,
        ins,
        [
            *outs,
            (shape((wins, WIN, D), F32), window_spec(0, WIN, D)),
            (shape((wins, WIN, D), BF16), window_spec(0, WIN, D)),
        ]
        + [(out, total_spec(out.shape)) for out in gradient_outs(REST_BLOCKS, part)]
        + [(shape((ROWS_VEC, D), F32), total_spec((ROWS_VEC, D)))],
        [
            pltpu.VMEM((D, D), BF16),
            pltpu.VMEM((D, FF), BF16),
            pltpu.VMEM((FF, D), BF16),
            pltpu.VMEM((D, D), F32),
            pltpu.VMEM((D, FF), F32),
            pltpu.VMEM((D, FF), F32),
            pltpu.VMEM((WIN, FF), BF16),
            pltpu.VMEM((WIN, FF), F32),
            pltpu.VMEM((WIN, FF), BF16),
            pltpu.VMEM((WIN, D), BF16),
        ],
        wins * 18_000_000_000,
        wins * 12_000_000,
    )


def call_attention_back(
    begin, part, meta, packing, weight_parts, x, qkv, d_o, lse, d_mixed
):
    dp, _, seg, _ = x.shape
    wins = d_o.shape[0]
    shape = jax.ShapeDtypeStruct
    return run_kernel(
        functools.partial(attention_back_kernel, packing, wins, part, part % 16 == 0),
        wins,
        meta,
        [
            (x, input_spec(dp, seg, begin)),
            (qkv, window_spec(begin, WIN, 3 * D)),
            (d_o, window_spec(0, WIN, D)),
            (lse, window_spec(begin, HEADS, WIN)),
            (d_mixed, window_spec(0, WIN, D)),
        ]
        + [(piece, whole_spec(piece.shape)) for piece in weight_parts],
        [(shape((dp, wins, seg, D), BF16), segment_spec(dp, seg))]
        + [(out, total_spec(out.shape)) for out in gradient_outs(QKV_BLOCKS, part)]
        + [(shape((8, D), F32), total_spec((8, D)))],
        [
            pltpu.VMEM((D, 3 * D), BF16),
            pltpu.VMEM((WIN, WIN), F32),
            pltpu.VMEM((WIN, 3 * D), BF16),
            pltpu.VMEM((D, 3 * D), F32),
        ],
        wins * 12_500_000_000,
        wins * 8_000_000,
    )


def split_first_kernel(terms, bits, *refs):
    ins, outs = refs[:terms], refs[terms:]

    def total(side, at):
        return sum(ref[side, :, at].astype(F32) for ref in ins).astype(BF16)

    for y in range(2):
        for which in range(2):
            outs[which][:, y] = total(0, 2 * y + (bits[0] if which == 0 else 1 - bits[0]))
    for x in range(2):
        for which in range(2):
            outs[2 + which][:, x] = total(1, 2 * (bits[1] if which == 0 else 1 - bits[1]) + x)


def split_second_kernel(bits, *refs):
    for side in range(2):
        mine, got = refs[2 * side : 2 * side + 2]
        for which in range(2):
            bit = bits[1 - side]
            at = bit if which == 0 else 1 - bit
            refs[4 + 2 * side + which][...] = (
                mine[:, at].astype(F32) + got[:, at].astype(F32)
            ).astype(BF16)


def slabs_kernel(dp, me_ref, *refs):
    pairs, vec, outs, total = refs[: len(refs) - dp - 2], refs[-dp - 2], refs[-dp - 1 : -1], refs[-1]
    base = 0
    for n in range(0, len(pairs), 2):
        blocks = pairs[n].shape[0]
        total[base : base + blocks] = pairs[n][...].astype(F32) + pairs[n + 1][...].astype(F32)
        base += blocks
    owned = outs[0].shape[0] - 1
    for s in range(dp):
        slab = total[pl.ds((me_ref[0] ^ s) * owned, owned)]
        outs[s][:owned] = slab.astype(outs[s].dtype)
        outs[s][owned] = vec[...].astype(BF16).astype(outs[s].dtype)


def update_kernel(packing, scalars, *refs):
    count = 2 * len(packing)
    parts, root_parts, refs = refs[:count], refs[count : 2 * count], refs[2 * count :]
    own, left_stats, right_stats, left_roots, weights = refs[:5]
    left_new, right_new, weights_new, full, roots = refs[5:]
    fill_stack(full, packing, parts, scalars[0])
    fill_stack(roots, packing, root_parts, scalars[0])
    blocks, rows, _ = own.shape
    at = scalars[1] * rows
    lane = lax.broadcasted_iota(jnp.int32, (rows, BLK), 1)
    line = lax.broadcasted_iota(jnp.int32, (rows, BLK), 0)
    pick = jnp.where(lane == line + at, 1.0, 0.0).astype(BF16)
    for b in range(blocks):
        whole = full[b]
        crossed = dot_nt(jnp.concatenate([own[b], pick], axis=0), whole)
        left_new[b] = DECAY * left_stats[b] + (1.0 - DECAY) * crossed[:rows]
        turned = jnp.concatenate([left_roots[b].astype(BF16), crossed[rows:].astype(BF16)], axis=0)
        passed = dot_nn(turned, whole)
        right_new[b] = DECAY * right_stats[b] + (1.0 - DECAY) * passed[rows:]
        step = dot_nn(passed[:rows].astype(BF16), roots[b])
        weights_new[b] = weights[b] - MATRIX_RATE * step


def call_small(kernel, steps, scalars, ins, outs, scratch=()):
    def spec(shape, axis):
        if isinstance(axis, pl.BlockSpec):
            return axis
        block = tuple(n // steps if d == axis else n for d, n in enumerate(shape))
        return pl.BlockSpec(block, lambda g, m: tuple(g if d == axis else 0 for d in range(len(shape))))

    return pl.pallas_call(
        kernel,
        grid_spec=pltpu.PrefetchScalarGridSpec(
            num_scalar_prefetch=1,
            grid=(steps,),
            in_specs=[spec(values.shape, axis) for values, axis in ins],
            out_specs=[spec(shape.shape, axis) for shape, axis in outs],
            scratch_shapes=list(scratch),
        ),
        out_shape=[shape for shape, _ in outs],
        compiler_params=pltpu.CompilerParams(
            dimension_semantics=("arbitrary",), vmem_limit_bytes=32 * 1024 * 1024
        ),
    )(scalars, *[values for values, _ in ins])


def update_blocks(scalars, packing, parts, root_parts, own, *shards):
    blocks = own.shape[0]
    out = jax.ShapeDtypeStruct(own.shape, F32)
    share = blocks // 2
    ats = (QKV_BLOCKS // share, QKV_BLOCKS // share, 2 * QKV_BLOCKS // share, 2 * QKV_BLOCKS // share)
    return call_small(
        functools.partial(update_kernel, packing),
        1,
        scalars,
        [(part, None) for part in parts]
        + [(part, blocks_spec(part, share, at)) for part, at in zip(root_parts, ats)]
        + [(values, None) for values in (own, *shards)],
        [(out, None)] * 3,
        [pltpu.VMEM((blocks, BLK, BLK), BF16)] * 2,
    )


def split_first(bits, *terms):
    blocks, height, cols = terms[0].shape
    half = blocks // 2
    view = (2, half, 4, height // 4, cols)
    out = jax.ShapeDtypeStruct((half, 2, height // 4, cols), BF16)
    return call_small(
        functools.partial(split_first_kernel, len(terms)),
        max(half // 6, 1),
        bits,
        [(term.reshape(view), 1) for term in terms],
        [(out, 0)] * 4,
    )


def split_second(bits, *parts):
    half, _, rows, cols = parts[0].shape
    out = jax.ShapeDtypeStruct((half, rows, cols), BF16)
    return call_small(
        split_second_kernel, 1, bits, [(part, 0) for part in parts], [(out, 0)] * 4
    )


def make_slabs(dp, me, parts, vec):
    _, rows, cols = parts[0].shape
    blocks = sum(part.shape[0] for part in parts) // 2
    shape = (blocks // dp + 1, rows, cols)
    return call_small(
        functools.partial(slabs_kernel, dp),
        1,
        me,
        [(part, None) for part in [*parts, vec]],
        [(jax.ShapeDtypeStruct(shape, F32 if s == 0 else BF16), None) for s in range(dp)],
        [pltpu.VMEM((blocks, rows, cols), F32)],
    )


def swap(values, axis, size, k):
    return lax.ppermute(values, axis, [(i, i ^ k) for i in range(size)])


def bits_of(size):
    return [1 << i for i in range(size.bit_length() - 1)]


def hop_orders(seq_count):
    high = [k for k in bits_of(seq_count) if k > 1]
    return (high, high[::-1])


def gather_hop(state, k, seq_count, seq_index, *marks):
    cur, lead = state
    got = after(swap(cur, "seq", seq_count, k), *marks)
    odd = (seq_index & k) != 0
    cur = jnp.stack([jnp.where(odd, got, cur), jnp.where(odd, cur, got)], axis=0)
    return cur, [k] + lead


def gather_end(state):
    cur, lead = state
    count = len(lead)
    blocks, rows, cols = cur.shape[count:]
    axes = [count] + [lead.index(k) for k in sorted(lead, reverse=True)] + [count + 1, count + 2]
    return cur.transpose(axes).reshape(blocks, rows << count, cols)


def halves(cur):
    half = cur.shape[0] // 2
    return [cur[:half], cur[half:]]


def gather_split(cur, seq_count, seq_index):
    done = []
    for part, order in zip(halves(cur), hop_orders(seq_count)):
        state = (part, [])
        for k in order + [1]:
            state = gather_hop(state, k, seq_count, seq_index)
        done.append(gather_end(state))
    return jnp.concatenate(done, axis=0)


def pack_weights(rows, roots, orders, seq_count, seq_index):
    states = [
        (jnp.concatenate(pair, axis=0), []) for pair in zip(halves(rows), halves(roots))
    ]
    for step in range(len(orders[0])):
        states = [
            gather_hop(state, order[step], seq_count, seq_index)
            for state, order in zip(states, orders)
        ]
        if step == 0:
            cur, lead = states[0]
            axis = len(lead)
            states = [
                (lax.slice_in_dim(cur, 0, QKV_BLOCKS, axis=axis), lead),
                (lax.slice_in_dim(cur, QKV_BLOCKS, cur.shape[axis], axis=axis), lead),
                states[1],
            ]
            orders = (orders[0], orders[0], orders[1])
    return states


def join_cores(states, seq_count, seq_index, *marks):
    if states[0][0].shape[-2] % 16:
        states = [gather_hop(state, 1, seq_count, seq_index) for state in states]
        return (), [jnp.concatenate([gather_end(state) for state in states], axis=0)]
    parts = []
    for cur, _ in states:
        parts += [cur, after(swap(cur, "seq", seq_count, 1), *marks)]
    return tuple(tuple(lead) for _, lead in states), parts


def scatter_first(whole, seq_count, seq_index):
    left = sorted(bits_of(seq_count), reverse=True)
    blocks, height, cols = whole.shape
    rows = height // seq_count
    cur = whole.reshape(blocks, seq_count // 2, 2, rows, cols)
    mine, other = [
        lax.dynamic_index_in_dim(cur, bit, 2, keepdims=False)
        for bit in (seq_index % 2, 1 - seq_index % 2)
    ]
    cur = mine.astype(F32) + swap(other, "seq", seq_count, 1).astype(F32)
    left.remove(1)
    cur = cur.astype(BF16).reshape([blocks] + [2] * len(left) + [rows, cols])
    return [(half, left) for half in halves(cur)]


def scatter_hop(state, k, seq_count, seq_index, *marks):
    cur, left = state
    axis = 1 + left.index(k)
    bit = (seq_index // k) % 2
    mine = lax.dynamic_index_in_dim(cur, bit, axis, keepdims=False)
    other = lax.dynamic_index_in_dim(cur, 1 - bit, axis, keepdims=False)
    got = after(swap(other, "seq", seq_count, k), *marks)
    cur = (mine.astype(F32) + got.astype(F32)).astype(BF16)
    return cur, [b for b in left if b != k]


def after(values, *marks):
    if not marks:
        return values
    return lax.optimization_barrier((values, marks))[0]


def body(
    inputs,
    cotangent,
    lengths,
    weights,
    vectors,
    positions,
    left_stats,
    right_stats,
    left_roots,
    right_roots,
    vector_second,
    position_second,
):
    seq_count = lax.axis_size("seq")
    dp_count = lax.axis_size("dp")
    seq_index = lax.axis_index("seq")
    dp_index = lax.axis_index("dp")
    micro, wins_dev, segment, model_width = inputs.shape
    wins = wins_dev // dp_count
    total_tokens = micro * wins_dev * seq_count * segment * dp_count
    owned, row_part, _ = weights.shape
    def exchange(rows):
        return lax.all_to_all(rows, "dp", 0, 0, tiled=True)

    grouped = (dp_count, wins, segment, model_width)
    own = weights.astype(BF16)
    orders = hop_orders(seq_count)
    hops = len(orders[0])

    def scatter_both(states, step, *marks):
        return [
            scatter_hop(state, order[step], seq_count, seq_index, *marks)
            for state, order in zip(states, orders)
        ]

    vec = vectors.reshape(-1, D)
    bias_qv = jnp.concatenate([vec[0:2], jnp.zeros((6, D), F32)], axis=0)
    vec_pad = jnp.concatenate([vec, jnp.zeros((ROWS_VEC - vec.shape[0], D), F32)], axis=0)

    metas = [
        lax.dynamic_index_in_dim(
            lengths[i].reshape(dp_count, wins), dp_index, 0, keepdims=False
        )
        for i in range(micro)
    ]
    metas = [
        jnp.concatenate([lens, (seq_index % 2)[None], dp_index[None]]).astype(jnp.int32)
        for lens in metas
    ]
    shards = [own] + [swap(own, "dp", dp_count, s) for s in range(1, dp_count)]
    weight_rows = jnp.concatenate(
        [lax.select_n(dp_index ^ j, *shards) for j in range(dp_count)], axis=0
    )
    hidden = (inputs.astype(F32) + positions[None, None]).astype(BF16)
    hidden = jnp.swapaxes(hidden.reshape((micro,) + grouped), 0, 1).reshape(
        dp_count, micro * wins, segment, model_width
    )
    x = exchange(after(hidden, *shards[1:]))
    roots_low = right_roots.astype(BF16)
    groups = pack_weights(weight_rows, roots_low, orders, seq_count, seq_index)
    cur, lead = groups[0]
    groups[0] = (after(cur, vec_pad, bias_qv, roots_low, *metas), lead)
    packing_qkv, parts_qkv = join_cores(groups[:1], seq_count, seq_index)
    meta_all = jnp.concatenate([lens[:-2] for lens in metas] + [metas[0][-2:]])
    cots = []
    for i in range(micro):
        marks = (cots[-1],) if i else (x, meta_all, *(cur for cur, _ in groups[1:]))
        cots.append(exchange(after(cotangent[i].reshape(grouped), *marks)))

    ffn, out_got, dx_got = [], [], []
    qkv, attended, lse = call_attention(meta_all, x, packing_qkv, parts_qkv, bias_qv)
    mark = (lse,)
    packing_rest, parts_rest = join_cores(groups[1:], seq_count, seq_index, lse)
    share = owned // 2
    if not packing_rest:
        (stack,) = parts_rest
        middle = QKV_BLOCKS + share
        roots_full = jnp.concatenate([stack[QKV_BLOCKS:middle], stack[-share:]], axis=0)
        parts_rest = [jnp.concatenate([stack[:QKV_BLOCKS], stack[middle:-share]], axis=0)]
    fast = seq_count == 8 and row_part % 16 == 0
    bits = jnp.stack([(seq_index // 2) % 2, (seq_index // 4) % 2]).astype(jnp.int32)

    def over_cores(parts, *marks):
        keep, send = parts
        return [keep, after(swap(send, "seq", seq_count, 1), *marks)]

    def hop(parts, count, *marks):
        mine_a, send_a, mine_b, send_b = parts
        k_a, k_b = (2, 4) if count == 0 else (4, 2)
        got_a = after(swap(send_a, "seq", seq_count, k_a), *marks)
        got_b = after(swap(send_b, "seq", seq_count, k_b), *marks)
        return [mine_a, got_a, mine_b, got_b]

    vec_sums = jnp.zeros((ROWS_VEC, D), F32)
    dw_rest, dw_qkv = [], []
    for i in range(micro):
        apart = i == micro - 1
        results = call_ffn(
            i * wins, total_tokens, row_part, apart, after(metas[i], *mark), cots[i], x, attended,
            packing_rest, parts_rest, vec_pad,
        )
        count = dp_count if apart else 1
        out, (d_mixed, d_o, *dw, vg) = results[:count], results[count:]
        if apart:
            got = [out[0]] + [swap(out[s], "dp", dp_count, s) for s in range(1, dp_count)]
            out_got.append(tuple(got))
        else:
            out_got.append(exchange(out[0]))
        ffn.append((d_mixed, d_o))
        vec_sums = vec_sums + vg
        mark = (vg,)
        dw_rest.append(dw)
    gates = mark + (out_got[0],)
    rest_core, qkv_core = [], []
    for i in range(micro):
        dx, *dw, db = call_attention_back(
            i * wins, row_part, after(metas[i], gates), packing_qkv, parts_qkv, x, qkv, ffn[i][1], lse,
            ffn[i][0],
        )
        vec_sums = vec_sums + jnp.concatenate([db, jnp.zeros_like(db)], axis=0)
        dw_qkv.append(dw)
        gates = (db,) + tuple(out_got[1:])
        if fast and i == 0:
            for n in range(micro):
                rest_core += over_cores(dw_rest[n], *(mark[:1] if n == 0 else (db,)))
            rest = split_first(bits, *rest_core)
            gates = gates + tuple(rest)
        if fast and i == micro - 1:
            rest = hop(rest, 0, db)
            qkv_core += over_cores(dw_qkv[0], db)
            dx = after(dx, *rest)
        dx_got.append(exchange(after(dx, *dx_got[-1:])))

    whole = (wins_dev, segment, model_width)
    out_got[-1] = jnp.stack([lax.select_n(dp_index ^ e, *out_got[-1]) for e in range(dp_count)])
    layer_out = jnp.stack([got.reshape(whole) for got in out_got], axis=0)

    for k in bits_of(seq_count):
        vec_sums = vec_sums + swap(vec_sums, "seq", seq_count, k)
    if fast:
        qkv_core += over_cores(dw_qkv[1])
        states = split_first(bits, *qkv_core)
        rest = hop(split_second(bits, *rest), 1)
        states = hop(split_second(bits, *hop(states, 0)), 1)
        slabs = make_slabs(
            dp_count, after(dp_index[None].astype(jnp.int32), dx_got[-1], layer_out), states + rest,
            vec_sums.reshape(row_part, BLK),
        )
    else:
        states = []
        for parts in (dw_qkv, dw_rest):
            total = sum(part[0].astype(F32) for part in parts).astype(BF16)
            group = scatter_first(total, seq_count, seq_index)
            for step in range(hops):
                group = scatter_both(group, step)
            states += group
        joined = jnp.concatenate([cur for cur, _ in states], axis=0)
        joined = joined.reshape((dp_count, owned) + joined.shape[1:])
        vec_rows = vec_sums.astype(BF16).reshape(-1, row_part, BLK)
        slabs = [
            jnp.concatenate(
                [lax.dynamic_index_in_dim(joined, dp_index ^ s, 0, keepdims=False), vec_rows]
            )
            for s in range(dp_count)
        ]
    slabs = [slabs[0].astype(F32)] + [
        swap(slabs[s], "dp", dp_count, s).astype(F32) for s in range(1, dp_count)
    ]
    grad_rows = sum(slab[:owned] for slab in slabs)
    vec_sums = sum(lax.select_n(dp_index ^ j, *[slab[owned:] for slab in slabs]) for j in range(dp_count))
    vec_sums = vec_sums.reshape(ROWS_VEC, D)
    grad_low = grad_rows.astype(BF16)
    if fast:
        states = [(part, []) for part in halves(grad_low)]
        for step in range(hops):
            states = [
                gather_hop(state, order[step], seq_count, seq_index)
                for state, order in zip(states, orders)
            ]
        packing, parts = join_cores(states, seq_count, seq_index)
        left_new, right_new, weights_new = update_blocks(
            jnp.stack([seq_index % 2, seq_index]).astype(jnp.int32), packing, parts, parts_rest,
            grad_low, left_stats, right_stats, left_roots, weights,
        )
    else:
        grad_full = gather_split(grad_low, seq_count, seq_index)
        row_start = seq_index * row_part

        def batched(spec, left, right):
            return jnp.einsum(spec, left, right, preferred_element_type=F32)

        left_new = DECAY * left_stats + (1.0 - DECAY) * batched("bij,bkj->bik", grad_low, grad_full)
        column_part = lax.dynamic_slice_in_dim(grad_full, row_start, row_part, 2)
        right_new = DECAY * right_stats + (1.0 - DECAY) * batched(
            "bki,bkj->bij", column_part, grad_full
        )
        left_applied = batched("bij,bjk->bik", left_roots.astype(BF16), grad_full)
        step_rows = batched("bij,bjk->bik", left_applied.astype(BF16), roots_full)
        weights_new = weights - MATRIX_RATE * step_rows

    place_sum = sum(jnp.sum(got.astype(F32), axis=(0, 1)) for got in dx_got)
    for k in bits_of(seq_count):
        low = place_sum.astype(BF16)
        place_sum = low.astype(F32) + swap(low, "seq", seq_count, k).astype(F32)
    vector_grads = vec_sums[: vec.shape[0]].reshape(-1)
    vector_second_new = DECAY * vector_second + (1.0 - DECAY) * vector_grads * vector_grads
    vectors_new = vectors - VECTOR_RATE * vector_grads / (jnp.sqrt(vector_second_new) + ROOT_EPS)
    position_grads = place_sum
    position_second_new = DECAY * position_second + (1.0 - DECAY) * position_grads * position_grads
    positions_new = positions - VECTOR_RATE * position_grads / (
        jnp.sqrt(position_second_new) + ROOT_EPS
    )
    return (
        layer_out,
        jnp.stack([got.astype(F32).reshape(whole) for got in dx_got], axis=0),
        grad_rows,
        left_new,
        right_new,
        weights_new,
        vector_grads,
        vector_second_new,
        vectors_new,
        position_grads,
        position_second_new,
        positions_new,
    )


def solution(mesh):
    rows = P(None, "seq", "dp", None)
    blocks = P("dp", "seq", None)
    in_specs = (
        rows, rows, P(None, "seq"), blocks, P(), P("dp", None),
        blocks, blocks, blocks, blocks, P(), P("dp", None),
    )
    out_specs = (
        rows, rows, blocks, blocks, blocks, blocks,
        P(), P(), P(), P("dp", None), P("dp", None), P("dp", None),
    )
    return jax.shard_map(body, mesh=mesh, in_specs=in_specs, out_specs=out_specs, check_vma=False)
```

```python
import functools
import itertools

import jax
import jax.numpy as jnp
from jax import lax
from jax.experimental import pallas as pl
from jax.experimental.pallas import tpu as pltpu
from jax.sharding import PartitionSpec as P

HEADS = 8
FF = 2048
WIN = 512
D = 512
BLK = 256
QKV_BLOCKS = 12
REST_BLOCKS = 36
HEAD_DIM = D // HEADS
PAIR = 2 * HEAD_DIM
PAIRS = HEADS // 2
FF_CHUNKS = FF // BLK
ROWS_VEC = 16
GROUP = 2

NORM_EPS = 1e-05
ROOT_EPS = 1e-08
DECAY = 0.5
MATRIX_RATE = 0.5
VECTOR_RATE = 0.2
MASKED = -1e30
SCALE = HEAD_DIM ** (-0.5)
ROOT_HALF = 0.7071067811865476
DENSITY = 0.3989422804014327

F32 = jnp.float32
BF16 = jnp.bfloat16


def dot_nn(left, right):
    return lax.dot_general(left, right, (((1,), (0,)), ((), ())), preferred_element_type=F32)


def dot_nt(left, right):
    return lax.dot_general(left, right, (((1,), (1,)), ((), ())), preferred_element_type=F32)


def each_piece(packing, refs, core):
    if not packing:
        yield 0, 0, refs[0]
        return
    base = 0
    for side, bits in enumerate(packing):
        for which in range(2):
            ref = refs[2 * side + which]
            blocks, rows = ref.shape[len(bits)], ref.shape[len(bits) + 1]
            last = core if which == 0 else 1 - core
            for at in itertools.product(range(2), repeat=len(bits)):
                first = sum(k * v for k, v in zip(bits, at))
                yield base, pl.multiple_of((first + last) * rows, rows), ref.at[at]
        base += blocks


def fill_qkv_matrix(full, packing, refs, core):
    side = D // BLK
    for base, offset, ref in each_piece(packing, refs, core):
        blocks, rows = ref.shape[:2]
        for n in range(blocks):
            b = base + n
            m, i, j = b // (side * side), (b // side) % side, b % side
            cols = slice(D * m + BLK * j, D * m + BLK * (j + 1))
            full[pl.ds(BLK * i + offset, rows), cols] = ref[n]


def fill_stack(stack, packing, refs, core):
    for base, offset, ref in each_piece(packing, refs, core):
        blocks, rows = ref.shape[:2]
        for n in range(blocks):
            stack[base + n, pl.ds(offset, rows), :] = ref[n]


def write_gradient(block_at, blocks, rows, core, outs):
    for b in range(blocks):
        if len(outs) == 1:
            outs[0][b] = block_at(b, 0, BLK).astype(BF16)
            continue
        for which, out in enumerate(outs):
            last = core if which == 0 else 1 - core
            for n in range(BLK // (2 * rows)):
                offset = pl.multiple_of((2 * n + last) * rows, rows)
                out[b, n * rows : (n + 1) * rows, :] = block_at(b, offset, rows).astype(BF16)


def fill_mask(mask, length):
    for i in range(WIN // BLK):
        keys = lax.broadcasted_iota(jnp.int32, (BLK, WIN), 0) + BLK * i
        queries = lax.broadcasted_iota(jnp.int32, (BLK, WIN), 1)
        keep = (keys <= queries) & (keys < length)
        mask[BLK * i : BLK * (i + 1), :] = jnp.where(keep, 0.0, MASKED).astype(F32)


def half_marks():
    lane = lax.broadcasted_iota(jnp.int32, (1, PAIR), 1)
    low = jnp.where(lane < HEAD_DIM, 1.0, 0.0)
    return (low.astype(BF16), (1.0 - low).astype(BF16))


def attention_kernel(packing, wins, meta, x_ref, bias, *refs):
    weight_refs = refs[: 2 * len(packing) or 1]
    qkv_ref, o_ref, lse_ref, full, mask = refs[len(weight_refs) :]
    step = pl.program_id(0)

    @pl.when(step == 0)
    def _():
        fill_qkv_matrix(full, packing, weight_refs, meta[wins])

    hidden = x_ref[:, 0].reshape(WIN, D)
    for m in range(3):
        cols = slice(D * m, D * (m + 1))
        rows = dot_nn(hidden, full[:, cols])
        if m != 1:
            rows = rows + bias[(m // 2) : (m // 2) + 1, :]
        qkv_ref[0, :, cols] = rows.astype(BF16)
    fill_mask(mask, meta[step])
    marks = half_marks()
    half = WIN // BLK
    for group in range(0, PAIRS, GROUP):
        cases, scores, probs = [], [], []
        for p in range(group, group + GROUP):
            at = PAIR * p
            q8 = qkv_ref[0, :, at : at + PAIR] * jnp.asarray(SCALE, BF16)
            key = qkv_ref[0, :, D + at : D + at + PAIR]
            for h in range(2):
                key_h = key * marks[h]
                for qb in range(half):
                    cols, span = slice(BLK * qb, BLK * (qb + 1)), BLK * (qb + 1)
                    cases.append((2 * p + h, qb))
                    scores.append(dot_nt(key_h[:span], q8[cols]) + mask[:span, cols])
        for (row, qb), s_t in zip(cases, scores):
            cols = slice(BLK * qb, BLK * (qb + 1))
            top = jnp.max(s_t, axis=0, keepdims=True)
            expo = jnp.exp(s_t - top)
            total = jnp.sum(expo, axis=0, keepdims=True)
            probs.append((expo * (1.0 / total)).astype(BF16))
            lse_ref[0, row : row + 1, cols] = top + jnp.log(total)
        for n, p in enumerate(range(group, group + GROUP)):
            at = PAIR * p
            val_t = jnp.transpose(qkv_ref[0, :, 2 * D + at : 2 * D + at + PAIR])
            pieces = []
            for h in range(2):
                rows = slice(HEAD_DIM * h, HEAD_DIM * (h + 1))
                first = (2 * n + h) * half
                pieces.append(
                    jnp.concatenate(
                        [
                            dot_nn(val_t[rows, : BLK * (qb + 1)], probs[first + qb])
                            for qb in range(half)
                        ],
                        axis=1,
                    )
                )
            o_ref[0, :, at : at + PAIR] = jnp.transpose(
                jnp.concatenate(pieces, axis=0)
            ).astype(BF16)


def qkv_block(acc, b, offset, rows):
    side = D // BLK
    m, i, j = b // (side * side), (b // side) % side, b % side
    return acc[pl.ds(BLK * i + offset, rows), D * m + BLK * j : D * m + BLK * (j + 1)]


def attention_back_kernel(packing, wins, part, split, meta, *refs):
    x_ref, qkv_ref, do_ref, lse_ref, da_ref = refs[:5]
    weight_refs = refs[5 : 5 + (2 * len(packing) or 1)]
    refs = refs[5 + len(weight_refs) :]
    dx_ref, refs = refs[0], refs[1:]
    dw_refs, refs = refs[: 2 if split else 1], refs[2 if split else 1 :]
    db_ref, full, mask, dqkv, acc = refs
    step = pl.program_id(0)

    @pl.when(step == 0)
    def _():
        fill_qkv_matrix(full, packing, weight_refs, meta[wins])
        acc[...] = jnp.zeros_like(acc)
        db_ref[...] = jnp.zeros_like(db_ref)

    fill_mask(mask, meta[step])
    marks = half_marks()
    for p in range(PAIRS):
        at = PAIR * p
        q8 = qkv_ref[0, :, at : at + PAIR] * jnp.asarray(SCALE, BF16)
        key = qkv_ref[0, :, D + at : D + at + PAIR]
        val = qkv_ref[0, :, 2 * D + at : 2 * D + at + PAIR]
        d_o = do_ref[0, :, at : at + PAIR]
        key_t = jnp.transpose(key)
        both = [(BLK * (qb + 1), slice(BLK * qb, BLK * (qb + 1))) for qb in range(WIN // BLK)]
        scores, grads = [], []
        for h in range(2):
            key_h, val_h = key * marks[h], val * marks[h]
            scores.append([dot_nt(key_h[:span], q8[cols]) + mask[:span, cols] for span, cols in both])
            grads.append([dot_nt(val_h[:span], d_o[cols]) for span, cols in both])
        lows, d_lows = [], []
        for h in range(2):
            row = 2 * p + h
            lows.append([])
            d_lows.append([])
            for (span, cols), s_t, d_probs in zip(both, scores[h], grads[h]):
                probs = jnp.exp(s_t - lse_ref[0, row : row + 1, cols])
                delta = jnp.sum(probs * d_probs, axis=0, keepdims=True)
                d_lows[h].append((probs * (d_probs - delta)).astype(BF16))
                lows[h].append(probs.astype(BF16))
        dq_pieces, dk_pieces, dv_pieces = [], [], []
        for h in range(2):
            rows = slice(HEAD_DIM * h, HEAD_DIM * (h + 1))
            dv_sum = dot_nn(lows[h][-1], d_o[both[-1][1]])
            dk_sum = dot_nn(d_lows[h][-1], q8[both[-1][1]])
            for (span, cols), low, d_low in list(zip(both, lows[h], d_lows[h]))[:-1]:
                dv_part, dk_part = dot_nn(low, d_o[cols]), dot_nn(d_low, q8[cols])
                dv_sum = jnp.concatenate([dv_sum[:span] + dv_part, dv_sum[span:]], axis=0)
                dk_sum = jnp.concatenate([dk_sum[:span] + dk_part, dk_sum[span:]], axis=0)
            dq_pieces.append(
                jnp.concatenate(
                    [dot_nn(key_t[rows, :span], d_low) for (span, _), d_low in zip(both, d_lows[h])],
                    axis=1,
                )
            )
            dk_pieces.append(dk_sum)
            dv_pieces.append(dv_sum)
        lane = lax.broadcasted_iota(jnp.int32, (WIN, PAIR), 1) < HEAD_DIM
        dq = jnp.transpose(jnp.concatenate(dq_pieces, axis=0)) * SCALE
        dk = jnp.where(lane, dk_pieces[0], dk_pieces[1])
        dv = jnp.where(lane, dv_pieces[0], dv_pieces[1])
        dqkv[:, at : at + PAIR] = dq.astype(BF16)
        dqkv[:, D + at : D + at + PAIR] = dk.astype(BF16)
        dqkv[:, 2 * D + at : 2 * D + at + PAIR] = dv.astype(BF16)
    h_t = jnp.transpose(x_ref[:, 0].reshape(WIN, D))
    for m in range(3):
        cols = slice(D * m, D * (m + 1))
        rows = dqkv[:, cols]
        acc[:, cols] += dot_nn(h_t, rows)
        if m != 1:
            db_ref[(m // 2) : (m // 2) + 1, :] += jnp.sum(
                rows.astype(F32), axis=0, keepdims=True
            )
    total = da_ref[0]
    for m in range(3):
        cols = slice(D * m, D * (m + 1))
        total = total + dot_nt(dqkv[:, cols], full[:, cols])
    dx_ref[:, 0] = total.astype(BF16).reshape(dx_ref.shape[0], dx_ref.shape[2], D)

    @pl.when(step == pl.num_programs(0) - 1)
    def _():
        write_gradient(
            functools.partial(qkv_block, acc), QKV_BLOCKS, part, meta[wins], dw_refs
        )


def normal_parts(u):
    size = jnp.abs(u)
    t = 1.0 / (1.0 + (0.3275911 * ROOT_HALF) * size)
    expo = jnp.exp(-0.5 * (u * u))
    poly = t * (
        0.5 * 0.254829592
        + t
        * (
            -0.5 * 0.284496736
            + t * (0.5 * 1.421413741 + t * (-0.5 * 1.453152027 + t * (0.5 * 1.061405429)))
        )
    )
    tail = poly * expo
    return jnp.where(u >= 0.0, 1.0 - tail, tail), expo


def norm_stats(rows):
    mean = jnp.mean(rows, axis=1, keepdims=True)
    centered = rows - mean
    spread = jnp.mean(centered * centered, axis=1, keepdims=True)
    inverse = lax.rsqrt(spread + NORM_EPS)
    return centered * inverse, inverse


def norm_back(d_rows, normal, inverse):
    mean_d = jnp.mean(d_rows, axis=1, keepdims=True)
    mean_dn = jnp.mean(d_rows * normal, axis=1, keepdims=True)
    return inverse * (d_rows - mean_d - normal * mean_dn)


def fill_ffn_matrices(w_out, w_up, w_down, packing, refs, core):
    side = D // BLK
    for base, offset, ref in each_piece(packing, refs, core):
        blocks, rows = ref.shape[:2]
        for n in range(blocks):
            full, i, j = ffn_place(base + n, (w_out, w_up, w_down))
            full[pl.ds(BLK * i + offset, rows), BLK * j : BLK * (j + 1)] = ref[n]


def ffn_place(b, matrices):
    side = D // BLK
    if b < side * side:
        return matrices[0], b // side, b % side
    b -= side * side
    if b < side * FF_CHUNKS:
        return matrices[1], b // FF_CHUNKS, b % FF_CHUNKS
    b -= side * FF_CHUNKS
    return matrices[2], b // side, b % side


def ffn_kernel(packing, wins, tokens, part, split, pieces, meta, *refs):
    cot_ref, x_ref, o_ref, vec = refs[:4]
    weight_refs = refs[4 : 4 + (2 * len(packing) or 1)]
    refs = refs[4 + len(weight_refs) :]
    out_refs, refs = refs[:pieces], refs[pieces:]
    da_ref, do_ref = refs[:2]
    refs = refs[2:]
    dw_refs, refs = refs[: 2 if split else 1], refs[2 if split else 1 :]
    vg_ref, w_out, w_up, w_down, acc_out, acc_up, acc_down, z_ref, gp_ref, du_ref, buf = refs
    step = pl.program_id(0)
    length = meta[step]
    accs = (acc_out, acc_up, acc_down)

    def acc_block(b, offset, rows):
        full, i, j = ffn_place(b, accs)
        if full is acc_down:
            i, j = j, i
        return full.at[pl.ds(BLK * i + offset, rows), BLK * j : BLK * (j + 1)]

    @pl.when(step == 0)
    def _():
        fill_ffn_matrices(w_out, w_up, w_down, packing, weight_refs, meta[wins])
        for acc in accs:
            acc[...] = jnp.zeros_like(acc)
        vg_ref[...] = jnp.zeros_like(vg_ref)

    def add_row(row, values, at=0):
        vg_ref[row : row + 1, at : at + values.shape[1]] += jnp.sum(
            values.astype(F32), axis=0, keepdims=True
        )

    bias_out, bias_down = vec[2:3, :], vec[7:8, :]
    gain_one, shift_one = vec[8:9, :], vec[9:10, :]
    gain_two, shift_two = vec[10:11, :], vec[11:12, :]
    attended = o_ref[0]
    mixed = x_ref[:, 0].reshape(WIN, D).astype(F32) + (dot_nn(attended, w_out[...]) + bias_out)
    n_one, inv_one = norm_stats(mixed)
    normed = n_one * gain_one + shift_one
    normed_low = normed.astype(BF16)
    for c in range(FF // D):
        cols = slice(D * c, D * (c + 1))
        u = dot_nn(normed_low, w_up[:, cols]) + vec[3 + c : 4 + c, :]
        phi, expo = normal_parts(u)
        z_ref[:, cols] = (u * phi).astype(BF16)
        gp_ref[:, cols] = phi + (u * expo) * DENSITY
    summed = normed + (dot_nn(z_ref[...], w_down[...]) + bias_down)
    n_two, inv_two = norm_stats(summed)
    result = (n_two * gain_two + shift_two).astype(BF16)
    if pieces == 1:
        out_ref = out_refs[0]
        out_ref[:, 0] = result.reshape(out_ref.shape[0], out_ref.shape[2], D)
    else:
        buf[...] = result
        for s, out_ref in enumerate(out_refs):
            rows = out_ref.shape[1]
            at = pl.multiple_of((meta[wins + 1] ^ s) * rows, rows)
            out_ref[0] = buf[pl.ds(at, rows), :]

    places = lax.broadcasted_iota(jnp.int32, (WIN, 1), 0)
    valid = jnp.where(places < length, 1.0 / tokens, 0.0).astype(F32)
    seed = cot_ref[:, 0].reshape(WIN, D).astype(F32) * valid
    add_row(10, seed * n_two)
    add_row(11, seed)
    d_summed = norm_back(seed * gain_two, n_two, inv_two)
    d_ff = d_summed.astype(BF16)
    add_row(7, d_ff)
    for c in range(FF // D):
        cols = slice(D * c, D * (c + 1))
        d_z = dot_nt(d_ff, w_down[cols, :])
        d_u = (d_z * gp_ref[:, cols]).astype(BF16)
        add_row(3 + c, d_u)
        du_ref[:, cols] = d_u
    d_ff_t = jnp.transpose(d_ff)
    normed_t = jnp.transpose(normed_low)
    for c in range(FF // D):
        cols = slice(D * c, D * (c + 1))
        acc_down[:, cols] += dot_nn(d_ff_t, z_ref[:, cols])
        acc_up[:, cols] += dot_nn(normed_t, du_ref[:, cols])
    d_normed = d_summed + dot_nt(du_ref[...], w_up[...])
    add_row(8, d_normed * n_one)
    add_row(9, d_normed)
    d_mixed = norm_back(d_normed * gain_one, n_one, inv_one)
    da_ref[0] = d_mixed
    d_branch = d_mixed.astype(BF16)
    add_row(2, d_branch)
    acc_out[...] += dot_nn(jnp.transpose(attended), d_branch)
    do_ref[0] = dot_nt(d_branch, w_out[...]).astype(BF16)

    @pl.when(step == pl.num_programs(0) - 1)
    def _():
        for j in range(D // BLK):
            for i in range(FF_CHUNKS):
                at = (slice(BLK * j, BLK * (j + 1)), slice(BLK * i, BLK * (i + 1)))
                acc_down[at] = jnp.transpose(acc_down[at])
        write_gradient(
            lambda b, offset, rows: acc_block(b, offset, rows)[...],
            REST_BLOCKS, part, meta[wins], dw_refs,
        )


def whole_spec(shape):
    zeros = (0,) * len(shape)
    return pl.BlockSpec(shape, lambda w, m: zeros, pipeline_mode=pl.Buffered(1))


def blocks_spec(part, count, at):
    lead = part.ndim - 3
    shape = part.shape[:lead] + (count,) + part.shape[lead + 1 :]
    return pl.BlockSpec(
        shape, lambda w, m: (0,) * lead + (at, 0, 0), pipeline_mode=pl.Buffered(1)
    )


def total_spec(shape):
    zeros = (0,) * len(shape)
    return pl.BlockSpec(shape, lambda w, m: zeros)


def window_spec(begin, *shape):
    zeros = (0,) * len(shape)
    return pl.BlockSpec((1,) + shape, lambda w, m: (begin + w,) + zeros)


def segment_spec(dp, seg):
    return pl.BlockSpec((dp, 1, seg, D), lambda w, m: (0, w, 0, 0))


def input_spec(dp, seg, begin):
    return pl.BlockSpec((dp, 1, seg, D), lambda w, m: (0, begin + w, 0, 0))


def gradient_outs(blocks, part):
    if part % 16:
        return [jax.ShapeDtypeStruct((blocks, BLK, BLK), BF16)]
    return [jax.ShapeDtypeStruct((blocks, BLK // 2, BLK), BF16)] * 2


def run_kernel(kernel, wins, meta, ins, outs, scratch, flops, moved):
    return pl.pallas_call(
        kernel,
        grid_spec=pltpu.PrefetchScalarGridSpec(
            num_scalar_prefetch=1,
            grid=(wins,),
            in_specs=[spec for _, spec in ins],
            out_specs=[spec for _, spec in outs],
            scratch_shapes=scratch,
        ),
        out_shape=[shape for shape, _ in outs],
        compiler_params=pltpu.CompilerParams(
            dimension_semantics=("arbitrary",), vmem_limit_bytes=56 * 1024 * 1024
        ),
        cost_estimate=pl.CostEstimate(
            flops=flops, bytes_accessed=moved, transcendentals=wins * WIN * FF
        ),
    )(meta, *[values for values, _ in ins])


def call_attention(wins, meta, x, packing, weight_parts, bias):
    dp, _, seg, _ = x.shape
    shape = jax.ShapeDtypeStruct
    return run_kernel(
        functools.partial(attention_kernel, packing, wins),
        wins,
        meta,
        [(x, input_spec(dp, seg, 0)), (bias, whole_spec(bias.shape))]
        + [(piece, whole_spec(piece.shape)) for piece in weight_parts],
        [
            (shape((wins, WIN, 3 * D), BF16), window_spec(0, WIN, 3 * D)),
            (shape((wins, WIN, D), BF16), window_spec(0, WIN, D)),
            (shape((wins, HEADS, WIN), F32), window_spec(0, HEADS, WIN)),
        ],
        [pltpu.VMEM((D, 3 * D), BF16), pltpu.VMEM((WIN, WIN), F32)],
        wins * 250_000_000,
        wins * 1_000_000,
    )


def call_ffn(wins, tokens, part, apart, meta, x, attended, packing, weight_parts, vec):
    dp, _, seg, _ = x.shape
    shape = jax.ShapeDtypeStruct
    counts = (QKV_BLOCKS, QKV_BLOCKS, 2 * QKV_BLOCKS, 2 * QKV_BLOCKS)
    ins = [
        (x, input_spec(dp, seg, wins)),
        (x, input_spec(dp, seg, 0)),
        (attended, window_spec(0, WIN, D)),
        (vec, whole_spec(vec.shape)),
    ] + [
        (piece, blocks_spec(piece, count, 0) if packing else whole_spec(piece.shape))
        for piece, count in zip(weight_parts, counts)
    ]
    outs = [(shape((dp, wins, seg, D), BF16), segment_spec(dp, seg))]
    if apart:
        outs = [(shape((wins, seg, D), BF16), window_spec(0, seg, D))] * dp
    return run_kernel(
        functools.partial(ffn_kernel, packing, wins, tokens, part, part % 16 == 0, dp if apart else 1),
        wins,
        meta,
        ins,
        [
            *outs,
            (shape((wins, WIN, D), F32), window_spec(0, WIN, D)),
            (shape((wins, WIN, D), BF16), window_spec(0, WIN, D)),
        ]
        + [(out, total_spec(out.shape)) for out in gradient_outs(REST_BLOCKS, part)]
        + [(shape((ROWS_VEC, D), F32), total_spec((ROWS_VEC, D)))],
        [
            pltpu.VMEM((D, D), BF16),
            pltpu.VMEM((D, FF), BF16),
            pltpu.VMEM((FF, D), BF16),
            pltpu.VMEM((D, D), F32),
            pltpu.VMEM((D, FF), F32),
            pltpu.VMEM((D, FF), F32),
            pltpu.VMEM((WIN, FF), BF16),
            pltpu.VMEM((WIN, FF), F32),
            pltpu.VMEM((WIN, FF), BF16),
            pltpu.VMEM((WIN, D), BF16),
        ],
        wins * 250_000_000,
        wins * 1_000_000,
    )


def call_attention_back(
    part, meta, packing, weight_parts, x, qkv, d_o, lse, d_mixed
):
    dp, _, seg, _ = x.shape
    wins = d_o.shape[0]
    shape = jax.ShapeDtypeStruct
    return run_kernel(
        functools.partial(attention_back_kernel, packing, wins, part, part % 16 == 0),
        wins,
        meta,
        [
            (x, input_spec(dp, seg, 0)),
            (qkv, window_spec(0, WIN, 3 * D)),
            (d_o, window_spec(0, WIN, D)),
            (lse, window_spec(0, HEADS, WIN)),
            (d_mixed, window_spec(0, WIN, D)),
        ]
        + [(piece, whole_spec(piece.shape)) for piece in weight_parts],
        [(shape((dp, wins, seg, D), BF16), segment_spec(dp, seg))]
        + [(out, total_spec(out.shape)) for out in gradient_outs(QKV_BLOCKS, part)]
        + [(shape((8, D), F32), total_spec((8, D)))],
        [
            pltpu.VMEM((D, 3 * D), BF16),
            pltpu.VMEM((WIN, WIN), F32),
            pltpu.VMEM((WIN, 3 * D), BF16),
            pltpu.VMEM((D, 3 * D), F32),
        ],
        wins * 12_500_000_000,
        wins * 8_000_000,
    )


def split_first_kernel(terms, bits, *refs):
    ins, outs = refs[:terms], refs[terms:]

    def total(side, at):
        return sum(ref[side, :, at].astype(F32) for ref in ins).astype(BF16)

    for y in range(2):
        for which in range(2):
            outs[which][:, y] = total(0, 2 * y + (bits[0] if which == 0 else 1 - bits[0]))
    for x in range(2):
        for which in range(2):
            outs[2 + which][:, x] = total(1, 2 * (bits[1] if which == 0 else 1 - bits[1]) + x)


def split_second_kernel(bits, *refs):
    for side in range(2):
        mine, got = refs[2 * side : 2 * side + 2]
        for which in range(2):
            bit = bits[1 - side]
            at = bit if which == 0 else 1 - bit
            refs[4 + 2 * side + which][...] = (
                mine[:, at].astype(F32) + got[:, at].astype(F32)
            ).astype(BF16)


def slabs_kernel(dp, me_ref, *refs):
    pairs, vec, outs, total = refs[: len(refs) - dp - 2], refs[-dp - 2], refs[-dp - 1 : -1], refs[-1]
    base = 0
    for n in range(0, len(pairs), 2):
        blocks = pairs[n].shape[0]
        total[base : base + blocks] = pairs[n][...].astype(F32) + pairs[n + 1][...].astype(F32)
        base += blocks
    owned = outs[0].shape[0] - 1
    for s in range(dp):
        slab = total[pl.ds((me_ref[0] ^ s) * owned, owned)]
        outs[s][:owned] = slab.astype(outs[s].dtype)
        outs[s][owned] = vec[...].astype(BF16).astype(outs[s].dtype)


def update_kernel(packing, scalars, *refs):
    count = 2 * len(packing)
    parts, root_parts, refs = refs[:count], refs[count : 2 * count], refs[2 * count :]
    own, left_stats, right_stats, left_roots, weights = refs[:5]
    left_new, right_new, weights_new, full, roots = refs[5:]
    fill_stack(full, packing, parts, scalars[0])
    fill_stack(roots, packing, root_parts, scalars[0])
    blocks, rows, _ = own.shape
    at = scalars[1] * rows
    lane = lax.broadcasted_iota(jnp.int32, (rows, BLK), 1)
    line = lax.broadcasted_iota(jnp.int32, (rows, BLK), 0)
    pick = jnp.where(lane == line + at, 1.0, 0.0).astype(BF16)
    for b in range(blocks):
        whole = full[b]
        crossed = dot_nt(jnp.concatenate([own[b], pick], axis=0), whole)
        left_new[b] = DECAY * left_stats[b] + (1.0 - DECAY) * crossed[:rows]
        turned = jnp.concatenate([left_roots[b].astype(BF16), crossed[rows:].astype(BF16)], axis=0)
        passed = dot_nn(turned, whole)
        right_new[b] = DECAY * right_stats[b] + (1.0 - DECAY) * passed[rows:]
        step = dot_nn(passed[:rows].astype(BF16), roots[b])
        weights_new[b] = weights[b] - MATRIX_RATE * step


def call_small(kernel, steps, scalars, ins, outs, scratch=()):
    def spec(shape, axis):
        if isinstance(axis, pl.BlockSpec):
            return axis
        block = tuple(n // steps if d == axis else n for d, n in enumerate(shape))
        return pl.BlockSpec(block, lambda g, m: tuple(g if d == axis else 0 for d in range(len(shape))))

    return pl.pallas_call(
        kernel,
        grid_spec=pltpu.PrefetchScalarGridSpec(
            num_scalar_prefetch=1,
            grid=(steps,),
            in_specs=[spec(values.shape, axis) for values, axis in ins],
            out_specs=[spec(shape.shape, axis) for shape, axis in outs],
            scratch_shapes=list(scratch),
        ),
        out_shape=[shape for shape, _ in outs],
        compiler_params=pltpu.CompilerParams(
            dimension_semantics=("arbitrary",), vmem_limit_bytes=32 * 1024 * 1024
        ),
    )(scalars, *[values for values, _ in ins])


def update_blocks(scalars, packing, parts, root_parts, own, *shards):
    blocks = own.shape[0]
    out = jax.ShapeDtypeStruct(own.shape, F32)
    share = blocks // 2
    ats = (QKV_BLOCKS // share, QKV_BLOCKS // share, 2 * QKV_BLOCKS // share, 2 * QKV_BLOCKS // share)
    return call_small(
        functools.partial(update_kernel, packing),
        1,
        scalars,
        [(part, None) for part in parts]
        + [(part, blocks_spec(part, share, at)) for part, at in zip(root_parts, ats)]
        + [(values, None) for values in (own, *shards)],
        [(out, None)] * 3,
        [pltpu.VMEM((blocks, BLK, BLK), BF16)] * 2,
    )


def split_first(bits, *terms):
    blocks, height, cols = terms[0].shape
    half = blocks // 2
    view = (2, half, 4, height // 4, cols)
    out = jax.ShapeDtypeStruct((half, 2, height // 4, cols), BF16)
    return call_small(
        functools.partial(split_first_kernel, len(terms)),
        max(half // 6, 1),
        bits,
        [(term.reshape(view), 1) for term in terms],
        [(out, 0)] * 4,
    )


def split_second(bits, *parts):
    half, _, rows, cols = parts[0].shape
    out = jax.ShapeDtypeStruct((half, rows, cols), BF16)
    return call_small(
        split_second_kernel, 1, bits, [(part, 0) for part in parts], [(out, 0)] * 4
    )


def make_slabs(dp, me, parts, vec):
    _, rows, cols = parts[0].shape
    blocks = sum(part.shape[0] for part in parts) // 2
    shape = (blocks // dp + 1, rows, cols)
    return call_small(
        functools.partial(slabs_kernel, dp),
        1,
        me,
        [(part, None) for part in [*parts, vec]],
        [(jax.ShapeDtypeStruct(shape, F32 if s == 0 else BF16), None) for s in range(dp)],
        [pltpu.VMEM((blocks, rows, cols), F32)],
    )


def swap(values, axis, size, k):
    return lax.ppermute(values, axis, [(i, i ^ k) for i in range(size)])


def bits_of(size):
    return [1 << i for i in range(size.bit_length() - 1)]


def hop_orders(seq_count):
    high = [k for k in bits_of(seq_count) if k > 1]
    return (high, high[::-1])


def gather_hop(state, k, seq_count, seq_index, *marks):
    cur, lead = state
    got = after(swap(cur, "seq", seq_count, k), *marks)
    odd = (seq_index & k) != 0
    cur = jnp.stack([jnp.where(odd, got, cur), jnp.where(odd, cur, got)], axis=0)
    return cur, [k] + lead


def gather_end(state):
    cur, lead = state
    count = len(lead)
    blocks, rows, cols = cur.shape[count:]
    axes = [count] + [lead.index(k) for k in sorted(lead, reverse=True)] + [count + 1, count + 2]
    return cur.transpose(axes).reshape(blocks, rows << count, cols)


def halves(cur):
    half = cur.shape[0] // 2
    return [cur[:half], cur[half:]]


def gather_split(cur, seq_count, seq_index):
    done = []
    for part, order in zip(halves(cur), hop_orders(seq_count)):
        state = (part, [])
        for k in order + [1]:
            state = gather_hop(state, k, seq_count, seq_index)
        done.append(gather_end(state))
    return jnp.concatenate(done, axis=0)


def pack_weights(rows, roots, orders, seq_count, seq_index):
    states = [
        (jnp.concatenate(pair, axis=0), []) for pair in zip(halves(rows), halves(roots))
    ]
    for step in range(len(orders[0])):
        states = [
            gather_hop(state, order[step], seq_count, seq_index)
            for state, order in zip(states, orders)
        ]
        if step == 0:
            cur, lead = states[0]
            axis = len(lead)
            states = [
                (lax.slice_in_dim(cur, 0, QKV_BLOCKS, axis=axis), lead),
                (lax.slice_in_dim(cur, QKV_BLOCKS, cur.shape[axis], axis=axis), lead),
                states[1],
            ]
            orders = (orders[0], orders[0], orders[1])
    return states


def join_cores(states, seq_count, seq_index, *marks):
    if states[0][0].shape[-2] % 16:
        states = [gather_hop(state, 1, seq_count, seq_index) for state in states]
        return (), [jnp.concatenate([gather_end(state) for state in states], axis=0)]
    parts = []
    for cur, _ in states:
        parts += [cur, after(swap(cur, "seq", seq_count, 1), *marks)]
    return tuple(tuple(lead) for _, lead in states), parts


def scatter_first(whole, seq_count, seq_index):
    left = sorted(bits_of(seq_count), reverse=True)
    blocks, height, cols = whole.shape
    rows = height // seq_count
    cur = whole.reshape(blocks, seq_count // 2, 2, rows, cols)
    mine, other = [
        lax.dynamic_index_in_dim(cur, bit, 2, keepdims=False)
        for bit in (seq_index % 2, 1 - seq_index % 2)
    ]
    cur = mine.astype(F32) + swap(other, "seq", seq_count, 1).astype(F32)
    left.remove(1)
    cur = cur.astype(BF16).reshape([blocks] + [2] * len(left) + [rows, cols])
    return [(half, left) for half in halves(cur)]


def scatter_hop(state, k, seq_count, seq_index, *marks):
    cur, left = state
    axis = 1 + left.index(k)
    bit = (seq_index // k) % 2
    mine = lax.dynamic_index_in_dim(cur, bit, axis, keepdims=False)
    other = lax.dynamic_index_in_dim(cur, 1 - bit, axis, keepdims=False)
    got = after(swap(other, "seq", seq_count, k), *marks)
    cur = (mine.astype(F32) + got.astype(F32)).astype(BF16)
    return cur, [b for b in left if b != k]


def after(values, *marks):
    if not marks:
        return values
    return lax.optimization_barrier((values, marks))[0]


def body(
    inputs,
    cotangent,
    lengths,
    weights,
    vectors,
    positions,
    left_stats,
    right_stats,
    left_roots,
    right_roots,
    vector_second,
    position_second,
):
    seq_count = lax.axis_size("seq")
    dp_count = lax.axis_size("dp")
    seq_index = lax.axis_index("seq")
    dp_index = lax.axis_index("dp")
    micro, wins_dev, segment, model_width = inputs.shape
    wins = wins_dev // dp_count
    total_tokens = micro * wins_dev * seq_count * segment * dp_count
    owned, row_part, _ = weights.shape
    def exchange(rows):
        return lax.all_to_all(rows, "dp", 0, 0, tiled=True)

    grouped = (dp_count, wins, segment, model_width)
    own = weights.astype(BF16)
    orders = hop_orders(seq_count)
    hops = len(orders[0])

    def scatter_both(states, step, *marks):
        return [
            scatter_hop(state, order[step], seq_count, seq_index, *marks)
            for state, order in zip(states, orders)
        ]

    vec = vectors.reshape(-1, D)
    bias_qv = jnp.concatenate([vec[0:2], jnp.zeros((6, D), F32)], axis=0)
    vec_pad = jnp.concatenate([vec, jnp.zeros((ROWS_VEC - vec.shape[0], D), F32)], axis=0)

    metas = [
        lax.dynamic_index_in_dim(
            lengths[i].reshape(dp_count, wins), dp_index, 0, keepdims=False
        )
        for i in range(micro)
    ]
    metas = [
        jnp.concatenate([lens, (seq_index % 2)[None], dp_index[None]]).astype(jnp.int32)
        for lens in metas
    ]
    shards = [own] + [swap(own, "dp", dp_count, s) for s in range(1, dp_count)]
    weight_rows = jnp.concatenate(
        [lax.select_n(dp_index ^ j, *shards) for j in range(dp_count)], axis=0
    )
    pairs = [
        jnp.concatenate(
            [
                (inputs[i].astype(F32) + positions[None]).astype(BF16).reshape(grouped),
                cotangent[i].reshape(grouped),
            ],
            axis=1,
        )
        for i in range(micro)
    ]
    taken = [exchange(after(pairs[0], *shards[1:]))]
    roots_low = right_roots.astype(BF16)
    groups = pack_weights(weight_rows, roots_low, orders, seq_count, seq_index)
    cur, lead = groups[0]
    groups[0] = (after(cur, vec_pad, bias_qv, roots_low, *metas), lead)
    packing_qkv, parts_qkv = join_cores(groups[:1], seq_count, seq_index)
    for i in range(1, micro):
        marks = (taken[-1], *metas, *parts_qkv, *(cur for cur, _ in groups[1:]))
        taken.append(exchange(after(pairs[i], *marks)))
    ffn, out_got, dx_got = [], [], []
    forward = [
        call_attention(wins, metas[0], taken[0], packing_qkv, parts_qkv, bias_qv)
    ]
    mark = (forward[0][2],)
    lse = forward[0][2]
    packing_rest, parts_rest = join_cores(groups[1:], seq_count, seq_index, lse)
    share = owned // 2
    if not packing_rest:
        (stack,) = parts_rest
        middle = QKV_BLOCKS + share
        roots_full = jnp.concatenate([stack[QKV_BLOCKS:middle], stack[-share:]], axis=0)
        parts_rest = [jnp.concatenate([stack[:QKV_BLOCKS], stack[middle:-share]], axis=0)]
    fast = seq_count == 8 and row_part % 16 == 0
    bits = jnp.stack([(seq_index // 2) % 2, (seq_index // 4) % 2]).astype(jnp.int32)

    def over_cores(parts, *marks):
        keep, send = parts
        return [keep, after(swap(send, "seq", seq_count, 1), *marks)]

    def hop(parts, count, *marks):
        mine_a, send_a, mine_b, send_b = parts
        k_a, k_b = (2, 4) if count == 0 else (4, 2)
        got_a = after(swap(send_a, "seq", seq_count, k_a), *marks)
        got_b = after(swap(send_b, "seq", seq_count, k_b), *marks)
        return [mine_a, got_a, mine_b, got_b]

    vec_sums = jnp.zeros((ROWS_VEC, D), F32)
    dw_rest, dw_qkv = [], []
    for i in range(micro):
        if i > 0:
            forward.append(
                call_attention(
                    wins, after(metas[i], *mark), taken[i], packing_qkv, parts_qkv, bias_qv
                )
            )
            mark = (forward[i][2],)
        results = call_ffn(
            wins, total_tokens, row_part, True, after(metas[i], *mark), taken[i], forward[i][1],
            packing_rest, parts_rest, vec_pad,
        )
        out, (d_mixed, d_o, *dw, vg) = results[:dp_count], results[dp_count:]
        got = [out[0]] + [swap(out[s], "dp", dp_count, s) for s in range(1, dp_count)]
        out_got.append(tuple(got))
        ffn.append((d_mixed, d_o))
        vec_sums = vec_sums + vg
        mark = (vg,)
        dw_rest.append(dw)
    gates = mark + (out_got[0],)
    rest_core, qkv_core = [], []
    for i in range(micro):
        dx, *dw, db = call_attention_back(
            row_part, after(metas[i], gates), packing_qkv, parts_qkv, taken[i], forward[i][0],
            ffn[i][1], forward[i][2], ffn[i][0],
        )
        vec_sums = vec_sums + jnp.concatenate([db, jnp.zeros_like(db)], axis=0)
        dw_qkv.append(dw)
        gates = (db,) + tuple(out_got[1:])
        if fast and i == 0:
            for n in range(micro):
                rest_core += over_cores(dw_rest[n], *(mark[:1] if n == 0 else (db,)))
            rest = split_first(bits, *rest_core)
            gates = gates + tuple(rest)
        if fast and i == micro - 1:
            rest = hop(rest, 0, db)
            qkv_core += over_cores(dw_qkv[0], db)
            dx = after(dx, *rest)
        dx_got.append(exchange(after(dx, *dx_got[-1:])))

    whole = (wins_dev, segment, model_width)
    out_got = [
        jnp.stack([lax.select_n(dp_index ^ e, *got) for e in range(dp_count)]) for got in out_got
    ]
    layer_out = jnp.stack([got.reshape(whole) for got in out_got], axis=0)

    for k in bits_of(seq_count):
        vec_sums = vec_sums + swap(vec_sums, "seq", seq_count, k)
    if fast:
        qkv_core += over_cores(dw_qkv[1])
        states = split_first(bits, *qkv_core)
        rest = hop(split_second(bits, *rest), 1)
        states = hop(split_second(bits, *hop(states, 0)), 1)
        slabs = make_slabs(
            dp_count, after(dp_index[None].astype(jnp.int32), dx_got[-1], layer_out), states + rest,
            vec_sums.reshape(row_part, BLK),
        )
    else:
        states = []
        for parts in (dw_qkv, dw_rest):
            total = sum(part[0].astype(F32) for part in parts).astype(BF16)
            group = scatter_first(total, seq_count, seq_index)
            for step in range(hops):
                group = scatter_both(group, step)
            states += group
        joined = jnp.concatenate([cur for cur, _ in states], axis=0)
        joined = joined.reshape((dp_count, owned) + joined.shape[1:])
        vec_rows = vec_sums.astype(BF16).reshape(-1, row_part, BLK)
        slabs = [
            jnp.concatenate(
                [lax.dynamic_index_in_dim(joined, dp_index ^ s, 0, keepdims=False), vec_rows]
            )
            for s in range(dp_count)
        ]
    slabs = [slabs[0].astype(F32)] + [
        swap(slabs[s], "dp", dp_count, s).astype(F32) for s in range(1, dp_count)
    ]
    grad_rows = sum(slab[:owned] for slab in slabs)
    vec_sums = sum(lax.select_n(dp_index ^ j, *[slab[owned:] for slab in slabs]) for j in range(dp_count))
    vec_sums = vec_sums.reshape(ROWS_VEC, D)
    grad_low = grad_rows.astype(BF16)
    if fast:
        states = [(part, []) for part in halves(grad_low)]
        for step in range(hops):
            states = [
                gather_hop(state, order[step], seq_count, seq_index)
                for state, order in zip(states, orders)
            ]
        packing, parts = join_cores(states, seq_count, seq_index)
        left_new, right_new, weights_new = update_blocks(
            jnp.stack([seq_index % 2, seq_index]).astype(jnp.int32), packing, parts, parts_rest,
            grad_low, left_stats, right_stats, left_roots, weights,
        )
    else:
        grad_full = gather_split(grad_low, seq_count, seq_index)
        row_start = seq_index * row_part

        def batched(spec, left, right):
            return jnp.einsum(spec, left, right, preferred_element_type=F32)

        left_new = DECAY * left_stats + (1.0 - DECAY) * batched("bij,bkj->bik", grad_low, grad_full)
        column_part = lax.dynamic_slice_in_dim(grad_full, row_start, row_part, 2)
        right_new = DECAY * right_stats + (1.0 - DECAY) * batched(
            "bki,bkj->bij", column_part, grad_full
        )
        left_applied = batched("bij,bjk->bik", left_roots.astype(BF16), grad_full)
        step_rows = batched("bij,bjk->bik", left_applied.astype(BF16), roots_full)
        weights_new = weights - MATRIX_RATE * step_rows

    place_sum = sum(jnp.sum(got.astype(F32), axis=(0, 1)) for got in dx_got)
    for k in bits_of(seq_count):
        low = place_sum.astype(BF16)
        place_sum = low.astype(F32) + swap(low, "seq", seq_count, k).astype(F32)
    vector_grads = vec_sums[: vec.shape[0]].reshape(-1)
    vector_second_new = DECAY * vector_second + (1.0 - DECAY) * vector_grads * vector_grads
    vectors_new = vectors - VECTOR_RATE * vector_grads / (jnp.sqrt(vector_second_new) + ROOT_EPS)
    position_grads = place_sum
    position_second_new = DECAY * position_second + (1.0 - DECAY) * position_grads * position_grads
    positions_new = positions - VECTOR_RATE * position_grads / (
        jnp.sqrt(position_second_new) + ROOT_EPS
    )
    return (
        layer_out,
        jnp.stack([got.astype(F32).reshape(whole) for got in dx_got], axis=0),
        grad_rows,
        left_new,
        right_new,
        weights_new,
        vector_grads,
        vector_second_new,
        vectors_new,
        position_grads,
        position_second_new,
        positions_new,
    )


def solution(mesh):
    rows = P(None, "seq", "dp", None)
    blocks = P("dp", "seq", None)
    in_specs = (
        rows, rows, P(None, "seq"), blocks, P(), P("dp", None),
        blocks, blocks, blocks, blocks, P(), P("dp", None),
    )
    out_specs = (
        rows, rows, blocks, blocks, blocks, blocks,
        P(), P(), P(), P("dp", None), P("dp", None), P("dp", None),
    )
    return jax.shard_map(body, mesh=mesh, in_specs=in_specs, out_specs=out_specs, check_vma=False)
```

```python
import functools
import itertools

import jax
import jax.numpy as jnp
from jax import lax
from jax.experimental import pallas as pl
from jax.experimental.pallas import tpu as pltpu
from jax.sharding import PartitionSpec as P

HEADS = 8
FF = 2048
WIN = 512
D = 512
BLK = 256
QKV_BLOCKS = 12
REST_BLOCKS = 36
HEAD_DIM = D // HEADS
PAIR = 2 * HEAD_DIM
PAIRS = HEADS // 2
FF_CHUNKS = FF // BLK
ROWS_VEC = 16
GROUP = 2

NORM_EPS = 1e-05
ROOT_EPS = 1e-08
DECAY = 0.5
MATRIX_RATE = 0.5
VECTOR_RATE = 0.2
MASKED = -1e30
SCALE = HEAD_DIM ** (-0.5)
ROOT_HALF = 0.7071067811865476
DENSITY = 0.3989422804014327

F32 = jnp.float32
BF16 = jnp.bfloat16


def dot_nn(left, right):
    return lax.dot_general(left, right, (((1,), (0,)), ((), ())), preferred_element_type=F32)


def dot_nt(left, right):
    return lax.dot_general(left, right, (((1,), (1,)), ((), ())), preferred_element_type=F32)


def each_piece(packing, refs, core):
    if not packing:
        yield 0, 0, refs[0]
        return
    base = 0
    for side, bits in enumerate(packing):
        for which in range(2):
            ref = refs[2 * side + which]
            blocks, rows = ref.shape[len(bits)], ref.shape[len(bits) + 1]
            last = core if which == 0 else 1 - core
            for at in itertools.product(range(2), repeat=len(bits)):
                first = sum(k * v for k, v in zip(bits, at))
                yield base, pl.multiple_of((first + last) * rows, rows), ref.at[at]
        base += blocks


def fill_qkv_matrix(full, packing, refs, core):
    side = D // BLK
    for base, offset, ref in each_piece(packing, refs, core):
        blocks, rows = ref.shape[:2]
        for n in range(blocks):
            b = base + n
            m, i, j = b // (side * side), (b // side) % side, b % side
            cols = slice(D * m + BLK * j, D * m + BLK * (j + 1))
            full[pl.ds(BLK * i + offset, rows), cols] = ref[n]


def fill_stack(stack, packing, refs, core):
    for base, offset, ref in each_piece(packing, refs, core):
        blocks, rows = ref.shape[:2]
        for n in range(blocks):
            stack[base + n, pl.ds(offset, rows), :] = ref[n]


def write_gradient(block_at, blocks, rows, core, outs):
    for b in range(blocks):
        if len(outs) == 1:
            outs[0][b] = block_at(b, 0, BLK).astype(BF16)
            continue
        for which, out in enumerate(outs):
            last = core if which == 0 else 1 - core
            for n in range(BLK // (2 * rows)):
                offset = pl.multiple_of((2 * n + last) * rows, rows)
                out[b, n * rows : (n + 1) * rows, :] = block_at(b, offset, rows).astype(BF16)


def fill_mask(mask, length):
    for i in range(WIN // BLK):
        keys = lax.broadcasted_iota(jnp.int32, (BLK, WIN), 0) + BLK * i
        queries = lax.broadcasted_iota(jnp.int32, (BLK, WIN), 1)
        keep = (keys <= queries) & (keys < length)
        mask[BLK * i : BLK * (i + 1), :] = jnp.where(keep, 0.0, MASKED).astype(F32)


def half_marks():
    lane = lax.broadcasted_iota(jnp.int32, (1, PAIR), 1)
    low = jnp.where(lane < HEAD_DIM, 1.0, 0.0)
    return (low.astype(BF16), (1.0 - low).astype(BF16))


def attention_kernel(packing, wins, meta, x_ref, bias, *refs):
    weight_refs = refs[: 2 * len(packing) or 1]
    qkv_ref, o_ref, lse_ref, full, mask = refs[len(weight_refs) :]
    step = pl.program_id(0)

    @pl.when(step == 0)
    def _():
        fill_qkv_matrix(full, packing, weight_refs, meta[wins])

    hidden = x_ref[:, 0].reshape(WIN, D)
    for m in range(3):
        cols = slice(D * m, D * (m + 1))
        rows = dot_nn(hidden, full[:, cols])
        if m != 1:
            rows = rows + bias[(m // 2) : (m // 2) + 1, :]
        qkv_ref[0, :, cols] = rows.astype(BF16)
    fill_mask(mask, meta[step])
    marks = half_marks()
    half = WIN // BLK
    for group in range(0, PAIRS, GROUP):
        cases, scores, probs = [], [], []
        for p in range(group, group + GROUP):
            at = PAIR * p
            q8 = qkv_ref[0, :, at : at + PAIR] * jnp.asarray(SCALE, BF16)
            key = qkv_ref[0, :, D + at : D + at + PAIR]
            for h in range(2):
                key_h = key * marks[h]
                for qb in range(half):
                    cols, span = slice(BLK * qb, BLK * (qb + 1)), BLK * (qb + 1)
                    cases.append((2 * p + h, qb))
                    scores.append(dot_nt(key_h[:span], q8[cols]) + mask[:span, cols])
        for (row, qb), s_t in zip(cases, scores):
            cols = slice(BLK * qb, BLK * (qb + 1))
            top = jnp.max(s_t, axis=0, keepdims=True)
            expo = jnp.exp(s_t - top)
            total = jnp.sum(expo, axis=0, keepdims=True)
            probs.append((expo * (1.0 / total)).astype(BF16))
            lse_ref[0, row : row + 1, cols] = top + jnp.log(total)
        for n, p in enumerate(range(group, group + GROUP)):
            at = PAIR * p
            val_t = jnp.transpose(qkv_ref[0, :, 2 * D + at : 2 * D + at + PAIR])
            pieces = []
            for h in range(2):
                rows = slice(HEAD_DIM * h, HEAD_DIM * (h + 1))
                first = (2 * n + h) * half
                pieces.append(
                    jnp.concatenate(
                        [
                            dot_nn(val_t[rows, : BLK * (qb + 1)], probs[first + qb])
                            for qb in range(half)
                        ],
                        axis=1,
                    )
                )
            o_ref[0, :, at : at + PAIR] = jnp.transpose(
                jnp.concatenate(pieces, axis=0)
            ).astype(BF16)


def qkv_block(acc, b, offset, rows):
    side = D // BLK
    m, i, j = b // (side * side), (b // side) % side, b % side
    return acc[pl.ds(BLK * i + offset, rows), D * m + BLK * j : D * m + BLK * (j + 1)]


def attention_back_kernel(packing, wins, part, split, meta, *refs):
    x_ref, qkv_ref, do_ref, lse_ref, da_ref = refs[:5]
    weight_refs = refs[5 : 5 + (2 * len(packing) or 1)]
    refs = refs[5 + len(weight_refs) :]
    dx_ref, refs = refs[0], refs[1:]
    dw_refs, refs = refs[: 2 if split else 1], refs[2 if split else 1 :]
    db_ref, full, mask, dqkv, acc = refs
    step = pl.program_id(0)

    @pl.when(step == 0)
    def _():
        fill_qkv_matrix(full, packing, weight_refs, meta[wins])
        acc[...] = jnp.zeros_like(acc)
        db_ref[...] = jnp.zeros_like(db_ref)

    fill_mask(mask, meta[step])
    marks = half_marks()
    for p in range(PAIRS):
        at = PAIR * p
        q8 = qkv_ref[0, :, at : at + PAIR] * jnp.asarray(SCALE, BF16)
        key = qkv_ref[0, :, D + at : D + at + PAIR]
        val = qkv_ref[0, :, 2 * D + at : 2 * D + at + PAIR]
        d_o = do_ref[0, :, at : at + PAIR]
        key_t = jnp.transpose(key)
        both = [(BLK * (qb + 1), slice(BLK * qb, BLK * (qb + 1))) for qb in range(WIN // BLK)]
        scores, grads = [], []
        for h in range(2):
            key_h, val_h = key * marks[h], val * marks[h]
            scores.append([dot_nt(key_h[:span], q8[cols]) + mask[:span, cols] for span, cols in both])
            grads.append([dot_nt(val_h[:span], d_o[cols]) for span, cols in both])
        lows, d_lows = [], []
        for h in range(2):
            row = 2 * p + h
            lows.append([])
            d_lows.append([])
            for (span, cols), s_t, d_probs in zip(both, scores[h], grads[h]):
                probs = jnp.exp(s_t - lse_ref[0, row : row + 1, cols])
                delta = jnp.sum(probs * d_probs, axis=0, keepdims=True)
                d_lows[h].append((probs * (d_probs - delta)).astype(BF16))
                lows[h].append(probs.astype(BF16))
        dq_pieces, dk_pieces, dv_pieces = [], [], []
        for h in range(2):
            rows = slice(HEAD_DIM * h, HEAD_DIM * (h + 1))
            dv_sum = dot_nn(lows[h][-1], d_o[both[-1][1]])
            dk_sum = dot_nn(d_lows[h][-1], q8[both[-1][1]])
            for (span, cols), low, d_low in list(zip(both, lows[h], d_lows[h]))[:-1]:
                dv_part, dk_part = dot_nn(low, d_o[cols]), dot_nn(d_low, q8[cols])
                dv_sum = jnp.concatenate([dv_sum[:span] + dv_part, dv_sum[span:]], axis=0)
                dk_sum = jnp.concatenate([dk_sum[:span] + dk_part, dk_sum[span:]], axis=0)
            dq_pieces.append(
                jnp.concatenate(
                    [dot_nn(key_t[rows, :span], d_low) for (span, _), d_low in zip(both, d_lows[h])],
                    axis=1,
                )
            )
            dk_pieces.append(dk_sum)
            dv_pieces.append(dv_sum)
        lane = lax.broadcasted_iota(jnp.int32, (WIN, PAIR), 1) < HEAD_DIM
        dq = jnp.transpose(jnp.concatenate(dq_pieces, axis=0)) * SCALE
        dk = jnp.where(lane, dk_pieces[0], dk_pieces[1])
        dv = jnp.where(lane, dv_pieces[0], dv_pieces[1])
        dqkv[:, at : at + PAIR] = dq.astype(BF16)
        dqkv[:, D + at : D + at + PAIR] = dk.astype(BF16)
        dqkv[:, 2 * D + at : 2 * D + at + PAIR] = dv.astype(BF16)
    h_t = jnp.transpose(x_ref[:, 0].reshape(WIN, D))
    for m in range(3):
        cols = slice(D * m, D * (m + 1))
        rows = dqkv[:, cols]
        acc[:, cols] += dot_nn(h_t, rows)
        if m != 1:
            db_ref[(m // 2) : (m // 2) + 1, :] += jnp.sum(
                rows.astype(F32), axis=0, keepdims=True
            )
    total = da_ref[0]
    for m in range(3):
        cols = slice(D * m, D * (m + 1))
        total = total + dot_nt(dqkv[:, cols], full[:, cols])
    dx_ref[:, 0] = total.astype(BF16).reshape(dx_ref.shape[0], dx_ref.shape[2], D)

    @pl.when(step == pl.num_programs(0) - 1)
    def _():
        write_gradient(
            functools.partial(qkv_block, acc), QKV_BLOCKS, part, meta[wins], dw_refs
        )


def normal_parts(u):
    size = jnp.abs(u)
    t = 1.0 / (1.0 + (0.3275911 * ROOT_HALF) * size)
    expo = jnp.exp(-0.5 * (u * u))
    poly = t * (
        0.5 * 0.254829592
        + t
        * (
            -0.5 * 0.284496736
            + t * (0.5 * 1.421413741 + t * (-0.5 * 1.453152027 + t * (0.5 * 1.061405429)))
        )
    )
    tail = poly * expo
    return jnp.where(u >= 0.0, 1.0 - tail, tail), expo


def norm_stats(rows):
    mean = jnp.mean(rows, axis=1, keepdims=True)
    centered = rows - mean
    spread = jnp.mean(centered * centered, axis=1, keepdims=True)
    inverse = lax.rsqrt(spread + NORM_EPS)
    return centered * inverse, inverse


def norm_back(d_rows, normal, inverse):
    mean_d = jnp.mean(d_rows, axis=1, keepdims=True)
    mean_dn = jnp.mean(d_rows * normal, axis=1, keepdims=True)
    return inverse * (d_rows - mean_d - normal * mean_dn)


def fill_ffn_matrices(w_out, w_up, w_down, packing, refs, core):
    side = D // BLK
    for base, offset, ref in each_piece(packing, refs, core):
        blocks, rows = ref.shape[:2]
        for n in range(blocks):
            full, i, j = ffn_place(base + n, (w_out, w_up, w_down))
            full[pl.ds(BLK * i + offset, rows), BLK * j : BLK * (j + 1)] = ref[n]


def ffn_place(b, matrices):
    side = D // BLK
    if b < side * side:
        return matrices[0], b // side, b % side
    b -= side * side
    if b < side * FF_CHUNKS:
        return matrices[1], b // FF_CHUNKS, b % FF_CHUNKS
    b -= side * FF_CHUNKS
    return matrices[2], b // side, b % side


def ffn_kernel(packing, wins, tokens, part, split, pieces, meta, *refs):
    cot_ref, x_ref, o_ref, vec = refs[:4]
    weight_refs = refs[4 : 4 + (2 * len(packing) or 1)]
    refs = refs[4 + len(weight_refs) :]
    out_refs, refs = refs[:pieces], refs[pieces:]
    da_ref, do_ref = refs[:2]
    refs = refs[2:]
    dw_refs, refs = refs[: 2 if split else 1], refs[2 if split else 1 :]
    vg_ref, w_out, w_up, w_down, acc_out, acc_up, acc_down, z_ref, gp_ref, du_ref, buf = refs
    step = pl.program_id(0)
    length = meta[step]
    accs = (acc_out, acc_up, acc_down)

    def acc_block(b, offset, rows):
        full, i, j = ffn_place(b, accs)
        if full is acc_down:
            i, j = j, i
        return full.at[pl.ds(BLK * i + offset, rows), BLK * j : BLK * (j + 1)]

    @pl.when(step == 0)
    def _():
        fill_ffn_matrices(w_out, w_up, w_down, packing, weight_refs, meta[wins])
        for acc in accs:
            acc[...] = jnp.zeros_like(acc)
        vg_ref[...] = jnp.zeros_like(vg_ref)

    def add_row(row, values, at=0):
        vg_ref[row : row + 1, at : at + values.shape[1]] += jnp.sum(
            values.astype(F32), axis=0, keepdims=True
        )

    bias_out, bias_down = vec[2:3, :], vec[7:8, :]
    gain_one, shift_one = vec[8:9, :], vec[9:10, :]
    gain_two, shift_two = vec[10:11, :], vec[11:12, :]
    attended = o_ref[0]
    mixed = x_ref[:, 0].reshape(WIN, D).astype(F32) + (dot_nn(attended, w_out[...]) + bias_out)
    n_one, inv_one = norm_stats(mixed)
    normed = n_one * gain_one + shift_one
    normed_low = normed.astype(BF16)
    for c in range(FF // D):
        cols = slice(D * c, D * (c + 1))
        u = dot_nn(normed_low, w_up[:, cols]) + vec[3 + c : 4 + c, :]
        phi, expo = normal_parts(u)
        z_ref[:, cols] = (u * phi).astype(BF16)
        gp_ref[:, cols] = phi + (u * expo) * DENSITY
    summed = normed + (dot_nn(z_ref[...], w_down[...]) + bias_down)
    n_two, inv_two = norm_stats(summed)
    result = (n_two * gain_two + shift_two).astype(BF16)
    if pieces == 1:
        out_ref = out_refs[0]
        out_ref[:, 0] = result.reshape(out_ref.shape[0], out_ref.shape[2], D)
    else:
        buf[...] = result
        for s, out_ref in enumerate(out_refs):
            rows = out_ref.shape[1]
            at = pl.multiple_of((meta[wins + 1] ^ s) * rows, rows)
            out_ref[0] = buf[pl.ds(at, rows), :]

    places = lax.broadcasted_iota(jnp.int32, (WIN, 1), 0)
    valid = jnp.where(places < length, 1.0 / tokens, 0.0).astype(F32)
    seed = cot_ref[:, 0].reshape(WIN, D).astype(F32) * valid
    add_row(10, seed * n_two)
    add_row(11, seed)
    d_summed = norm_back(seed * gain_two, n_two, inv_two)
    d_ff = d_summed.astype(BF16)
    add_row(7, d_ff)
    for c in range(FF // D):
        cols = slice(D * c, D * (c + 1))
        d_z = dot_nt(d_ff, w_down[cols, :])
        d_u = (d_z * gp_ref[:, cols]).astype(BF16)
        add_row(3 + c, d_u)
        du_ref[:, cols] = d_u
    d_ff_t = jnp.transpose(d_ff)
    normed_t = jnp.transpose(normed_low)
    for c in range(FF // D):
        cols = slice(D * c, D * (c + 1))
        acc_down[:, cols] += dot_nn(d_ff_t, z_ref[:, cols])
        acc_up[:, cols] += dot_nn(normed_t, du_ref[:, cols])
    d_normed = d_summed + dot_nt(du_ref[...], w_up[...])
    add_row(8, d_normed * n_one)
    add_row(9, d_normed)
    d_mixed = norm_back(d_normed * gain_one, n_one, inv_one)
    da_ref[0] = d_mixed
    d_branch = d_mixed.astype(BF16)
    add_row(2, d_branch)
    acc_out[...] += dot_nn(jnp.transpose(attended), d_branch)
    do_ref[0] = dot_nt(d_branch, w_out[...]).astype(BF16)

    @pl.when(step == pl.num_programs(0) - 1)
    def _():
        for j in range(D // BLK):
            for i in range(FF_CHUNKS):
                at = (slice(BLK * j, BLK * (j + 1)), slice(BLK * i, BLK * (i + 1)))
                acc_down[at] = jnp.transpose(acc_down[at])
        write_gradient(
            lambda b, offset, rows: acc_block(b, offset, rows)[...],
            REST_BLOCKS, part, meta[wins], dw_refs,
        )


def whole_spec(shape):
    zeros = (0,) * len(shape)
    return pl.BlockSpec(shape, lambda w, m: zeros, pipeline_mode=pl.Buffered(1))


def blocks_spec(part, count, at):
    lead = part.ndim - 3
    shape = part.shape[:lead] + (count,) + part.shape[lead + 1 :]
    return pl.BlockSpec(
        shape, lambda w, m: (0,) * lead + (at, 0, 0), pipeline_mode=pl.Buffered(1)
    )


def total_spec(shape):
    zeros = (0,) * len(shape)
    return pl.BlockSpec(shape, lambda w, m: zeros)


def window_spec(begin, *shape):
    zeros = (0,) * len(shape)
    return pl.BlockSpec((1,) + shape, lambda w, m: (begin + w,) + zeros)


def segment_spec(dp, seg):
    return pl.BlockSpec((dp, 1, seg, D), lambda w, m: (0, w, 0, 0))


def input_spec(dp, seg, begin):
    return pl.BlockSpec((dp, 1, seg, D), lambda w, m: (0, begin + w, 0, 0))


def gradient_outs(blocks, part):
    if part % 16:
        return [jax.ShapeDtypeStruct((blocks, BLK, BLK), BF16)]
    return [jax.ShapeDtypeStruct((blocks, BLK // 2, BLK), BF16)] * 2


def run_kernel(kernel, wins, meta, ins, outs, scratch, flops, moved):
    return pl.pallas_call(
        kernel,
        grid_spec=pltpu.PrefetchScalarGridSpec(
            num_scalar_prefetch=1,
            grid=(wins,),
            in_specs=[spec for _, spec in ins],
            out_specs=[spec for _, spec in outs],
            scratch_shapes=scratch,
        ),
        out_shape=[shape for shape, _ in outs],
        compiler_params=pltpu.CompilerParams(
            dimension_semantics=("arbitrary",), vmem_limit_bytes=56 * 1024 * 1024
        ),
        cost_estimate=pl.CostEstimate(
            flops=flops, bytes_accessed=moved, transcendentals=wins * WIN * FF
        ),
    )(meta, *[values for values, _ in ins])


def call_attention(wins, meta, x, packing, weight_parts, bias):
    dp, _, seg, _ = x.shape
    shape = jax.ShapeDtypeStruct
    return run_kernel(
        functools.partial(attention_kernel, packing, wins),
        wins,
        meta,
        [(x, input_spec(dp, seg, 0)), (bias, whole_spec(bias.shape))]
        + [(piece, whole_spec(piece.shape)) for piece in weight_parts],
        [
            (shape((wins, WIN, 3 * D), BF16), window_spec(0, WIN, 3 * D)),
            (shape((wins, WIN, D), BF16), window_spec(0, WIN, D)),
            (shape((wins, HEADS, WIN), F32), window_spec(0, HEADS, WIN)),
        ],
        [pltpu.VMEM((D, 3 * D), BF16), pltpu.VMEM((WIN, WIN), F32)],
        wins * 250_000_000,
        wins * 1_000_000,
    )


def call_ffn(wins, tokens, part, apart, meta, x, attended, packing, weight_parts, vec):
    dp, _, seg, _ = x.shape
    shape = jax.ShapeDtypeStruct
    counts = (QKV_BLOCKS, QKV_BLOCKS, 2 * QKV_BLOCKS, 2 * QKV_BLOCKS)
    ins = [
        (x, input_spec(dp, seg, wins)),
        (x, input_spec(dp, seg, 0)),
        (attended, window_spec(0, WIN, D)),
        (vec, whole_spec(vec.shape)),
    ] + [
        (piece, blocks_spec(piece, count, 0) if packing else whole_spec(piece.shape))
        for piece, count in zip(weight_parts, counts)
    ]
    outs = [(shape((dp, wins, seg, D), BF16), segment_spec(dp, seg))]
    if apart:
        outs = [(shape((wins, seg, D), BF16), window_spec(0, seg, D))] * dp
    return run_kernel(
        functools.partial(ffn_kernel, packing, wins, tokens, part, part % 16 == 0, dp if apart else 1),
        wins,
        meta,
        ins,
        [
            *outs,
            (shape((wins, WIN, D), F32), window_spec(0, WIN, D)),
            (shape((wins, WIN, D), BF16), window_spec(0, WIN, D)),
        ]
        + [(out, total_spec(out.shape)) for out in gradient_outs(REST_BLOCKS, part)]
        + [(shape((ROWS_VEC, D), F32), total_spec((ROWS_VEC, D)))],
        [
            pltpu.VMEM((D, D), BF16),
            pltpu.VMEM((D, FF), BF16),
            pltpu.VMEM((FF, D), BF16),
            pltpu.VMEM((D, D), F32),
            pltpu.VMEM((D, FF), F32),
            pltpu.VMEM((D, FF), F32),
            pltpu.VMEM((WIN, FF), BF16),
            pltpu.VMEM((WIN, FF), F32),
            pltpu.VMEM((WIN, FF), BF16),
            pltpu.VMEM((WIN, D), BF16),
        ],
        wins * 250_000_000,
        wins * 1_000_000,
    )


def call_attention_back(
    part, meta, packing, weight_parts, x, qkv, d_o, lse, d_mixed
):
    dp, _, seg, _ = x.shape
    wins = d_o.shape[0]
    shape = jax.ShapeDtypeStruct
    return run_kernel(
        functools.partial(attention_back_kernel, packing, wins, part, part % 16 == 0),
        wins,
        meta,
        [
            (x, input_spec(dp, seg, 0)),
            (qkv, window_spec(0, WIN, 3 * D)),
            (d_o, window_spec(0, WIN, D)),
            (lse, window_spec(0, HEADS, WIN)),
            (d_mixed, window_spec(0, WIN, D)),
        ]
        + [(piece, whole_spec(piece.shape)) for piece in weight_parts],
        [(shape((dp, wins, seg, D), BF16), segment_spec(dp, seg))]
        + [(out, total_spec(out.shape)) for out in gradient_outs(QKV_BLOCKS, part)]
        + [(shape((8, D), F32), total_spec((8, D)))],
        [
            pltpu.VMEM((D, 3 * D), BF16),
            pltpu.VMEM((WIN, WIN), F32),
            pltpu.VMEM((WIN, 3 * D), BF16),
            pltpu.VMEM((D, 3 * D), F32),
        ],
        wins * 12_500_000_000,
        wins * 8_000_000,
    )


def split_first_kernel(terms, bits, *refs):
    ins, outs = refs[:terms], refs[terms:]

    def total(side, at):
        return sum(ref[side, :, at].astype(F32) for ref in ins).astype(BF16)

    for y in range(2):
        for which in range(2):
            outs[which][:, y] = total(0, 2 * y + (bits[0] if which == 0 else 1 - bits[0]))
    for x in range(2):
        for which in range(2):
            outs[2 + which][:, x] = total(1, 2 * (bits[1] if which == 0 else 1 - bits[1]) + x)


def split_second_kernel(bits, *refs):
    for side in range(2):
        mine, got = refs[2 * side : 2 * side + 2]
        for which in range(2):
            bit = bits[1 - side]
            at = bit if which == 0 else 1 - bit
            refs[4 + 2 * side + which][...] = (
                mine[:, at].astype(F32) + got[:, at].astype(F32)
            ).astype(BF16)


def slabs_kernel(dp, me_ref, *refs):
    pairs, vec, outs, total = refs[: len(refs) - dp - 2], refs[-dp - 2], refs[-dp - 1 : -1], refs[-1]
    base = 0
    for n in range(0, len(pairs), 2):
        blocks = pairs[n].shape[0]
        total[base : base + blocks] = pairs[n][...].astype(F32) + pairs[n + 1][...].astype(F32)
        base += blocks
    owned = outs[0].shape[0] - 1
    for s in range(dp):
        slab = total[pl.ds((me_ref[0] ^ s) * owned, owned)]
        outs[s][:owned] = slab.astype(outs[s].dtype)
        outs[s][owned] = vec[...].astype(BF16).astype(outs[s].dtype)


def update_kernel(packing, scalars, *refs):
    count = 2 * len(packing)
    parts, root_parts, refs = refs[:count], refs[count : 2 * count], refs[2 * count :]
    own, left_stats, right_stats, left_roots, weights = refs[:5]
    left_new, right_new, weights_new, full, roots = refs[5:]
    fill_stack(full, packing, parts, scalars[0])
    fill_stack(roots, packing, root_parts, scalars[0])
    blocks, rows, _ = own.shape
    at = scalars[1] * rows
    lane = lax.broadcasted_iota(jnp.int32, (rows, BLK), 1)
    line = lax.broadcasted_iota(jnp.int32, (rows, BLK), 0)
    pick = jnp.where(lane == line + at, 1.0, 0.0).astype(BF16)
    for b in range(blocks):
        whole = full[b]
        crossed = dot_nt(jnp.concatenate([own[b], pick], axis=0), whole)
        left_new[b] = DECAY * left_stats[b] + (1.0 - DECAY) * crossed[:rows]
        turned = jnp.concatenate([left_roots[b].astype(BF16), crossed[rows:].astype(BF16)], axis=0)
        passed = dot_nn(turned, whole)
        right_new[b] = DECAY * right_stats[b] + (1.0 - DECAY) * passed[rows:]
        step = dot_nn(passed[:rows].astype(BF16), roots[b])
        weights_new[b] = weights[b] - MATRIX_RATE * step


def call_small(kernel, steps, scalars, ins, outs, scratch=(), room=14):
    def spec(shape, axis):
        if isinstance(axis, pl.BlockSpec):
            return axis
        block = tuple(n // steps if d == axis else n for d, n in enumerate(shape))
        return pl.BlockSpec(block, lambda g, m: tuple(g if d == axis else 0 for d in range(len(shape))))

    return pl.pallas_call(
        kernel,
        grid_spec=pltpu.PrefetchScalarGridSpec(
            num_scalar_prefetch=1,
            grid=(steps,),
            in_specs=[spec(values.shape, axis) for values, axis in ins],
            out_specs=[spec(shape.shape, axis) for shape, axis in outs],
            scratch_shapes=list(scratch),
        ),
        out_shape=[shape for shape, _ in outs],
        compiler_params=pltpu.CompilerParams(
            dimension_semantics=("arbitrary",), vmem_limit_bytes=room * 1024 * 1024
        ),
    )(scalars, *[values for values, _ in ins])


def update_blocks(scalars, packing, parts, root_parts, own, *shards):
    blocks = own.shape[0]
    out = jax.ShapeDtypeStruct(own.shape, F32)
    share = blocks // 2
    ats = (QKV_BLOCKS // share, QKV_BLOCKS // share, 2 * QKV_BLOCKS // share, 2 * QKV_BLOCKS // share)
    return call_small(
        functools.partial(update_kernel, packing),
        1,
        scalars,
        [(part, None) for part in parts]
        + [(part, blocks_spec(part, share, at)) for part, at in zip(root_parts, ats)]
        + [(values, None) for values in (own, *shards)],
        [(out, None)] * 3,
        [pltpu.VMEM((blocks, BLK, BLK), BF16)] * 2,
        24,
    )


def split_first(bits, *terms):
    blocks, height, cols = terms[0].shape
    half = blocks // 2
    view = (2, half, 4, height // 4, cols)
    out = jax.ShapeDtypeStruct((half, 2, height // 4, cols), BF16)
    return call_small(
        functools.partial(split_first_kernel, len(terms)),
        max(half // 6, 1),
        bits,
        [(term.reshape(view), 1) for term in terms],
        [(out, 0)] * 4,
    )


def split_second(bits, *parts):
    half, _, rows, cols = parts[0].shape
    out = jax.ShapeDtypeStruct((half, rows, cols), BF16)
    return call_small(
        split_second_kernel, 1, bits, [(part, 0) for part in parts], [(out, 0)] * 4
    )


def make_slabs(dp, me, parts, vec):
    _, rows, cols = parts[0].shape
    blocks = sum(part.shape[0] for part in parts) // 2
    shape = (blocks // dp + 1, rows, cols)
    return call_small(
        functools.partial(slabs_kernel, dp),
        1,
        me,
        [(part, None) for part in [*parts, vec]],
        [(jax.ShapeDtypeStruct(shape, F32 if s == 0 else BF16), None) for s in range(dp)],
        [pltpu.VMEM((blocks, rows, cols), F32)],
    )


def swap(values, axis, size, k):
    return lax.ppermute(values, axis, [(i, i ^ k) for i in range(size)])


def bits_of(size):
    return [1 << i for i in range(size.bit_length() - 1)]


def hop_orders(seq_count):
    high = [k for k in bits_of(seq_count) if k > 1]
    return (high, high[::-1])


def gather_hop(state, k, seq_count, seq_index, *marks):
    cur, lead = state
    got = after(swap(cur, "seq", seq_count, k), *marks)
    odd = (seq_index & k) != 0
    cur = jnp.stack([jnp.where(odd, got, cur), jnp.where(odd, cur, got)], axis=0)
    return cur, [k] + lead


def gather_end(state):
    cur, lead = state
    count = len(lead)
    blocks, rows, cols = cur.shape[count:]
    axes = [count] + [lead.index(k) for k in sorted(lead, reverse=True)] + [count + 1, count + 2]
    return cur.transpose(axes).reshape(blocks, rows << count, cols)


def halves(cur):
    half = cur.shape[0] // 2
    return [cur[:half], cur[half:]]


def gather_split(cur, seq_count, seq_index):
    done = []
    for part, order in zip(halves(cur), hop_orders(seq_count)):
        state = (part, [])
        for k in order + [1]:
            state = gather_hop(state, k, seq_count, seq_index)
        done.append(gather_end(state))
    return jnp.concatenate(done, axis=0)


def pack_weights(rows, roots, orders, seq_count, seq_index):
    states = [
        (jnp.concatenate(pair, axis=0), []) for pair in zip(halves(rows), halves(roots))
    ]
    for step in range(len(orders[0])):
        states = [
            gather_hop(state, order[step], seq_count, seq_index)
            for state, order in zip(states, orders)
        ]
        if step == 0:
            cur, lead = states[0]
            axis = len(lead)
            states = [
                (lax.slice_in_dim(cur, 0, QKV_BLOCKS, axis=axis), lead),
                (lax.slice_in_dim(cur, QKV_BLOCKS, cur.shape[axis], axis=axis), lead),
                states[1],
            ]
            orders = (orders[0], orders[0], orders[1])
    return states


def join_cores(states, seq_count, seq_index, *marks):
    if states[0][0].shape[-2] % 16:
        states = [gather_hop(state, 1, seq_count, seq_index) for state in states]
        return (), [jnp.concatenate([gather_end(state) for state in states], axis=0)]
    parts = []
    for cur, _ in states:
        parts += [cur, after(swap(cur, "seq", seq_count, 1), *marks)]
    return tuple(tuple(lead) for _, lead in states), parts


def scatter_first(whole, seq_count, seq_index):
    left = sorted(bits_of(seq_count), reverse=True)
    blocks, height, cols = whole.shape
    rows = height // seq_count
    cur = whole.reshape(blocks, seq_count // 2, 2, rows, cols)
    mine, other = [
        lax.dynamic_index_in_dim(cur, bit, 2, keepdims=False)
        for bit in (seq_index % 2, 1 - seq_index % 2)
    ]
    cur = mine.astype(F32) + swap(other, "seq", seq_count, 1).astype(F32)
    left.remove(1)
    cur = cur.astype(BF16).reshape([blocks] + [2] * len(left) + [rows, cols])
    return [(half, left) for half in halves(cur)]


def scatter_hop(state, k, seq_count, seq_index, *marks):
    cur, left = state
    axis = 1 + left.index(k)
    bit = (seq_index // k) % 2
    mine = lax.dynamic_index_in_dim(cur, bit, axis, keepdims=False)
    other = lax.dynamic_index_in_dim(cur, 1 - bit, axis, keepdims=False)
    got = after(swap(other, "seq", seq_count, k), *marks)
    cur = (mine.astype(F32) + got.astype(F32)).astype(BF16)
    return cur, [b for b in left if b != k]


def after(values, *marks):
    if not marks:
        return values
    return lax.optimization_barrier((values, marks))[0]


def body(
    inputs,
    cotangent,
    lengths,
    weights,
    vectors,
    positions,
    left_stats,
    right_stats,
    left_roots,
    right_roots,
    vector_second,
    position_second,
):
    seq_count = lax.axis_size("seq")
    dp_count = lax.axis_size("dp")
    seq_index = lax.axis_index("seq")
    dp_index = lax.axis_index("dp")
    micro, wins_dev, segment, model_width = inputs.shape
    wins = wins_dev // dp_count
    total_tokens = micro * wins_dev * seq_count * segment * dp_count
    owned, row_part, _ = weights.shape
    def exchange(rows):
        return lax.all_to_all(rows, "dp", 0, 0, tiled=True)

    grouped = (dp_count, wins, segment, model_width)
    own = weights.astype(BF16)
    orders = hop_orders(seq_count)
    hops = len(orders[0])

    def scatter_both(states, step, *marks):
        return [
            scatter_hop(state, order[step], seq_count, seq_index, *marks)
            for state, order in zip(states, orders)
        ]

    vec = vectors.reshape(-1, D)
    bias_qv = jnp.concatenate([vec[0:2], jnp.zeros((6, D), F32)], axis=0)
    vec_pad = jnp.concatenate([vec, jnp.zeros((ROWS_VEC - vec.shape[0], D), F32)], axis=0)

    metas = [
        lax.dynamic_index_in_dim(
            lengths[i].reshape(dp_count, wins), dp_index, 0, keepdims=False
        )
        for i in range(micro)
    ]
    metas = [
        jnp.concatenate([lens, (seq_index % 2)[None], dp_index[None]]).astype(jnp.int32)
        for lens in metas
    ]
    shards = [own] + [swap(own, "dp", dp_count, s) for s in range(1, dp_count)]
    weight_rows = jnp.concatenate(
        [lax.select_n(dp_index ^ j, *shards) for j in range(dp_count)], axis=0
    )
    pairs = [
        jnp.concatenate(
            [
                (inputs[i].astype(F32) + positions[None]).astype(BF16).reshape(grouped),
                cotangent[i].reshape(grouped),
            ],
            axis=1,
        )
        for i in range(micro)
    ]
    taken = [exchange(after(pairs[0], *shards[1:]))]
    roots_low = right_roots.astype(BF16)
    groups = pack_weights(weight_rows, roots_low, orders, seq_count, seq_index)
    cur, lead = groups[0]
    groups[0] = (after(cur, vec_pad, bias_qv, roots_low, *metas), lead)
    packing_qkv, parts_qkv = join_cores(groups[:1], seq_count, seq_index)
    for i in range(1, micro):
        marks = (taken[-1], *metas, *parts_qkv, *(cur for cur, _ in groups[1:]))
        taken.append(exchange(after(pairs[i], *marks)))
    ffn, out_got, dx_got = [], [], []
    forward = [
        call_attention(wins, metas[0], taken[0], packing_qkv, parts_qkv, bias_qv)
    ]
    mark = (forward[0][2],)
    lse = forward[0][2]
    packing_rest, parts_rest = join_cores(groups[1:], seq_count, seq_index, lse)
    share = owned // 2
    if not packing_rest:
        (stack,) = parts_rest
        middle = QKV_BLOCKS + share
        roots_full = jnp.concatenate([stack[QKV_BLOCKS:middle], stack[-share:]], axis=0)
        parts_rest = [jnp.concatenate([stack[:QKV_BLOCKS], stack[middle:-share]], axis=0)]
    fast = seq_count == 8 and row_part % 16 == 0
    bits = jnp.stack([(seq_index // 2) % 2, (seq_index // 4) % 2]).astype(jnp.int32)

    def over_cores(parts, *marks):
        keep, send = parts
        return [keep, after(swap(send, "seq", seq_count, 1), *marks)]

    def hop(parts, count, *marks):
        mine_a, send_a, mine_b, send_b = parts
        k_a, k_b = (2, 4) if count == 0 else (4, 2)
        got_a = after(swap(send_a, "seq", seq_count, k_a), *marks)
        got_b = after(swap(send_b, "seq", seq_count, k_b), *marks)
        return [mine_a, got_a, mine_b, got_b]

    vec_sums = jnp.zeros((ROWS_VEC, D), F32)
    dw_rest, dw_qkv = [], []
    for i in range(micro):
        if i > 0:
            forward.append(
                call_attention(
                    wins, after(metas[i], *mark), taken[i], packing_qkv, parts_qkv, bias_qv
                )
            )
            mark = (forward[i][2],)
        results = call_ffn(
            wins, total_tokens, row_part, True, after(metas[i], *mark), taken[i], forward[i][1],
            packing_rest, parts_rest, vec_pad,
        )
        out, (d_mixed, d_o, *dw, vg) = results[:dp_count], results[dp_count:]
        got = [out[0]] + [swap(out[s], "dp", dp_count, s) for s in range(1, dp_count)]
        out_got.append(tuple(got))
        ffn.append((d_mixed, d_o))
        vec_sums = vec_sums + vg
        mark = (vg,)
        dw_rest.append(dw)
    gates = mark + (out_got[0],)
    rest_core, qkv_core = [], []
    for i in range(micro):
        dx, *dw, db = call_attention_back(
            row_part, after(metas[i], gates), packing_qkv, parts_qkv, taken[i], forward[i][0],
            ffn[i][1], forward[i][2], ffn[i][0],
        )
        vec_sums = vec_sums + jnp.concatenate([db, jnp.zeros_like(db)], axis=0)
        dw_qkv.append(dw)
        gates = (db,) + tuple(out_got[1:])
        if fast and i == 0:
            for n in range(micro):
                rest_core += over_cores(dw_rest[n], *(mark[:1] if n == 0 else (db,)))
            rest = split_first(bits, *rest_core)
            gates = gates + tuple(rest)
        if fast and i == micro - 1:
            rest = hop(rest, 0, db)
            qkv_core += over_cores(dw_qkv[0], db)
            dx = after(dx, *rest)
        dx_got.append(exchange(after(dx, *dx_got[-1:])))

    whole = (wins_dev, segment, model_width)
    out_got = [
        jnp.stack([lax.select_n(dp_index ^ e, *got) for e in range(dp_count)]) for got in out_got
    ]
    layer_out = jnp.stack([got.reshape(whole) for got in out_got], axis=0)

    for k in bits_of(seq_count):
        vec_sums = vec_sums + swap(vec_sums, "seq", seq_count, k)
    if fast:
        qkv_core += over_cores(dw_qkv[1])
        rest = split_second(bits, *rest)
        states = split_first(after(bits, *rest), *qkv_core)
        rest = hop(rest, 1)
        states = hop(split_second(bits, *hop(states, 0)), 1)
        slabs = make_slabs(
            dp_count, after(dp_index[None].astype(jnp.int32), dx_got[-1], layer_out), states + rest,
            vec_sums.reshape(row_part, BLK),
        )
    else:
        states = []
        for parts in (dw_qkv, dw_rest):
            total = sum(part[0].astype(F32) for part in parts).astype(BF16)
            group = scatter_first(total, seq_count, seq_index)
            for step in range(hops):
                group = scatter_both(group, step)
            states += group
        joined = jnp.concatenate([cur for cur, _ in states], axis=0)
        joined = joined.reshape((dp_count, owned) + joined.shape[1:])
        vec_rows = vec_sums.astype(BF16).reshape(-1, row_part, BLK)
        slabs = [
            jnp.concatenate(
                [lax.dynamic_index_in_dim(joined, dp_index ^ s, 0, keepdims=False), vec_rows]
            )
            for s in range(dp_count)
        ]
    slabs = [slabs[0].astype(F32)] + [
        swap(slabs[s], "dp", dp_count, s).astype(F32) for s in range(1, dp_count)
    ]
    grad_rows = sum(slab[:owned] for slab in slabs)
    vec_sums = sum(lax.select_n(dp_index ^ j, *[slab[owned:] for slab in slabs]) for j in range(dp_count))
    vec_sums = vec_sums.reshape(ROWS_VEC, D)
    grad_low = grad_rows.astype(BF16)
    if fast:
        states = [(part, []) for part in halves(grad_low)]
        for step in range(hops):
            states = [
                gather_hop(state, order[step], seq_count, seq_index)
                for state, order in zip(states, orders)
            ]
        packing, parts = join_cores(states, seq_count, seq_index)
        left_new, right_new, weights_new = update_blocks(
            jnp.stack([seq_index % 2, seq_index]).astype(jnp.int32), packing, parts, parts_rest,
            grad_low, left_stats, right_stats, left_roots, weights,
        )
    else:
        grad_full = gather_split(grad_low, seq_count, seq_index)
        row_start = seq_index * row_part

        def batched(spec, left, right):
            return jnp.einsum(spec, left, right, preferred_element_type=F32)

        left_new = DECAY * left_stats + (1.0 - DECAY) * batched("bij,bkj->bik", grad_low, grad_full)
        column_part = lax.dynamic_slice_in_dim(grad_full, row_start, row_part, 2)
        right_new = DECAY * right_stats + (1.0 - DECAY) * batched(
            "bki,bkj->bij", column_part, grad_full
        )
        left_applied = batched("bij,bjk->bik", left_roots.astype(BF16), grad_full)
        step_rows = batched("bij,bjk->bik", left_applied.astype(BF16), roots_full)
        weights_new = weights - MATRIX_RATE * step_rows

    place_sum = sum(jnp.sum(got.astype(F32), axis=(0, 1)) for got in dx_got)
    for k in bits_of(seq_count):
        low = place_sum.astype(BF16)
        place_sum = low.astype(F32) + swap(low, "seq", seq_count, k).astype(F32)
    vector_grads = vec_sums[: vec.shape[0]].reshape(-1)
    vector_second_new = DECAY * vector_second + (1.0 - DECAY) * vector_grads * vector_grads
    vectors_new = vectors - VECTOR_RATE * vector_grads / (jnp.sqrt(vector_second_new) + ROOT_EPS)
    position_grads = place_sum
    position_second_new = DECAY * position_second + (1.0 - DECAY) * position_grads * position_grads
    positions_new = positions - VECTOR_RATE * position_grads / (
        jnp.sqrt(position_second_new) + ROOT_EPS
    )
    return (
        layer_out,
        jnp.stack([got.astype(F32).reshape(whole) for got in dx_got], axis=0),
        grad_rows,
        left_new,
        right_new,
        weights_new,
        vector_grads,
        vector_second_new,
        vectors_new,
        position_grads,
        position_second_new,
        positions_new,
    )


def solution(mesh):
    rows = P(None, "seq", "dp", None)
    blocks = P("dp", "seq", None)
    in_specs = (
        rows, rows, P(None, "seq"), blocks, P(), P("dp", None),
        blocks, blocks, blocks, blocks, P(), P("dp", None),
    )
    out_specs = (
        rows, rows, blocks, blocks, blocks, blocks,
        P(), P(), P(), P("dp", None), P("dp", None), P("dp", None),
    )
    return jax.shard_map(body, mesh=mesh, in_specs=in_specs, out_specs=out_specs, check_vma=False)
```

```python
import functools
import itertools

import jax
import jax.numpy as jnp
from jax import lax
from jax.experimental import pallas as pl
from jax.experimental.pallas import tpu as pltpu
from jax.sharding import PartitionSpec as P

HEADS = 8
FF = 2048
WIN = 512
D = 512
BLK = 256
QKV_BLOCKS = 12
REST_BLOCKS = 36
HEAD_DIM = D // HEADS
PAIR = 2 * HEAD_DIM
PAIRS = HEADS // 2
FF_CHUNKS = FF // BLK
ROWS_VEC = 16
GROUP = 2

NORM_EPS = 1e-05
ROOT_EPS = 1e-08
DECAY = 0.5
MATRIX_RATE = 0.5
VECTOR_RATE = 0.2
MASKED = -1e30
SCALE = HEAD_DIM ** (-0.5)
ROOT_HALF = 0.7071067811865476
DENSITY = 0.3989422804014327

F32 = jnp.float32
BF16 = jnp.bfloat16


def dot_nn(left, right):
    return lax.dot_general(left, right, (((1,), (0,)), ((), ())), preferred_element_type=F32)


def dot_nt(left, right):
    return lax.dot_general(left, right, (((1,), (1,)), ((), ())), preferred_element_type=F32)


def each_piece(packing, refs, core):
    if not packing:
        yield 0, 0, refs[0]
        return
    base = 0
    for side, bits in enumerate(packing):
        for which in range(2):
            ref = refs[2 * side + which]
            blocks, rows = ref.shape[len(bits)], ref.shape[len(bits) + 1]
            last = core if which == 0 else 1 - core
            for at in itertools.product(range(2), repeat=len(bits)):
                first = sum(k * v for k, v in zip(bits, at))
                yield base, pl.multiple_of((first + last) * rows, rows), ref.at[at]
        base += blocks


def fill_qkv_matrix(full, packing, refs, core):
    side = D // BLK
    for base, offset, ref in each_piece(packing, refs, core):
        blocks, rows = ref.shape[:2]
        for n in range(blocks):
            b = base + n
            m, i, j = b // (side * side), (b // side) % side, b % side
            cols = slice(D * m + BLK * j, D * m + BLK * (j + 1))
            full[pl.ds(BLK * i + offset, rows), cols] = ref[n]


def fill_stack(stack, packing, refs, core):
    for base, offset, ref in each_piece(packing, refs, core):
        blocks, rows = ref.shape[:2]
        for n in range(blocks):
            stack[base + n, pl.ds(offset, rows), :] = ref[n]


def write_gradient(block_at, blocks, rows, core, outs):
    for b in range(blocks):
        if len(outs) == 1:
            outs[0][b] = block_at(b, 0, BLK).astype(BF16)
            continue
        for which, out in enumerate(outs):
            last = core if which == 0 else 1 - core
            for n in range(BLK // (2 * rows)):
                offset = pl.multiple_of((2 * n + last) * rows, rows)
                out[b, n * rows : (n + 1) * rows, :] = block_at(b, offset, rows).astype(BF16)


def fill_mask(mask, length):
    for i in range(WIN // BLK):
        keys = lax.broadcasted_iota(jnp.int32, (BLK, WIN), 0) + BLK * i
        queries = lax.broadcasted_iota(jnp.int32, (BLK, WIN), 1)
        keep = (keys <= queries) & (keys < length)
        mask[BLK * i : BLK * (i + 1), :] = jnp.where(keep, 0.0, MASKED).astype(F32)


def half_marks():
    lane = lax.broadcasted_iota(jnp.int32, (1, PAIR), 1)
    low = jnp.where(lane < HEAD_DIM, 1.0, 0.0)
    return (low.astype(BF16), (1.0 - low).astype(BF16))


def attention_kernel(packing, wins, meta, x_ref, bias, *refs):
    weight_refs = refs[: 2 * len(packing) or 1]
    qkv_ref, o_ref, lse_ref, full, mask = refs[len(weight_refs) :]
    step = pl.program_id(0)

    @pl.when(step == 0)
    def _():
        fill_qkv_matrix(full, packing, weight_refs, meta[wins])

    hidden = x_ref[:, 0].reshape(WIN, D)
    for m in range(3):
        cols = slice(D * m, D * (m + 1))
        rows = dot_nn(hidden, full[:, cols])
        if m != 1:
            rows = rows + bias[(m // 2) : (m // 2) + 1, :]
        qkv_ref[0, :, cols] = rows.astype(BF16)
    fill_mask(mask, meta[step])
    marks = half_marks()
    half = WIN // BLK
    for group in range(0, PAIRS, GROUP):
        cases, scores, probs = [], [], []
        for p in range(group, group + GROUP):
            at = PAIR * p
            q8 = qkv_ref[0, :, at : at + PAIR] * jnp.asarray(SCALE, BF16)
            key = qkv_ref[0, :, D + at : D + at + PAIR]
            for h in range(2):
                key_h = key * marks[h]
                for qb in range(half):
                    cols, span = slice(BLK * qb, BLK * (qb + 1)), BLK * (qb + 1)
                    cases.append((2 * p + h, qb))
                    scores.append(dot_nt(key_h[:span], q8[cols]) + mask[:span, cols])
        for (row, qb), s_t in zip(cases, scores):
            cols = slice(BLK * qb, BLK * (qb + 1))
            top = jnp.max(s_t, axis=0, keepdims=True)
            expo = jnp.exp(s_t - top)
            total = jnp.sum(expo, axis=0, keepdims=True)
            probs.append((expo * (1.0 / total)).astype(BF16))
            lse_ref[0, row : row + 1, cols] = top + jnp.log(total)
        for n, p in enumerate(range(group, group + GROUP)):
            at = PAIR * p
            val_t = jnp.transpose(qkv_ref[0, :, 2 * D + at : 2 * D + at + PAIR])
            pieces = []
            for h in range(2):
                rows = slice(HEAD_DIM * h, HEAD_DIM * (h + 1))
                first = (2 * n + h) * half
                pieces.append(
                    jnp.concatenate(
                        [
                            dot_nn(val_t[rows, : BLK * (qb + 1)], probs[first + qb])
                            for qb in range(half)
                        ],
                        axis=1,
                    )
                )
            o_ref[0, :, at : at + PAIR] = jnp.transpose(
                jnp.concatenate(pieces, axis=0)
            ).astype(BF16)


def qkv_block(acc, b, offset, rows):
    side = D // BLK
    m, i, j = b // (side * side), (b // side) % side, b % side
    return acc[pl.ds(BLK * i + offset, rows), D * m + BLK * j : D * m + BLK * (j + 1)]


def attention_back_kernel(packing, wins, part, split, meta, *refs):
    x_ref, qkv_ref, do_ref, lse_ref, da_ref = refs[:5]
    weight_refs = refs[5 : 5 + (2 * len(packing) or 1)]
    refs = refs[5 + len(weight_refs) :]
    dx_ref, refs = refs[0], refs[1:]
    dw_refs, refs = refs[: 2 if split else 1], refs[2 if split else 1 :]
    db_ref, full, mask, dqkv, acc = refs
    step = pl.program_id(0)

    @pl.when(step == 0)
    def _():
        fill_qkv_matrix(full, packing, weight_refs, meta[wins])
        acc[...] = jnp.zeros_like(acc)
        db_ref[...] = jnp.zeros_like(db_ref)

    fill_mask(mask, meta[step])
    marks = half_marks()
    for p in range(PAIRS):
        at = PAIR * p
        q8 = qkv_ref[0, :, at : at + PAIR] * jnp.asarray(SCALE, BF16)
        key = qkv_ref[0, :, D + at : D + at + PAIR]
        val = qkv_ref[0, :, 2 * D + at : 2 * D + at + PAIR]
        d_o = do_ref[0, :, at : at + PAIR]
        key_t = jnp.transpose(key)
        both = [(BLK * (qb + 1), slice(BLK * qb, BLK * (qb + 1))) for qb in range(WIN // BLK)]
        scores, grads = [], []
        for h in range(2):
            key_h, val_h = key * marks[h], val * marks[h]
            scores.append([dot_nt(key_h[:span], q8[cols]) + mask[:span, cols] for span, cols in both])
            grads.append([dot_nt(val_h[:span], d_o[cols]) for span, cols in both])
        lows, d_lows = [], []
        for h in range(2):
            row = 2 * p + h
            lows.append([])
            d_lows.append([])
            for (span, cols), s_t, d_probs in zip(both, scores[h], grads[h]):
                probs = jnp.exp(s_t - lse_ref[0, row : row + 1, cols])
                delta = jnp.sum(probs * d_probs, axis=0, keepdims=True)
                d_lows[h].append((probs * (d_probs - delta)).astype(BF16))
                lows[h].append(probs.astype(BF16))
        dq_pieces, dk_pieces, dv_pieces = [], [], []
        for h in range(2):
            rows = slice(HEAD_DIM * h, HEAD_DIM * (h + 1))
            dv_sum = dot_nn(lows[h][-1], d_o[both[-1][1]])
            dk_sum = dot_nn(d_lows[h][-1], q8[both[-1][1]])
            for (span, cols), low, d_low in list(zip(both, lows[h], d_lows[h]))[:-1]:
                dv_part, dk_part = dot_nn(low, d_o[cols]), dot_nn(d_low, q8[cols])
                dv_sum = jnp.concatenate([dv_sum[:span] + dv_part, dv_sum[span:]], axis=0)
                dk_sum = jnp.concatenate([dk_sum[:span] + dk_part, dk_sum[span:]], axis=0)
            dq_pieces.append(
                jnp.concatenate(
                    [dot_nn(key_t[rows, :span], d_low) for (span, _), d_low in zip(both, d_lows[h])],
                    axis=1,
                )
            )
            dk_pieces.append(dk_sum)
            dv_pieces.append(dv_sum)
        lane = lax.broadcasted_iota(jnp.int32, (WIN, PAIR), 1) < HEAD_DIM
        dq = jnp.transpose(jnp.concatenate(dq_pieces, axis=0)) * SCALE
        dk = jnp.where(lane, dk_pieces[0], dk_pieces[1])
        dv = jnp.where(lane, dv_pieces[0], dv_pieces[1])
        dqkv[:, at : at + PAIR] = dq.astype(BF16)
        dqkv[:, D + at : D + at + PAIR] = dk.astype(BF16)
        dqkv[:, 2 * D + at : 2 * D + at + PAIR] = dv.astype(BF16)
    h_t = jnp.transpose(x_ref[:, 0].reshape(WIN, D))
    for m in range(3):
        cols = slice(D * m, D * (m + 1))
        rows = dqkv[:, cols]
        acc[:, cols] += dot_nn(h_t, rows)
        if m != 1:
            db_ref[(m // 2) : (m // 2) + 1, :] += jnp.sum(
                rows.astype(F32), axis=0, keepdims=True
            )
    total = da_ref[0]
    for m in range(3):
        cols = slice(D * m, D * (m + 1))
        total = total + dot_nt(dqkv[:, cols], full[:, cols])
    dx_ref[:, 0] = total.astype(BF16).reshape(dx_ref.shape[0], dx_ref.shape[2], D)

    @pl.when(step == pl.num_programs(0) - 1)
    def _():
        write_gradient(
            functools.partial(qkv_block, acc), QKV_BLOCKS, part, meta[wins], dw_refs
        )


def normal_parts(u):
    size = jnp.abs(u)
    t = 1.0 / (1.0 + (0.3275911 * ROOT_HALF) * size)
    expo = jnp.exp(-0.5 * (u * u))
    poly = t * (
        0.5 * 0.254829592
        + t
        * (
            -0.5 * 0.284496736
            + t * (0.5 * 1.421413741 + t * (-0.5 * 1.453152027 + t * (0.5 * 1.061405429)))
        )
    )
    tail = poly * expo
    return jnp.where(u >= 0.0, 1.0 - tail, tail), expo


def norm_stats(rows):
    mean = jnp.mean(rows, axis=1, keepdims=True)
    centered = rows - mean
    spread = jnp.mean(centered * centered, axis=1, keepdims=True)
    inverse = lax.rsqrt(spread + NORM_EPS)
    return centered * inverse, inverse


def norm_back(d_rows, normal, inverse):
    mean_d = jnp.mean(d_rows, axis=1, keepdims=True)
    mean_dn = jnp.mean(d_rows * normal, axis=1, keepdims=True)
    return inverse * (d_rows - mean_d - normal * mean_dn)


def fill_ffn_matrices(w_out, w_up, w_down, packing, refs, core):
    side = D // BLK
    for base, offset, ref in each_piece(packing, refs, core):
        blocks, rows = ref.shape[:2]
        for n in range(blocks):
            full, i, j = ffn_place(base + n, (w_out, w_up, w_down))
            full[pl.ds(BLK * i + offset, rows), BLK * j : BLK * (j + 1)] = ref[n]


def ffn_place(b, matrices):
    side = D // BLK
    if b < side * side:
        return matrices[0], b // side, b % side
    b -= side * side
    if b < side * FF_CHUNKS:
        return matrices[1], b // FF_CHUNKS, b % FF_CHUNKS
    b -= side * FF_CHUNKS
    return matrices[2], b // side, b % side


def ffn_kernel(packing, wins, tokens, part, split, pieces, meta, *refs):
    cot_ref, x_ref, o_ref, vec = refs[:4]
    weight_refs = refs[4 : 4 + (2 * len(packing) or 1)]
    refs = refs[4 + len(weight_refs) :]
    out_refs, refs = refs[:pieces], refs[pieces:]
    da_ref, do_ref = refs[:2]
    refs = refs[2:]
    dw_refs, refs = refs[: 2 if split else 1], refs[2 if split else 1 :]
    vg_ref, w_out, w_up, w_down, acc_out, acc_up, acc_down, z_ref, gp_ref, du_ref, buf = refs
    step = pl.program_id(0)
    length = meta[step]
    accs = (acc_out, acc_up, acc_down)

    def acc_block(b, offset, rows):
        full, i, j = ffn_place(b, accs)
        if full is acc_down:
            i, j = j, i
        return full.at[pl.ds(BLK * i + offset, rows), BLK * j : BLK * (j + 1)]

    @pl.when(step == 0)
    def _():
        fill_ffn_matrices(w_out, w_up, w_down, packing, weight_refs, meta[wins])
        for acc in accs:
            acc[...] = jnp.zeros_like(acc)
        vg_ref[...] = jnp.zeros_like(vg_ref)

    def add_row(row, values, at=0):
        vg_ref[row : row + 1, at : at + values.shape[1]] += jnp.sum(
            values.astype(F32), axis=0, keepdims=True
        )

    bias_out, bias_down = vec[2:3, :], vec[7:8, :]
    gain_one, shift_one = vec[8:9, :], vec[9:10, :]
    gain_two, shift_two = vec[10:11, :], vec[11:12, :]
    attended = o_ref[0]
    mixed = x_ref[:, 0].reshape(WIN, D).astype(F32) + (dot_nn(attended, w_out[...]) + bias_out)
    n_one, inv_one = norm_stats(mixed)
    normed = n_one * gain_one + shift_one
    normed_low = normed.astype(BF16)
    for c in range(FF // D):
        cols = slice(D * c, D * (c + 1))
        u = dot_nn(normed_low, w_up[:, cols]) + vec[3 + c : 4 + c, :]
        phi, expo = normal_parts(u)
        z_ref[:, cols] = (u * phi).astype(BF16)
        gp_ref[:, cols] = phi + (u * expo) * DENSITY
    summed = normed + (dot_nn(z_ref[...], w_down[...]) + bias_down)
    n_two, inv_two = norm_stats(summed)
    result = (n_two * gain_two + shift_two).astype(BF16)
    if pieces == 1:
        out_ref = out_refs[0]
        out_ref[:, 0] = result.reshape(out_ref.shape[0], out_ref.shape[2], D)
    else:
        buf[...] = result
        for s, out_ref in enumerate(out_refs):
            rows = out_ref.shape[1]
            at = pl.multiple_of((meta[wins + 1] ^ s) * rows, rows)
            out_ref[0] = buf[pl.ds(at, rows), :]

    places = lax.broadcasted_iota(jnp.int32, (WIN, 1), 0)
    valid = jnp.where(places < length, 1.0 / tokens, 0.0).astype(F32)
    seed = cot_ref[:, 0].reshape(WIN, D).astype(F32) * valid
    add_row(10, seed * n_two)
    add_row(11, seed)
    d_summed = norm_back(seed * gain_two, n_two, inv_two)
    d_ff = d_summed.astype(BF16)
    add_row(7, d_ff)
    for c in range(FF // D):
        cols = slice(D * c, D * (c + 1))
        d_z = dot_nt(d_ff, w_down[cols, :])
        d_u = (d_z * gp_ref[:, cols]).astype(BF16)
        add_row(3 + c, d_u)
        du_ref[:, cols] = d_u
    d_ff_t = jnp.transpose(d_ff)
    normed_t = jnp.transpose(normed_low)
    for c in range(FF // D):
        cols = slice(D * c, D * (c + 1))
        acc_down[:, cols] += dot_nn(d_ff_t, z_ref[:, cols])
        acc_up[:, cols] += dot_nn(normed_t, du_ref[:, cols])
    d_normed = d_summed + dot_nt(du_ref[...], w_up[...])
    add_row(8, d_normed * n_one)
    add_row(9, d_normed)
    d_mixed = norm_back(d_normed * gain_one, n_one, inv_one)
    da_ref[0] = d_mixed
    d_branch = d_mixed.astype(BF16)
    add_row(2, d_branch)
    acc_out[...] += dot_nn(jnp.transpose(attended), d_branch)
    do_ref[0] = dot_nt(d_branch, w_out[...]).astype(BF16)

    @pl.when(step == pl.num_programs(0) - 1)
    def _():
        for j in range(D // BLK):
            for i in range(FF_CHUNKS):
                at = (slice(BLK * j, BLK * (j + 1)), slice(BLK * i, BLK * (i + 1)))
                acc_down[at] = jnp.transpose(acc_down[at])
        write_gradient(
            lambda b, offset, rows: acc_block(b, offset, rows)[...],
            REST_BLOCKS, part, meta[wins], dw_refs,
        )


def whole_spec(shape):
    zeros = (0,) * len(shape)
    return pl.BlockSpec(shape, lambda w, m: zeros, pipeline_mode=pl.Buffered(1))


def blocks_spec(part, count, at):
    lead = part.ndim - 3
    shape = part.shape[:lead] + (count,) + part.shape[lead + 1 :]
    return pl.BlockSpec(
        shape, lambda w, m: (0,) * lead + (at, 0, 0), pipeline_mode=pl.Buffered(1)
    )


def total_spec(shape):
    zeros = (0,) * len(shape)
    return pl.BlockSpec(shape, lambda w, m: zeros)


def window_spec(begin, *shape):
    zeros = (0,) * len(shape)
    return pl.BlockSpec((1,) + shape, lambda w, m: (begin + w,) + zeros)


def segment_spec(dp, seg):
    return pl.BlockSpec((dp, 1, seg, D), lambda w, m: (0, w, 0, 0))


def input_spec(dp, seg, begin):
    return pl.BlockSpec((dp, 1, seg, D), lambda w, m: (0, begin + w, 0, 0))


def gradient_outs(blocks, part):
    if part % 16:
        return [jax.ShapeDtypeStruct((blocks, BLK, BLK), BF16)]
    return [jax.ShapeDtypeStruct((blocks, BLK // 2, BLK), BF16)] * 2


def run_kernel(kernel, wins, meta, ins, outs, scratch, flops, moved):
    return pl.pallas_call(
        kernel,
        grid_spec=pltpu.PrefetchScalarGridSpec(
            num_scalar_prefetch=1,
            grid=(wins,),
            in_specs=[spec for _, spec in ins],
            out_specs=[spec for _, spec in outs],
            scratch_shapes=scratch,
        ),
        out_shape=[shape for shape, _ in outs],
        compiler_params=pltpu.CompilerParams(
            dimension_semantics=("arbitrary",), vmem_limit_bytes=56 * 1024 * 1024
        ),
        cost_estimate=pl.CostEstimate(
            flops=flops, bytes_accessed=moved, transcendentals=wins * WIN * FF
        ),
    )(meta, *[values for values, _ in ins])


def call_attention(wins, meta, x, packing, weight_parts, bias):
    dp, _, seg, _ = x.shape
    shape = jax.ShapeDtypeStruct
    return run_kernel(
        functools.partial(attention_kernel, packing, wins),
        wins,
        meta,
        [(x, input_spec(dp, seg, 0)), (bias, whole_spec(bias.shape))]
        + [(piece, whole_spec(piece.shape)) for piece in weight_parts],
        [
            (shape((wins, WIN, 3 * D), BF16), window_spec(0, WIN, 3 * D)),
            (shape((wins, WIN, D), BF16), window_spec(0, WIN, D)),
            (shape((wins, HEADS, WIN), F32), window_spec(0, HEADS, WIN)),
        ],
        [pltpu.VMEM((D, 3 * D), BF16), pltpu.VMEM((WIN, WIN), F32)],
        wins * 3_000_000_000,
        wins * 1_000_000,
    )


def call_ffn(wins, tokens, part, apart, meta, x, attended, packing, weight_parts, vec):
    dp, _, seg, _ = x.shape
    shape = jax.ShapeDtypeStruct
    counts = (QKV_BLOCKS, QKV_BLOCKS, 2 * QKV_BLOCKS, 2 * QKV_BLOCKS)
    ins = [
        (x, input_spec(dp, seg, wins)),
        (x, input_spec(dp, seg, 0)),
        (attended, window_spec(0, WIN, D)),
        (vec, whole_spec(vec.shape)),
    ] + [
        (piece, blocks_spec(piece, count, 0) if packing else whole_spec(piece.shape))
        for piece, count in zip(weight_parts, counts)
    ]
    outs = [(shape((dp, wins, seg, D), BF16), segment_spec(dp, seg))]
    if apart:
        outs = [(shape((wins, seg, D), BF16), window_spec(0, seg, D))] * dp
    return run_kernel(
        functools.partial(ffn_kernel, packing, wins, tokens, part, part % 16 == 0, dp if apart else 1),
        wins,
        meta,
        ins,
        [
            *outs,
            (shape((wins, WIN, D), F32), window_spec(0, WIN, D)),
            (shape((wins, WIN, D), BF16), window_spec(0, WIN, D)),
        ]
        + [(out, total_spec(out.shape)) for out in gradient_outs(REST_BLOCKS, part)]
        + [(shape((ROWS_VEC, D), F32), total_spec((ROWS_VEC, D)))],
        [
            pltpu.VMEM((D, D), BF16),
            pltpu.VMEM((D, FF), BF16),
            pltpu.VMEM((FF, D), BF16),
            pltpu.VMEM((D, D), F32),
            pltpu.VMEM((D, FF), F32),
            pltpu.VMEM((D, FF), F32),
            pltpu.VMEM((WIN, FF), BF16),
            pltpu.VMEM((WIN, FF), F32),
            pltpu.VMEM((WIN, FF), BF16),
            pltpu.VMEM((WIN, D), BF16),
        ],
        wins * 250_000_000,
        wins * 1_000_000,
    )


def call_attention_back(
    part, meta, packing, weight_parts, x, qkv, d_o, lse, d_mixed
):
    dp, _, seg, _ = x.shape
    wins = d_o.shape[0]
    shape = jax.ShapeDtypeStruct
    return run_kernel(
        functools.partial(attention_back_kernel, packing, wins, part, part % 16 == 0),
        wins,
        meta,
        [
            (x, input_spec(dp, seg, 0)),
            (qkv, window_spec(0, WIN, 3 * D)),
            (d_o, window_spec(0, WIN, D)),
            (lse, window_spec(0, HEADS, WIN)),
            (d_mixed, window_spec(0, WIN, D)),
        ]
        + [(piece, whole_spec(piece.shape)) for piece in weight_parts],
        [(shape((dp, wins, seg, D), BF16), segment_spec(dp, seg))]
        + [(out, total_spec(out.shape)) for out in gradient_outs(QKV_BLOCKS, part)]
        + [(shape((8, D), F32), total_spec((8, D)))],
        [
            pltpu.VMEM((D, 3 * D), BF16),
            pltpu.VMEM((WIN, WIN), F32),
            pltpu.VMEM((WIN, 3 * D), BF16),
            pltpu.VMEM((D, 3 * D), F32),
        ],
        wins * 30_000_000_000,
        wins * 8_000_000,
    )


def split_first_kernel(terms, bits, *refs):
    ins, outs = refs[:terms], refs[terms:]

    def total(side, at):
        return sum(ref[side, :, at].astype(F32) for ref in ins).astype(BF16)

    for y in range(2):
        for which in range(2):
            outs[which][:, y] = total(0, 2 * y + (bits[0] if which == 0 else 1 - bits[0]))
    for x in range(2):
        for which in range(2):
            outs[2 + which][:, x] = total(1, 2 * (bits[1] if which == 0 else 1 - bits[1]) + x)


def split_second_kernel(bits, *refs):
    for side in range(2):
        mine, got = refs[2 * side : 2 * side + 2]
        for which in range(2):
            bit = bits[1 - side]
            at = bit if which == 0 else 1 - bit
            refs[4 + 2 * side + which][...] = (
                mine[:, at].astype(F32) + got[:, at].astype(F32)
            ).astype(BF16)


def slabs_kernel(dp, me_ref, *refs):
    pairs, vec, outs, total = refs[: len(refs) - dp - 2], refs[-dp - 2], refs[-dp - 1 : -1], refs[-1]
    base = 0
    for n in range(0, len(pairs), 2):
        blocks = pairs[n].shape[0]
        total[base : base + blocks] = pairs[n][...].astype(F32) + pairs[n + 1][...].astype(F32)
        base += blocks
    owned = outs[0].shape[0] - 1
    for s in range(dp):
        slab = total[pl.ds((me_ref[0] ^ s) * owned, owned)]
        outs[s][:owned] = slab.astype(outs[s].dtype)
        outs[s][owned] = vec[...].astype(BF16).astype(outs[s].dtype)


def update_kernel(packing, scalars, *refs):
    count = 2 * len(packing)
    parts, root_parts, refs = refs[:count], refs[count : 2 * count], refs[2 * count :]
    own, left_stats, right_stats, left_roots, weights = refs[:5]
    left_new, right_new, weights_new, full, roots = refs[5:]
    fill_stack(full, packing, parts, scalars[0])
    fill_stack(roots, packing, root_parts, scalars[0])
    blocks, rows, _ = own.shape
    at = scalars[1] * rows
    lane = lax.broadcasted_iota(jnp.int32, (rows, BLK), 1)
    line = lax.broadcasted_iota(jnp.int32, (rows, BLK), 0)
    pick = jnp.where(lane == line + at, 1.0, 0.0).astype(BF16)
    for b in range(blocks):
        whole = full[b]
        crossed = dot_nt(jnp.concatenate([own[b], pick], axis=0), whole)
        left_new[b] = DECAY * left_stats[b] + (1.0 - DECAY) * crossed[:rows]
        turned = jnp.concatenate([left_roots[b].astype(BF16), crossed[rows:].astype(BF16)], axis=0)
        passed = dot_nn(turned, whole)
        right_new[b] = DECAY * right_stats[b] + (1.0 - DECAY) * passed[rows:]
        step = dot_nn(passed[:rows].astype(BF16), roots[b])
        weights_new[b] = weights[b] - MATRIX_RATE * step


def call_small(kernel, steps, scalars, ins, outs, scratch=(), room=14):
    def spec(shape, axis):
        if isinstance(axis, pl.BlockSpec):
            return axis
        block = tuple(n // steps if d == axis else n for d, n in enumerate(shape))
        return pl.BlockSpec(block, lambda g, m: tuple(g if d == axis else 0 for d in range(len(shape))))

    return pl.pallas_call(
        kernel,
        grid_spec=pltpu.PrefetchScalarGridSpec(
            num_scalar_prefetch=1,
            grid=(steps,),
            in_specs=[spec(values.shape, axis) for values, axis in ins],
            out_specs=[spec(shape.shape, axis) for shape, axis in outs],
            scratch_shapes=list(scratch),
        ),
        out_shape=[shape for shape, _ in outs],
        compiler_params=pltpu.CompilerParams(
            dimension_semantics=("arbitrary",), vmem_limit_bytes=room * 1024 * 1024
        ),
    )(scalars, *[values for values, _ in ins])


def update_blocks(scalars, packing, parts, root_parts, own, *shards):
    blocks = own.shape[0]
    out = jax.ShapeDtypeStruct(own.shape, F32)
    share = blocks // 2
    ats = (QKV_BLOCKS // share, QKV_BLOCKS // share, 2 * QKV_BLOCKS // share, 2 * QKV_BLOCKS // share)
    return call_small(
        functools.partial(update_kernel, packing),
        1,
        scalars,
        [(part, None) for part in parts]
        + [(part, blocks_spec(part, share, at)) for part, at in zip(root_parts, ats)]
        + [(values, None) for values in (own, *shards)],
        [(out, None)] * 3,
        [pltpu.VMEM((blocks, BLK, BLK), BF16)] * 2,
        24,
    )


def split_first(bits, *terms):
    blocks, height, cols = terms[0].shape
    half = blocks // 2
    view = (2, half, 4, height // 4, cols)
    out = jax.ShapeDtypeStruct((half, 2, height // 4, cols), BF16)
    return call_small(
        functools.partial(split_first_kernel, len(terms)),
        max(half // 6, 1),
        bits,
        [(term.reshape(view), 1) for term in terms],
        [(out, 0)] * 4,
    )


def split_second(bits, *parts):
    half, _, rows, cols = parts[0].shape
    out = jax.ShapeDtypeStruct((half, rows, cols), BF16)
    return call_small(
        split_second_kernel, 1, bits, [(part, 0) for part in parts], [(out, 0)] * 4
    )


def make_slabs(dp, me, parts, vec):
    _, rows, cols = parts[0].shape
    blocks = sum(part.shape[0] for part in parts) // 2
    shape = (blocks // dp + 1, rows, cols)
    return call_small(
        functools.partial(slabs_kernel, dp),
        1,
        me,
        [(part, None) for part in [*parts, vec]],
        [(jax.ShapeDtypeStruct(shape, F32 if s == 0 else BF16), None) for s in range(dp)],
        [pltpu.VMEM((blocks, rows, cols), F32)],
    )


def swap(values, axis, size, k):
    return lax.ppermute(values, axis, [(i, i ^ k) for i in range(size)])


def bits_of(size):
    return [1 << i for i in range(size.bit_length() - 1)]


def hop_orders(seq_count):
    high = [k for k in bits_of(seq_count) if k > 1]
    return (high, high[::-1])


def gather_hop(state, k, seq_count, seq_index, *marks):
    cur, lead = state
    got = after(swap(cur, "seq", seq_count, k), *marks)
    odd = (seq_index & k) != 0
    cur = jnp.stack([jnp.where(odd, got, cur), jnp.where(odd, cur, got)], axis=0)
    return cur, [k] + lead


def gather_end(state):
    cur, lead = state
    count = len(lead)
    blocks, rows, cols = cur.shape[count:]
    axes = [count] + [lead.index(k) for k in sorted(lead, reverse=True)] + [count + 1, count + 2]
    return cur.transpose(axes).reshape(blocks, rows << count, cols)


def halves(cur):
    half = cur.shape[0] // 2
    return [cur[:half], cur[half:]]


def gather_split(cur, seq_count, seq_index):
    done = []
    for part, order in zip(halves(cur), hop_orders(seq_count)):
        state = (part, [])
        for k in order + [1]:
            state = gather_hop(state, k, seq_count, seq_index)
        done.append(gather_end(state))
    return jnp.concatenate(done, axis=0)


def pack_weights(rows, roots, orders, seq_count, seq_index):
    states = [
        (jnp.concatenate(pair, axis=0), []) for pair in zip(halves(rows), halves(roots))
    ]
    for step in range(len(orders[0])):
        states = [
            gather_hop(state, order[step], seq_count, seq_index)
            for state, order in zip(states, orders)
        ]
        if step == 0:
            cur, lead = states[0]
            axis = len(lead)
            states = [
                (lax.slice_in_dim(cur, 0, QKV_BLOCKS, axis=axis), lead),
                (lax.slice_in_dim(cur, QKV_BLOCKS, cur.shape[axis], axis=axis), lead),
                states[1],
            ]
            orders = (orders[0], orders[0], orders[1])
    return states


def join_cores(states, seq_count, seq_index, *marks):
    if states[0][0].shape[-2] % 16:
        states = [gather_hop(state, 1, seq_count, seq_index) for state in states]
        return (), [jnp.concatenate([gather_end(state) for state in states], axis=0)]
    parts = []
    for cur, _ in states:
        parts += [cur, after(swap(cur, "seq", seq_count, 1), *marks)]
    return tuple(tuple(lead) for _, lead in states), parts


def scatter_first(whole, seq_count, seq_index):
    left = sorted(bits_of(seq_count), reverse=True)
    blocks, height, cols = whole.shape
    rows = height // seq_count
    cur = whole.reshape(blocks, seq_count // 2, 2, rows, cols)
    mine, other = [
        lax.dynamic_index_in_dim(cur, bit, 2, keepdims=False)
        for bit in (seq_index % 2, 1 - seq_index % 2)
    ]
    cur = mine.astype(F32) + swap(other, "seq", seq_count, 1).astype(F32)
    left.remove(1)
    cur = cur.astype(BF16).reshape([blocks] + [2] * len(left) + [rows, cols])
    return [(half, left) for half in halves(cur)]


def scatter_hop(state, k, seq_count, seq_index, *marks):
    cur, left = state
    axis = 1 + left.index(k)
    bit = (seq_index // k) % 2
    mine = lax.dynamic_index_in_dim(cur, bit, axis, keepdims=False)
    other = lax.dynamic_index_in_dim(cur, 1 - bit, axis, keepdims=False)
    got = after(swap(other, "seq", seq_count, k), *marks)
    cur = (mine.astype(F32) + got.astype(F32)).astype(BF16)
    return cur, [b for b in left if b != k]


def after(values, *marks):
    if not marks:
        return values
    return lax.optimization_barrier((values, marks))[0]


def body(
    inputs,
    cotangent,
    lengths,
    weights,
    vectors,
    positions,
    left_stats,
    right_stats,
    left_roots,
    right_roots,
    vector_second,
    position_second,
):
    seq_count = lax.axis_size("seq")
    dp_count = lax.axis_size("dp")
    seq_index = lax.axis_index("seq")
    dp_index = lax.axis_index("dp")
    micro, wins_dev, segment, model_width = inputs.shape
    wins = wins_dev // dp_count
    total_tokens = micro * wins_dev * seq_count * segment * dp_count
    owned, row_part, _ = weights.shape
    def exchange(rows):
        return lax.all_to_all(rows, "dp", 0, 0, tiled=True)

    grouped = (dp_count, wins, segment, model_width)
    own = weights.astype(BF16)
    orders = hop_orders(seq_count)
    hops = len(orders[0])

    def scatter_both(states, step, *marks):
        return [
            scatter_hop(state, order[step], seq_count, seq_index, *marks)
            for state, order in zip(states, orders)
        ]

    vec = vectors.reshape(-1, D)
    bias_qv = jnp.concatenate([vec[0:2], jnp.zeros((6, D), F32)], axis=0)
    vec_pad = jnp.concatenate([vec, jnp.zeros((ROWS_VEC - vec.shape[0], D), F32)], axis=0)

    metas = [
        lax.dynamic_index_in_dim(
            lengths[i].reshape(dp_count, wins), dp_index, 0, keepdims=False
        )
        for i in range(micro)
    ]
    metas = [
        jnp.concatenate([lens, (seq_index % 2)[None], dp_index[None]]).astype(jnp.int32)
        for lens in metas
    ]
    shards = [own] + [swap(own, "dp", dp_count, s) for s in range(1, dp_count)]
    weight_rows = jnp.concatenate(
        [lax.select_n(dp_index ^ j, *shards) for j in range(dp_count)], axis=0
    )
    pairs = [
        jnp.concatenate(
            [
                (inputs[i].astype(F32) + positions[None]).astype(BF16).reshape(grouped),
                cotangent[i].reshape(grouped),
            ],
            axis=1,
        )
        for i in range(micro)
    ]
    taken = [exchange(after(pairs[0], *shards[1:]))]
    roots_low = right_roots.astype(BF16)
    groups = pack_weights(weight_rows, roots_low, orders, seq_count, seq_index)
    cur, lead = groups[0]
    groups[0] = (after(cur, vec_pad, bias_qv, roots_low, *metas), lead)
    packing_qkv, parts_qkv = join_cores(groups[:1], seq_count, seq_index)
    for i in range(1, micro):
        marks = (taken[-1], *metas, *parts_qkv, *(cur for cur, _ in groups[1:]))
        taken.append(exchange(after(pairs[i], *marks)))
    ffn, out_got, dx_got = [], [], []
    forward = [
        call_attention(wins, metas[0], taken[0], packing_qkv, parts_qkv, bias_qv)
    ]
    mark = (forward[0][2],)
    lse = forward[0][2]
    packing_rest, parts_rest = join_cores(groups[1:], seq_count, seq_index, lse)
    share = owned // 2
    if not packing_rest:
        (stack,) = parts_rest
        middle = QKV_BLOCKS + share
        roots_full = jnp.concatenate([stack[QKV_BLOCKS:middle], stack[-share:]], axis=0)
        parts_rest = [jnp.concatenate([stack[:QKV_BLOCKS], stack[middle:-share]], axis=0)]
    fast = seq_count == 8 and row_part % 16 == 0
    bits = jnp.stack([(seq_index // 2) % 2, (seq_index // 4) % 2]).astype(jnp.int32)

    def over_cores(parts, *marks):
        keep, send = parts
        return [keep, after(swap(send, "seq", seq_count, 1), *marks)]

    def hop(parts, count, *marks):
        mine_a, send_a, mine_b, send_b = parts
        k_a, k_b = (2, 4) if count == 0 else (4, 2)
        got_a = after(swap(send_a, "seq", seq_count, k_a), *marks)
        got_b = after(swap(send_b, "seq", seq_count, k_b), *marks)
        return [mine_a, got_a, mine_b, got_b]

    vec_sums = jnp.zeros((ROWS_VEC, D), F32)
    dw_rest, dw_qkv = [], []
    for i in range(micro):
        if i > 0:
            forward.append(
                call_attention(
                    wins, after(metas[i], *mark), taken[i], packing_qkv, parts_qkv, bias_qv
                )
            )
            mark = (forward[i][2],)
        results = call_ffn(
            wins, total_tokens, row_part, True, after(metas[i], *mark), taken[i], forward[i][1],
            packing_rest, parts_rest, vec_pad,
        )
        out, (d_mixed, d_o, *dw, vg) = results[:dp_count], results[dp_count:]
        got = [out[0]] + [swap(out[s], "dp", dp_count, s) for s in range(1, dp_count)]
        out_got.append(tuple(got))
        ffn.append((d_mixed, d_o))
        vec_sums = vec_sums + vg
        mark = (vg,)
        dw_rest.append(dw)
    gates = mark + (out_got[0],)
    rest_core, qkv_core = [], []
    for i in range(micro):
        dx, *dw, db = call_attention_back(
            row_part, after(metas[i], gates), packing_qkv, parts_qkv, taken[i], forward[i][0],
            ffn[i][1], forward[i][2], ffn[i][0],
        )
        vec_sums = vec_sums + jnp.concatenate([db, jnp.zeros_like(db)], axis=0)
        dw_qkv.append(dw)
        gates = (db,) + tuple(out_got[1:])
        if fast and i == 0:
            for n in range(micro):
                rest_core += over_cores(dw_rest[n], *(mark[:1] if n == 0 else (db,)))
            rest = split_first(bits, *rest_core)
            gates = gates + tuple(rest)
        if fast and i == micro - 1:
            rest = hop(rest, 0, db)
            qkv_core += over_cores(dw_qkv[0], db)
            dx = after(dx, *rest)
        dx_got.append(exchange(after(dx, *dx_got[-1:])))

    whole = (wins_dev, segment, model_width)
    out_got = [
        jnp.stack([lax.select_n(dp_index ^ e, *got) for e in range(dp_count)]) for got in out_got
    ]
    layer_out = jnp.stack([got.reshape(whole) for got in out_got], axis=0)

    for k in bits_of(seq_count):
        vec_sums = vec_sums + swap(vec_sums, "seq", seq_count, k)
    if fast:
        qkv_core += over_cores(dw_qkv[1])
        rest = split_second(bits, *rest)
        states = split_first(after(bits, *rest), *qkv_core)
        rest = hop(rest, 1)
        states = hop(split_second(bits, *hop(states, 0)), 1)
        slabs = make_slabs(
            dp_count, after(dp_index[None].astype(jnp.int32), dx_got[-1], layer_out), states + rest,
            vec_sums.reshape(row_part, BLK),
        )
    else:
        states = []
        for parts in (dw_qkv, dw_rest):
            total = sum(part[0].astype(F32) for part in parts).astype(BF16)
            group = scatter_first(total, seq_count, seq_index)
            for step in range(hops):
                group = scatter_both(group, step)
            states += group
        joined = jnp.concatenate([cur for cur, _ in states], axis=0)
        joined = joined.reshape((dp_count, owned) + joined.shape[1:])
        vec_rows = vec_sums.astype(BF16).reshape(-1, row_part, BLK)
        slabs = [
            jnp.concatenate(
                [lax.dynamic_index_in_dim(joined, dp_index ^ s, 0, keepdims=False), vec_rows]
            )
            for s in range(dp_count)
        ]
    slabs = [slabs[0].astype(F32)] + [
        swap(slabs[s], "dp", dp_count, s).astype(F32) for s in range(1, dp_count)
    ]
    grad_rows = sum(slab[:owned] for slab in slabs)
    vec_sums = sum(lax.select_n(dp_index ^ j, *[slab[owned:] for slab in slabs]) for j in range(dp_count))
    vec_sums = vec_sums.reshape(ROWS_VEC, D)
    grad_low = grad_rows.astype(BF16)
    if fast:
        states = [(part, []) for part in halves(grad_low)]
        for step in range(hops):
            states = [
                gather_hop(state, order[step], seq_count, seq_index)
                for state, order in zip(states, orders)
            ]
        packing, parts = join_cores(states, seq_count, seq_index)
        left_new, right_new, weights_new = update_blocks(
            jnp.stack([seq_index % 2, seq_index]).astype(jnp.int32), packing, parts, parts_rest,
            grad_low, left_stats, right_stats, left_roots, weights,
        )
    else:
        grad_full = gather_split(grad_low, seq_count, seq_index)
        row_start = seq_index * row_part

        def batched(spec, left, right):
            return jnp.einsum(spec, left, right, preferred_element_type=F32)

        left_new = DECAY * left_stats + (1.0 - DECAY) * batched("bij,bkj->bik", grad_low, grad_full)
        column_part = lax.dynamic_slice_in_dim(grad_full, row_start, row_part, 2)
        right_new = DECAY * right_stats + (1.0 - DECAY) * batched(
            "bki,bkj->bij", column_part, grad_full
        )
        left_applied = batched("bij,bjk->bik", left_roots.astype(BF16), grad_full)
        step_rows = batched("bij,bjk->bik", left_applied.astype(BF16), roots_full)
        weights_new = weights - MATRIX_RATE * step_rows

    place_sum = sum(jnp.sum(got.astype(F32), axis=(0, 1)) for got in dx_got)
    for k in bits_of(seq_count):
        low = place_sum.astype(BF16)
        place_sum = low.astype(F32) + swap(low, "seq", seq_count, k).astype(F32)
    vector_grads = vec_sums[: vec.shape[0]].reshape(-1)
    vector_second_new = DECAY * vector_second + (1.0 - DECAY) * vector_grads * vector_grads
    vectors_new = vectors - VECTOR_RATE * vector_grads / (jnp.sqrt(vector_second_new) + ROOT_EPS)
    position_grads = place_sum
    position_second_new = DECAY * position_second + (1.0 - DECAY) * position_grads * position_grads
    positions_new = positions - VECTOR_RATE * position_grads / (
        jnp.sqrt(position_second_new) + ROOT_EPS
    )
    return (
        layer_out,
        jnp.stack([got.astype(F32).reshape(whole) for got in dx_got], axis=0),
        grad_rows,
        left_new,
        right_new,
        weights_new,
        vector_grads,
        vector_second_new,
        vectors_new,
        position_grads,
        position_second_new,
        positions_new,
    )


def solution(mesh):
    rows = P(None, "seq", "dp", None)
    blocks = P("dp", "seq", None)
    in_specs = (
        rows, rows, P(None, "seq"), blocks, P(), P("dp", None),
        blocks, blocks, blocks, blocks, P(), P("dp", None),
    )
    out_specs = (
        rows, rows, blocks, blocks, blocks, blocks,
        P(), P(), P(), P("dp", None), P("dp", None), P("dp", None),
    )
    return jax.shard_map(body, mesh=mesh, in_specs=in_specs, out_specs=out_specs, check_vma=False)
```

```python
import functools
import itertools

import jax
import jax.numpy as jnp
from jax import lax
from jax.experimental import pallas as pl
from jax.experimental.pallas import tpu as pltpu
from jax.sharding import PartitionSpec as P

HEADS = 8
FF = 2048
WIN = 512
D = 512
BLK = 256
QKV_BLOCKS = 12
REST_BLOCKS = 36
HEAD_DIM = D // HEADS
PAIR = 2 * HEAD_DIM
PAIRS = HEADS // 2
FF_CHUNKS = FF // BLK
ROWS_VEC = 16
GROUP = 2

NORM_EPS = 1e-05
ROOT_EPS = 1e-08
DECAY = 0.5
MATRIX_RATE = 0.5
VECTOR_RATE = 0.2
MASKED = -1e30
SCALE = HEAD_DIM ** (-0.5)
ROOT_HALF = 0.7071067811865476
DENSITY = 0.3989422804014327

F32 = jnp.float32
BF16 = jnp.bfloat16


def dot_nn(left, right):
    return lax.dot_general(left, right, (((1,), (0,)), ((), ())), preferred_element_type=F32)


def dot_nt(left, right):
    return lax.dot_general(left, right, (((1,), (1,)), ((), ())), preferred_element_type=F32)


def each_piece(packing, refs, core):
    if not packing:
        yield 0, 0, refs[0]
        return
    base = 0
    for side, bits in enumerate(packing):
        for which in range(2):
            ref = refs[2 * side + which]
            blocks, rows = ref.shape[len(bits)], ref.shape[len(bits) + 1]
            last = core if which == 0 else 1 - core
            for at in itertools.product(range(2), repeat=len(bits)):
                first = sum(k * v for k, v in zip(bits, at))
                yield base, pl.multiple_of((first + last) * rows, rows), ref.at[at]
        base += blocks


def fill_qkv_matrix(full, packing, refs, core):
    side = D // BLK
    for base, offset, ref in each_piece(packing, refs, core):
        blocks, rows = ref.shape[:2]
        for n in range(blocks):
            b = base + n
            m, i, j = b // (side * side), (b // side) % side, b % side
            cols = slice(D * m + BLK * j, D * m + BLK * (j + 1))
            full[pl.ds(BLK * i + offset, rows), cols] = ref[n]


def fill_stack(stack, packing, refs, core):
    for base, offset, ref in each_piece(packing, refs, core):
        blocks, rows = ref.shape[:2]
        for n in range(blocks):
            stack[base + n, pl.ds(offset, rows), :] = ref[n]


def write_gradient(block_at, blocks, rows, core, outs):
    for b in range(blocks):
        if len(outs) == 1:
            outs[0][b] = block_at(b, 0, BLK).astype(BF16)
            continue
        for which, out in enumerate(outs):
            last = core if which == 0 else 1 - core
            for n in range(BLK // (2 * rows)):
                offset = pl.multiple_of((2 * n + last) * rows, rows)
                out[b, n * rows : (n + 1) * rows, :] = block_at(b, offset, rows).astype(BF16)


def fill_mask(mask, length):
    for i in range(WIN // BLK):
        keys = lax.broadcasted_iota(jnp.int32, (BLK, WIN), 0) + BLK * i
        queries = lax.broadcasted_iota(jnp.int32, (BLK, WIN), 1)
        keep = (keys <= queries) & (keys < length)
        mask[BLK * i : BLK * (i + 1), :] = jnp.where(keep, 0.0, MASKED).astype(F32)


def half_marks():
    lane = lax.broadcasted_iota(jnp.int32, (1, PAIR), 1)
    low = jnp.where(lane < HEAD_DIM, 1.0, 0.0)
    return (low.astype(BF16), (1.0 - low).astype(BF16))


def attention_kernel(packing, wins, meta, x_ref, bias, *refs):
    weight_refs = refs[: 2 * len(packing) or 1]
    qkv_ref, o_ref, lse_ref, full, mask = refs[len(weight_refs) :]
    step = pl.program_id(0)

    @pl.when(step == 0)
    def _():
        fill_qkv_matrix(full, packing, weight_refs, meta[wins])

    hidden = x_ref[:, 0].reshape(WIN, D)
    for m in range(3):
        cols = slice(D * m, D * (m + 1))
        rows = dot_nn(hidden, full[:, cols])
        if m != 1:
            rows = rows + bias[(m // 2) : (m // 2) + 1, :]
        qkv_ref[0, :, cols] = rows.astype(BF16)
    fill_mask(mask, meta[step])
    marks = half_marks()
    half = WIN // BLK
    for group in range(0, PAIRS, GROUP):
        cases, scores, probs = [], [], []
        for p in range(group, group + GROUP):
            at = PAIR * p
            q8 = qkv_ref[0, :, at : at + PAIR] * jnp.asarray(SCALE, BF16)
            key = qkv_ref[0, :, D + at : D + at + PAIR]
            for h in range(2):
                key_h = key * marks[h]
                for qb in range(half):
                    cols, span = slice(BLK * qb, BLK * (qb + 1)), BLK * (qb + 1)
                    cases.append((2 * p + h, qb))
                    scores.append(dot_nt(key_h[:span], q8[cols]) + mask[:span, cols])
        for (row, qb), s_t in zip(cases, scores):
            cols = slice(BLK * qb, BLK * (qb + 1))
            top = jnp.max(s_t, axis=0, keepdims=True)
            expo = jnp.exp(s_t - top)
            total = jnp.sum(expo, axis=0, keepdims=True)
            probs.append((expo * (1.0 / total)).astype(BF16))
            lse_ref[0, row : row + 1, cols] = top + jnp.log(total)
        for n, p in enumerate(range(group, group + GROUP)):
            at = PAIR * p
            val_t = jnp.transpose(qkv_ref[0, :, 2 * D + at : 2 * D + at + PAIR])
            pieces = []
            for h in range(2):
                rows = slice(HEAD_DIM * h, HEAD_DIM * (h + 1))
                first = (2 * n + h) * half
                pieces.append(
                    jnp.concatenate(
                        [
                            dot_nn(val_t[rows, : BLK * (qb + 1)], probs[first + qb])
                            for qb in range(half)
                        ],
                        axis=1,
                    )
                )
            o_ref[0, :, at : at + PAIR] = jnp.transpose(
                jnp.concatenate(pieces, axis=0)
            ).astype(BF16)


def qkv_block(acc, b, offset, rows):
    side = D // BLK
    m, i, j = b // (side * side), (b // side) % side, b % side
    return acc[pl.ds(BLK * i + offset, rows), D * m + BLK * j : D * m + BLK * (j + 1)]


def attention_back_kernel(packing, wins, part, split, meta, *refs):
    x_ref, qkv_ref, do_ref, lse_ref, da_ref = refs[:5]
    weight_refs = refs[5 : 5 + (2 * len(packing) or 1)]
    refs = refs[5 + len(weight_refs) :]
    dx_ref, refs = refs[0], refs[1:]
    dw_refs, refs = refs[: 2 if split else 1], refs[2 if split else 1 :]
    db_ref, full, mask, dqkv, acc = refs
    step = pl.program_id(0)

    @pl.when(step == 0)
    def _():
        fill_qkv_matrix(full, packing, weight_refs, meta[wins])
        acc[...] = jnp.zeros_like(acc)
        db_ref[...] = jnp.zeros_like(db_ref)

    fill_mask(mask, meta[step])
    marks = half_marks()
    for p in range(PAIRS):
        at = PAIR * p
        q8 = qkv_ref[0, :, at : at + PAIR] * jnp.asarray(SCALE, BF16)
        key = qkv_ref[0, :, D + at : D + at + PAIR]
        val = qkv_ref[0, :, 2 * D + at : 2 * D + at + PAIR]
        d_o = do_ref[0, :, at : at + PAIR]
        key_t = jnp.transpose(key)
        both = [(BLK * (qb + 1), slice(BLK * qb, BLK * (qb + 1))) for qb in range(WIN // BLK)]
        scores, grads = [], []
        for h in range(2):
            key_h, val_h = key * marks[h], val * marks[h]
            scores.append([dot_nt(key_h[:span], q8[cols]) + mask[:span, cols] for span, cols in both])
            grads.append([dot_nt(val_h[:span], d_o[cols]) for span, cols in both])
        lows, d_lows = [], []
        for h in range(2):
            row = 2 * p + h
            lows.append([])
            d_lows.append([])
            for (span, cols), s_t, d_probs in zip(both, scores[h], grads[h]):
                probs = jnp.exp(s_t - lse_ref[0, row : row + 1, cols])
                delta = jnp.sum(probs * d_probs, axis=0, keepdims=True)
                d_lows[h].append((probs * (d_probs - delta)).astype(BF16))
                lows[h].append(probs.astype(BF16))
        dq_pieces, dk_pieces, dv_pieces = [], [], []
        for h in range(2):
            rows = slice(HEAD_DIM * h, HEAD_DIM * (h + 1))
            dv_sum = dot_nn(lows[h][-1], d_o[both[-1][1]])
            dk_sum = dot_nn(d_lows[h][-1], q8[both[-1][1]])
            for (span, cols), low, d_low in list(zip(both, lows[h], d_lows[h]))[:-1]:
                dv_part, dk_part = dot_nn(low, d_o[cols]), dot_nn(d_low, q8[cols])
                dv_sum = jnp.concatenate([dv_sum[:span] + dv_part, dv_sum[span:]], axis=0)
                dk_sum = jnp.concatenate([dk_sum[:span] + dk_part, dk_sum[span:]], axis=0)
            dq_pieces.append(
                jnp.concatenate(
                    [dot_nn(key_t[rows, :span], d_low) for (span, _), d_low in zip(both, d_lows[h])],
                    axis=1,
                )
            )
            dk_pieces.append(dk_sum)
            dv_pieces.append(dv_sum)
        lane = lax.broadcasted_iota(jnp.int32, (WIN, PAIR), 1) < HEAD_DIM
        dq = jnp.transpose(jnp.concatenate(dq_pieces, axis=0)) * SCALE
        dk = jnp.where(lane, dk_pieces[0], dk_pieces[1])
        dv = jnp.where(lane, dv_pieces[0], dv_pieces[1])
        dqkv[:, at : at + PAIR] = dq.astype(BF16)
        dqkv[:, D + at : D + at + PAIR] = dk.astype(BF16)
        dqkv[:, 2 * D + at : 2 * D + at + PAIR] = dv.astype(BF16)
    h_t = jnp.transpose(x_ref[:, 0].reshape(WIN, D))
    for m in range(3):
        cols = slice(D * m, D * (m + 1))
        rows = dqkv[:, cols]
        acc[:, cols] += dot_nn(h_t, rows)
        if m != 1:
            db_ref[(m // 2) : (m // 2) + 1, :] += jnp.sum(
                rows.astype(F32), axis=0, keepdims=True
            )
    total = da_ref[0]
    for m in range(3):
        cols = slice(D * m, D * (m + 1))
        total = total + dot_nt(dqkv[:, cols], full[:, cols])
    dx_ref[:, 0] = total.astype(BF16).reshape(dx_ref.shape[0], dx_ref.shape[2], D)

    @pl.when(step == pl.num_programs(0) - 1)
    def _():
        write_gradient(
            functools.partial(qkv_block, acc), QKV_BLOCKS, part, meta[wins], dw_refs
        )


def normal_parts(u):
    size = jnp.abs(u)
    t = 1.0 / (1.0 + (0.3275911 * ROOT_HALF) * size)
    expo = jnp.exp(-0.5 * (u * u))
    poly = t * (
        0.5 * 0.254829592
        + t
        * (
            -0.5 * 0.284496736
            + t * (0.5 * 1.421413741 + t * (-0.5 * 1.453152027 + t * (0.5 * 1.061405429)))
        )
    )
    tail = poly * expo
    return jnp.where(u >= 0.0, 1.0 - tail, tail), expo


def norm_stats(rows):
    mean = jnp.mean(rows, axis=1, keepdims=True)
    centered = rows - mean
    spread = jnp.mean(centered * centered, axis=1, keepdims=True)
    inverse = lax.rsqrt(spread + NORM_EPS)
    return centered * inverse, inverse


def norm_back(d_rows, normal, inverse):
    mean_d = jnp.mean(d_rows, axis=1, keepdims=True)
    mean_dn = jnp.mean(d_rows * normal, axis=1, keepdims=True)
    return inverse * (d_rows - mean_d - normal * mean_dn)


def fill_ffn_matrices(w_out, w_up, w_down, packing, refs, core):
    side = D // BLK
    for base, offset, ref in each_piece(packing, refs, core):
        blocks, rows = ref.shape[:2]
        for n in range(blocks):
            full, i, j = ffn_place(base + n, (w_out, w_up, w_down))
            full[pl.ds(BLK * i + offset, rows), BLK * j : BLK * (j + 1)] = ref[n]


def ffn_place(b, matrices):
    side = D // BLK
    if b < side * side:
        return matrices[0], b // side, b % side
    b -= side * side
    if b < side * FF_CHUNKS:
        return matrices[1], b // FF_CHUNKS, b % FF_CHUNKS
    b -= side * FF_CHUNKS
    return matrices[2], b // side, b % side


def ffn_kernel(packing, wins, tokens, part, split, pieces, meta, *refs):
    cot_ref, x_ref, o_ref, vec = refs[:4]
    weight_refs = refs[4 : 4 + (2 * len(packing) or 1)]
    refs = refs[4 + len(weight_refs) :]
    out_refs, refs = refs[:pieces], refs[pieces:]
    da_ref, do_ref = refs[:2]
    refs = refs[2:]
    dw_refs, refs = refs[: 2 if split else 1], refs[2 if split else 1 :]
    vg_ref, w_out, w_up, w_down, acc_out, acc_up, acc_down, z_ref, gp_ref, du_ref, buf = refs
    step = pl.program_id(0)
    length = meta[step]
    accs = (acc_out, acc_up, acc_down)

    def acc_block(b, offset, rows):
        full, i, j = ffn_place(b, accs)
        if full is acc_down:
            i, j = j, i
        return full.at[pl.ds(BLK * i + offset, rows), BLK * j : BLK * (j + 1)]

    @pl.when(step == 0)
    def _():
        fill_ffn_matrices(w_out, w_up, w_down, packing, weight_refs, meta[wins])
        for acc in accs:
            acc[...] = jnp.zeros_like(acc)
        vg_ref[...] = jnp.zeros_like(vg_ref)

    def add_row(row, values, at=0):
        vg_ref[row : row + 1, at : at + values.shape[1]] += jnp.sum(
            values.astype(F32), axis=0, keepdims=True
        )

    bias_out, bias_down = vec[2:3, :], vec[7:8, :]
    gain_one, shift_one = vec[8:9, :], vec[9:10, :]
    gain_two, shift_two = vec[10:11, :], vec[11:12, :]
    attended = o_ref[0]
    mixed = x_ref[:, 0].reshape(WIN, D).astype(F32) + (dot_nn(attended, w_out[...]) + bias_out)
    n_one, inv_one = norm_stats(mixed)
    normed = n_one * gain_one + shift_one
    normed_low = normed.astype(BF16)
    for c in range(FF // D):
        cols = slice(D * c, D * (c + 1))
        u = dot_nn(normed_low, w_up[:, cols]) + vec[3 + c : 4 + c, :]
        phi, expo = normal_parts(u)
        z_ref[:, cols] = (u * phi).astype(BF16)
        gp_ref[:, cols] = phi + (u * expo) * DENSITY
    summed = normed + (dot_nn(z_ref[...], w_down[...]) + bias_down)
    n_two, inv_two = norm_stats(summed)
    result = (n_two * gain_two + shift_two).astype(BF16)
    if pieces == 1:
        out_ref = out_refs[0]
        out_ref[:, 0] = result.reshape(out_ref.shape[0], out_ref.shape[2], D)
    else:
        buf[...] = result
        for s, out_ref in enumerate(out_refs):
            rows = out_ref.shape[1]
            at = pl.multiple_of((meta[wins + 1] ^ s) * rows, rows)
            out_ref[0] = buf[pl.ds(at, rows), :]

    places = lax.broadcasted_iota(jnp.int32, (WIN, 1), 0)
    valid = jnp.where(places < length, 1.0 / tokens, 0.0).astype(F32)
    seed = cot_ref[:, 0].reshape(WIN, D).astype(F32) * valid
    add_row(10, seed * n_two)
    add_row(11, seed)
    d_summed = norm_back(seed * gain_two, n_two, inv_two)
    d_ff = d_summed.astype(BF16)
    add_row(7, d_ff)
    for c in range(FF // D):
        cols = slice(D * c, D * (c + 1))
        d_z = dot_nt(d_ff, w_down[cols, :])
        d_u = (d_z * gp_ref[:, cols]).astype(BF16)
        add_row(3 + c, d_u)
        du_ref[:, cols] = d_u
    d_ff_t = jnp.transpose(d_ff)
    normed_t = jnp.transpose(normed_low)
    for c in range(FF // D):
        cols = slice(D * c, D * (c + 1))
        acc_down[:, cols] += dot_nn(d_ff_t, z_ref[:, cols])
        acc_up[:, cols] += dot_nn(normed_t, du_ref[:, cols])
    d_normed = d_summed + dot_nt(du_ref[...], w_up[...])
    add_row(8, d_normed * n_one)
    add_row(9, d_normed)
    d_mixed = norm_back(d_normed * gain_one, n_one, inv_one)
    da_ref[0] = d_mixed
    d_branch = d_mixed.astype(BF16)
    add_row(2, d_branch)
    acc_out[...] += dot_nn(jnp.transpose(attended), d_branch)
    do_ref[0] = dot_nt(d_branch, w_out[...]).astype(BF16)

    @pl.when(step == pl.num_programs(0) - 1)
    def _():
        for j in range(D // BLK):
            for i in range(FF_CHUNKS):
                at = (slice(BLK * j, BLK * (j + 1)), slice(BLK * i, BLK * (i + 1)))
                acc_down[at] = jnp.transpose(acc_down[at])
        write_gradient(
            lambda b, offset, rows: acc_block(b, offset, rows)[...],
            REST_BLOCKS, part, meta[wins], dw_refs,
        )


def whole_spec(shape):
    zeros = (0,) * len(shape)
    return pl.BlockSpec(shape, lambda w, m: zeros, pipeline_mode=pl.Buffered(1))


def blocks_spec(part, count, at):
    lead = part.ndim - 3
    shape = part.shape[:lead] + (count,) + part.shape[lead + 1 :]
    return pl.BlockSpec(
        shape, lambda w, m: (0,) * lead + (at, 0, 0), pipeline_mode=pl.Buffered(1)
    )


def total_spec(shape):
    zeros = (0,) * len(shape)
    return pl.BlockSpec(shape, lambda w, m: zeros)


def window_spec(begin, *shape):
    zeros = (0,) * len(shape)
    return pl.BlockSpec((1,) + shape, lambda w, m: (begin + w,) + zeros)


def segment_spec(dp, seg):
    return pl.BlockSpec((dp, 1, seg, D), lambda w, m: (0, w, 0, 0))


def input_spec(dp, seg, begin):
    return pl.BlockSpec((dp, 1, seg, D), lambda w, m: (0, begin + w, 0, 0))


def gradient_outs(blocks, part):
    if part % 16:
        return [jax.ShapeDtypeStruct((blocks, BLK, BLK), BF16)]
    return [jax.ShapeDtypeStruct((blocks, BLK // 2, BLK), BF16)] * 2


def run_kernel(kernel, wins, meta, ins, outs, scratch, flops, moved):
    return pl.pallas_call(
        kernel,
        grid_spec=pltpu.PrefetchScalarGridSpec(
            num_scalar_prefetch=1,
            grid=(wins,),
            in_specs=[spec for _, spec in ins],
            out_specs=[spec for _, spec in outs],
            scratch_shapes=scratch,
        ),
        out_shape=[shape for shape, _ in outs],
        compiler_params=pltpu.CompilerParams(
            dimension_semantics=("arbitrary",), vmem_limit_bytes=56 * 1024 * 1024
        ),
        cost_estimate=pl.CostEstimate(
            flops=flops, bytes_accessed=moved, transcendentals=wins * WIN * FF
        ),
    )(meta, *[values for values, _ in ins])


def call_attention(wins, meta, x, packing, weight_parts, bias):
    dp, _, seg, _ = x.shape
    shape = jax.ShapeDtypeStruct
    return run_kernel(
        functools.partial(attention_kernel, packing, wins),
        wins,
        meta,
        [(x, input_spec(dp, seg, 0)), (bias, whole_spec(bias.shape))]
        + [(piece, whole_spec(piece.shape)) for piece in weight_parts],
        [
            (shape((wins, WIN, 3 * D), BF16), window_spec(0, WIN, 3 * D)),
            (shape((wins, WIN, D), BF16), window_spec(0, WIN, D)),
            (shape((wins, HEADS, WIN), F32), window_spec(0, HEADS, WIN)),
        ],
        [pltpu.VMEM((D, 3 * D), BF16), pltpu.VMEM((WIN, WIN), F32)],
        wins * 3_000_000_000,
        wins * 1_000_000,
    )


def call_ffn(wins, tokens, part, apart, meta, x, attended, packing, weight_parts, vec):
    dp, _, seg, _ = x.shape
    shape = jax.ShapeDtypeStruct
    counts = (QKV_BLOCKS, QKV_BLOCKS, 2 * QKV_BLOCKS, 2 * QKV_BLOCKS)
    ins = [
        (x, input_spec(dp, seg, wins)),
        (x, input_spec(dp, seg, 0)),
        (attended, window_spec(0, WIN, D)),
        (vec, whole_spec(vec.shape)),
    ] + [
        (piece, blocks_spec(piece, count, 0) if packing else whole_spec(piece.shape))
        for piece, count in zip(weight_parts, counts)
    ]
    outs = [(shape((dp, wins, seg, D), BF16), segment_spec(dp, seg))]
    if apart:
        outs = [(shape((wins, seg, D), BF16), window_spec(0, seg, D))] * dp
    return run_kernel(
        functools.partial(ffn_kernel, packing, wins, tokens, part, part % 16 == 0, dp if apart else 1),
        wins,
        meta,
        ins,
        [
            *outs,
            (shape((wins, WIN, D), F32), window_spec(0, WIN, D)),
            (shape((wins, WIN, D), BF16), window_spec(0, WIN, D)),
        ]
        + [(out, total_spec(out.shape)) for out in gradient_outs(REST_BLOCKS, part)]
        + [(shape((ROWS_VEC, D), F32), total_spec((ROWS_VEC, D)))],
        [
            pltpu.VMEM((D, D), BF16),
            pltpu.VMEM((D, FF), BF16),
            pltpu.VMEM((FF, D), BF16),
            pltpu.VMEM((D, D), F32),
            pltpu.VMEM((D, FF), F32),
            pltpu.VMEM((D, FF), F32),
            pltpu.VMEM((WIN, FF), BF16),
            pltpu.VMEM((WIN, FF), F32),
            pltpu.VMEM((WIN, FF), BF16),
            pltpu.VMEM((WIN, D), BF16),
        ],
        wins * 250_000_000,
        wins * 1_000_000,
    )


def call_attention_back(
    part, meta, packing, weight_parts, x, qkv, d_o, lse, d_mixed
):
    dp, _, seg, _ = x.shape
    wins = d_o.shape[0]
    shape = jax.ShapeDtypeStruct
    return run_kernel(
        functools.partial(attention_back_kernel, packing, wins, part, part % 16 == 0),
        wins,
        meta,
        [
            (x, input_spec(dp, seg, 0)),
            (qkv, window_spec(0, WIN, 3 * D)),
            (d_o, window_spec(0, WIN, D)),
            (lse, window_spec(0, HEADS, WIN)),
            (d_mixed, window_spec(0, WIN, D)),
        ]
        + [(piece, whole_spec(piece.shape)) for piece in weight_parts],
        [(shape((dp, wins, seg, D), BF16), segment_spec(dp, seg))]
        + [(out, total_spec(out.shape)) for out in gradient_outs(QKV_BLOCKS, part)]
        + [(shape((8, D), F32), total_spec((8, D)))],
        [
            pltpu.VMEM((D, 3 * D), BF16),
            pltpu.VMEM((WIN, WIN), F32),
            pltpu.VMEM((WIN, 3 * D), BF16),
            pltpu.VMEM((D, 3 * D), F32),
        ],
        wins * 30_000_000_000,
        wins * 8_000_000,
    )


def split_first_kernel(terms, bits, *refs):
    ins, outs = refs[:terms], refs[terms:]

    def total(side, at):
        return sum(ref[side, :, at].astype(F32) for ref in ins).astype(BF16)

    for y in range(2):
        for which in range(2):
            outs[which][:, y] = total(0, 2 * y + (bits[0] if which == 0 else 1 - bits[0]))
    for x in range(2):
        for which in range(2):
            outs[2 + which][:, x] = total(1, 2 * (bits[1] if which == 0 else 1 - bits[1]) + x)


def split_second_kernel(bits, *refs):
    for side in range(2):
        mine, got = refs[2 * side : 2 * side + 2]
        for which in range(2):
            bit = bits[1 - side]
            at = bit if which == 0 else 1 - bit
            refs[4 + 2 * side + which][...] = (
                mine[:, at].astype(F32) + got[:, at].astype(F32)
            ).astype(BF16)


def slabs_kernel(dp, me_ref, *refs):
    pairs, vec, outs, total = refs[: len(refs) - dp - 2], refs[-dp - 2], refs[-dp - 1 : -1], refs[-1]
    base = 0
    for n in range(0, len(pairs), 2):
        blocks = pairs[n].shape[0]
        total[base : base + blocks] = pairs[n][...].astype(F32) + pairs[n + 1][...].astype(F32)
        base += blocks
    owned = outs[0].shape[0] - 1
    for s in range(dp):
        slab = total[pl.ds((me_ref[0] ^ s) * owned, owned)]
        outs[s][:owned] = slab.astype(outs[s].dtype)
        outs[s][owned] = vec[...].astype(BF16).astype(outs[s].dtype)


def update_kernel(packing, scalars, *refs):
    count = 2 * len(packing)
    parts, root_parts, refs = refs[:count], refs[count : 2 * count], refs[2 * count :]
    own, left_stats, right_stats, left_roots, weights = refs[:5]
    left_new, right_new, weights_new, full, roots = refs[5:]
    fill_stack(full, packing, parts, scalars[0])
    fill_stack(roots, packing, root_parts, scalars[0])
    blocks, rows, _ = own.shape
    at = scalars[1] * rows
    lane = lax.broadcasted_iota(jnp.int32, (rows, BLK), 1)
    line = lax.broadcasted_iota(jnp.int32, (rows, BLK), 0)
    pick = jnp.where(lane == line + at, 1.0, 0.0).astype(BF16)
    for b in range(blocks):
        whole = full[b]
        crossed = dot_nt(jnp.concatenate([own[b], pick], axis=0), whole)
        left_new[b] = DECAY * left_stats[b] + (1.0 - DECAY) * crossed[:rows]
        turned = jnp.concatenate([left_roots[b].astype(BF16), crossed[rows:].astype(BF16)], axis=0)
        passed = dot_nn(turned, whole)
        right_new[b] = DECAY * right_stats[b] + (1.0 - DECAY) * passed[rows:]
        step = dot_nn(passed[:rows].astype(BF16), roots[b])
        weights_new[b] = weights[b] - MATRIX_RATE * step


def call_small(kernel, steps, scalars, ins, outs, scratch=(), room=14):
    def spec(shape, axis):
        if isinstance(axis, pl.BlockSpec):
            return axis
        block = tuple(n // steps if d == axis else n for d, n in enumerate(shape))
        return pl.BlockSpec(block, lambda g, m: tuple(g if d == axis else 0 for d in range(len(shape))))

    return pl.pallas_call(
        kernel,
        grid_spec=pltpu.PrefetchScalarGridSpec(
            num_scalar_prefetch=1,
            grid=(steps,),
            in_specs=[spec(values.shape, axis) for values, axis in ins],
            out_specs=[spec(shape.shape, axis) for shape, axis in outs],
            scratch_shapes=list(scratch),
        ),
        out_shape=[shape for shape, _ in outs],
        compiler_params=pltpu.CompilerParams(
            dimension_semantics=("arbitrary",), vmem_limit_bytes=room * 1024 * 1024
        ),
    )(scalars, *[values for values, _ in ins])


def update_blocks(scalars, packing, parts, root_parts, own, *shards):
    blocks = own.shape[0]
    out = jax.ShapeDtypeStruct(own.shape, F32)
    share = blocks // 2
    ats = (QKV_BLOCKS // share, QKV_BLOCKS // share, 2 * QKV_BLOCKS // share, 2 * QKV_BLOCKS // share)
    return call_small(
        functools.partial(update_kernel, packing),
        1,
        scalars,
        [(part, None) for part in parts]
        + [(part, blocks_spec(part, share, at)) for part, at in zip(root_parts, ats)]
        + [(values, None) for values in (own, *shards)],
        [(out, None)] * 3,
        [pltpu.VMEM((blocks, BLK, BLK), BF16)] * 2,
        24,
    )


def split_first(bits, *terms):
    blocks, height, cols = terms[0].shape
    half = blocks // 2
    view = (2, half, 4, height // 4, cols)
    out = jax.ShapeDtypeStruct((half, 2, height // 4, cols), BF16)
    return call_small(
        functools.partial(split_first_kernel, len(terms)),
        max(half // 3, 1),
        bits,
        [(term.reshape(view), 1) for term in terms],
        [(out, 0)] * 4,
    )


def split_second(bits, *parts):
    half, _, rows, cols = parts[0].shape
    out = jax.ShapeDtypeStruct((half, rows, cols), BF16)
    return call_small(
        split_second_kernel, 1, bits, [(part, 0) for part in parts], [(out, 0)] * 4
    )


def make_slabs(dp, me, parts, vec):
    _, rows, cols = parts[0].shape
    blocks = sum(part.shape[0] for part in parts) // 2
    shape = (blocks // dp + 1, rows, cols)
    return call_small(
        functools.partial(slabs_kernel, dp),
        1,
        me,
        [(part, None) for part in [*parts, vec]],
        [(jax.ShapeDtypeStruct(shape, F32 if s == 0 else BF16), None) for s in range(dp)],
        [pltpu.VMEM((blocks, rows, cols), F32)],
    )


def swap(values, axis, size, k):
    return lax.ppermute(values, axis, [(i, i ^ k) for i in range(size)])


def bits_of(size):
    return [1 << i for i in range(size.bit_length() - 1)]


def hop_orders(seq_count):
    high = [k for k in bits_of(seq_count) if k > 1]
    return (high, high[::-1])


def gather_hop(state, k, seq_count, seq_index, *marks):
    cur, lead = state
    got = after(swap(cur, "seq", seq_count, k), *marks)
    odd = (seq_index & k) != 0
    cur = jnp.stack([jnp.where(odd, got, cur), jnp.where(odd, cur, got)], axis=0)
    return cur, [k] + lead


def gather_end(state):
    cur, lead = state
    count = len(lead)
    blocks, rows, cols = cur.shape[count:]
    axes = [count] + [lead.index(k) for k in sorted(lead, reverse=True)] + [count + 1, count + 2]
    return cur.transpose(axes).reshape(blocks, rows << count, cols)


def halves(cur):
    half = cur.shape[0] // 2
    return [cur[:half], cur[half:]]


def gather_split(cur, seq_count, seq_index):
    done = []
    for part, order in zip(halves(cur), hop_orders(seq_count)):
        state = (part, [])
        for k in order + [1]:
            state = gather_hop(state, k, seq_count, seq_index)
        done.append(gather_end(state))
    return jnp.concatenate(done, axis=0)


def pack_weights(rows, roots, orders, seq_count, seq_index):
    states = [
        (jnp.concatenate(pair, axis=0), []) for pair in zip(halves(rows), halves(roots))
    ]
    for step in range(len(orders[0])):
        states = [
            gather_hop(state, order[step], seq_count, seq_index)
            for state, order in zip(states, orders)
        ]
        if step == 0:
            cur, lead = states[0]
            axis = len(lead)
            states = [
                (lax.slice_in_dim(cur, 0, QKV_BLOCKS, axis=axis), lead),
                (lax.slice_in_dim(cur, QKV_BLOCKS, cur.shape[axis], axis=axis), lead),
                states[1],
            ]
            orders = (orders[0], orders[0], orders[1])
    return states


def join_cores(states, seq_count, seq_index, *marks):
    if states[0][0].shape[-2] % 16:
        states = [gather_hop(state, 1, seq_count, seq_index) for state in states]
        return (), [jnp.concatenate([gather_end(state) for state in states], axis=0)]
    parts = []
    for cur, _ in states:
        parts += [cur, after(swap(cur, "seq", seq_count, 1), *marks)]
    return tuple(tuple(lead) for _, lead in states), parts


def scatter_first(whole, seq_count, seq_index):
    left = sorted(bits_of(seq_count), reverse=True)
    blocks, height, cols = whole.shape
    rows = height // seq_count
    cur = whole.reshape(blocks, seq_count // 2, 2, rows, cols)
    mine, other = [
        lax.dynamic_index_in_dim(cur, bit, 2, keepdims=False)
        for bit in (seq_index % 2, 1 - seq_index % 2)
    ]
    cur = mine.astype(F32) + swap(other, "seq", seq_count, 1).astype(F32)
    left.remove(1)
    cur = cur.astype(BF16).reshape([blocks] + [2] * len(left) + [rows, cols])
    return [(half, left) for half in halves(cur)]


def scatter_hop(state, k, seq_count, seq_index, *marks):
    cur, left = state
    axis = 1 + left.index(k)
    bit = (seq_index // k) % 2
    mine = lax.dynamic_index_in_dim(cur, bit, axis, keepdims=False)
    other = lax.dynamic_index_in_dim(cur, 1 - bit, axis, keepdims=False)
    got = after(swap(other, "seq", seq_count, k), *marks)
    cur = (mine.astype(F32) + got.astype(F32)).astype(BF16)
    return cur, [b for b in left if b != k]


def after(values, *marks):
    if not marks:
        return values
    return lax.optimization_barrier((values, marks))[0]


def body(
    inputs,
    cotangent,
    lengths,
    weights,
    vectors,
    positions,
    left_stats,
    right_stats,
    left_roots,
    right_roots,
    vector_second,
    position_second,
):
    seq_count = lax.axis_size("seq")
    dp_count = lax.axis_size("dp")
    seq_index = lax.axis_index("seq")
    dp_index = lax.axis_index("dp")
    micro, wins_dev, segment, model_width = inputs.shape
    wins = wins_dev // dp_count
    total_tokens = micro * wins_dev * seq_count * segment * dp_count
    owned, row_part, _ = weights.shape
    def exchange(rows):
        return lax.all_to_all(rows, "dp", 0, 0, tiled=True)

    grouped = (dp_count, wins, segment, model_width)
    own = weights.astype(BF16)
    orders = hop_orders(seq_count)
    hops = len(orders[0])

    def scatter_both(states, step, *marks):
        return [
            scatter_hop(state, order[step], seq_count, seq_index, *marks)
            for state, order in zip(states, orders)
        ]

    vec = vectors.reshape(-1, D)
    bias_qv = jnp.concatenate([vec[0:2], jnp.zeros((6, D), F32)], axis=0)
    vec_pad = jnp.concatenate([vec, jnp.zeros((ROWS_VEC - vec.shape[0], D), F32)], axis=0)

    metas = [
        lax.dynamic_index_in_dim(
            lengths[i].reshape(dp_count, wins), dp_index, 0, keepdims=False
        )
        for i in range(micro)
    ]
    metas = [
        jnp.concatenate([lens, (seq_index % 2)[None], dp_index[None]]).astype(jnp.int32)
        for lens in metas
    ]
    shards = [own] + [swap(own, "dp", dp_count, s) for s in range(1, dp_count)]
    weight_rows = jnp.concatenate(
        [lax.select_n(dp_index ^ j, *shards) for j in range(dp_count)], axis=0
    )
    pairs = [
        jnp.concatenate(
            [
                (inputs[i].astype(F32) + positions[None]).astype(BF16).reshape(grouped),
                cotangent[i].reshape(grouped),
            ],
            axis=1,
        )
        for i in range(micro)
    ]
    taken = [exchange(after(pairs[0], *shards[1:]))]
    roots_low = right_roots.astype(BF16)
    groups = pack_weights(weight_rows, roots_low, orders, seq_count, seq_index)
    cur, lead = groups[0]
    groups[0] = (after(cur, vec_pad, bias_qv, roots_low, *metas), lead)
    packing_qkv, parts_qkv = join_cores(groups[:1], seq_count, seq_index)
    for i in range(1, micro):
        marks = (taken[-1], *metas, *parts_qkv, *(cur for cur, _ in groups[1:]))
        taken.append(exchange(after(pairs[i], *marks)))
    ffn, out_got, dx_got = [], [], []
    forward = [
        call_attention(wins, metas[0], taken[0], packing_qkv, parts_qkv, bias_qv)
    ]
    mark = (forward[0][2],)
    lse = forward[0][2]
    packing_rest, parts_rest = join_cores(groups[1:], seq_count, seq_index, lse)
    share = owned // 2
    if not packing_rest:
        (stack,) = parts_rest
        middle = QKV_BLOCKS + share
        roots_full = jnp.concatenate([stack[QKV_BLOCKS:middle], stack[-share:]], axis=0)
        parts_rest = [jnp.concatenate([stack[:QKV_BLOCKS], stack[middle:-share]], axis=0)]
    fast = seq_count == 8 and row_part % 16 == 0
    bits = jnp.stack([(seq_index // 2) % 2, (seq_index // 4) % 2]).astype(jnp.int32)

    def over_cores(parts, *marks):
        keep, send = parts
        return [keep, after(swap(send, "seq", seq_count, 1), *marks)]

    def hop(parts, count, *marks):
        mine_a, send_a, mine_b, send_b = parts
        k_a, k_b = (2, 4) if count == 0 else (4, 2)
        got_a = after(swap(send_a, "seq", seq_count, k_a), *marks)
        got_b = after(swap(send_b, "seq", seq_count, k_b), *marks)
        return [mine_a, got_a, mine_b, got_b]

    vec_sums = jnp.zeros((ROWS_VEC, D), F32)
    dw_rest, dw_qkv = [], []
    for i in range(micro):
        if i > 0:
            forward.append(
                call_attention(
                    wins, after(metas[i], *mark), taken[i], packing_qkv, parts_qkv, bias_qv
                )
            )
            mark = (forward[i][2],)
        results = call_ffn(
            wins, total_tokens, row_part, True, after(metas[i], *mark), taken[i], forward[i][1],
            packing_rest, parts_rest, vec_pad,
        )
        out, (d_mixed, d_o, *dw, vg) = results[:dp_count], results[dp_count:]
        got = [out[0]] + [swap(out[s], "dp", dp_count, s) for s in range(1, dp_count)]
        out_got.append(tuple(got))
        ffn.append((d_mixed, d_o))
        vec_sums = vec_sums + vg
        mark = (vg,)
        dw_rest.append(dw)
    gates = mark + (out_got[0],)
    rest_core, qkv_core = [], []
    for i in range(micro):
        dx, *dw, db = call_attention_back(
            row_part, after(metas[i], gates), packing_qkv, parts_qkv, taken[i], forward[i][0],
            ffn[i][1], forward[i][2], ffn[i][0],
        )
        vec_sums = vec_sums + jnp.concatenate([db, jnp.zeros_like(db)], axis=0)
        dw_qkv.append(dw)
        gates = (db,) + tuple(out_got[1:])
        if fast and i == 0:
            for n in range(micro):
                rest_core += over_cores(dw_rest[n], *(mark[:1] if n == 0 else (db,)))
            rest = split_first(bits, *rest_core)
            gates = gates + tuple(rest)
        if fast and i == micro - 1:
            rest = hop(rest, 0, db)
            qkv_core += over_cores(dw_qkv[0], db)
            dx = after(dx, *rest)
        dx_got.append(exchange(after(dx, *dx_got[-1:])))

    whole = (wins_dev, segment, model_width)
    out_got = [
        jnp.stack([lax.select_n(dp_index ^ e, *got) for e in range(dp_count)]) for got in out_got
    ]
    layer_out = jnp.stack([got.reshape(whole) for got in out_got], axis=0)

    for k in bits_of(seq_count):
        vec_sums = vec_sums + swap(vec_sums, "seq", seq_count, k)
    if fast:
        qkv_core += over_cores(dw_qkv[1])
        rest = split_second(bits, *rest)
        states = split_first(after(bits, *rest), *qkv_core)
        rest = hop(rest, 1)
        states = hop(split_second(bits, *hop(states, 0)), 1)
        slabs = make_slabs(
            dp_count, after(dp_index[None].astype(jnp.int32), dx_got[-1], layer_out), states + rest,
            vec_sums.reshape(row_part, BLK),
        )
    else:
        states = []
        for parts in (dw_qkv, dw_rest):
            total = sum(part[0].astype(F32) for part in parts).astype(BF16)
            group = scatter_first(total, seq_count, seq_index)
            for step in range(hops):
                group = scatter_both(group, step)
            states += group
        joined = jnp.concatenate([cur for cur, _ in states], axis=0)
        joined = joined.reshape((dp_count, owned) + joined.shape[1:])
        vec_rows = vec_sums.astype(BF16).reshape(-1, row_part, BLK)
        slabs = [
            jnp.concatenate(
                [lax.dynamic_index_in_dim(joined, dp_index ^ s, 0, keepdims=False), vec_rows]
            )
            for s in range(dp_count)
        ]
    slabs = [slabs[0].astype(F32)] + [
        swap(slabs[s], "dp", dp_count, s).astype(F32) for s in range(1, dp_count)
    ]
    grad_rows = sum(slab[:owned] for slab in slabs)
    vec_sums = sum(lax.select_n(dp_index ^ j, *[slab[owned:] for slab in slabs]) for j in range(dp_count))
    vec_sums = vec_sums.reshape(ROWS_VEC, D)
    grad_low = grad_rows.astype(BF16)
    if fast:
        states = [(part, []) for part in halves(grad_low)]
        for step in range(hops):
            states = [
                gather_hop(state, order[step], seq_count, seq_index)
                for state, order in zip(states, orders)
            ]
        packing, parts = join_cores(states, seq_count, seq_index)
        left_new, right_new, weights_new = update_blocks(
            jnp.stack([seq_index % 2, seq_index]).astype(jnp.int32), packing, parts, parts_rest,
            grad_low, left_stats, right_stats, left_roots, weights,
        )
    else:
        grad_full = gather_split(grad_low, seq_count, seq_index)
        row_start = seq_index * row_part

        def batched(spec, left, right):
            return jnp.einsum(spec, left, right, preferred_element_type=F32)

        left_new = DECAY * left_stats + (1.0 - DECAY) * batched("bij,bkj->bik", grad_low, grad_full)
        column_part = lax.dynamic_slice_in_dim(grad_full, row_start, row_part, 2)
        right_new = DECAY * right_stats + (1.0 - DECAY) * batched(
            "bki,bkj->bij", column_part, grad_full
        )
        left_applied = batched("bij,bjk->bik", left_roots.astype(BF16), grad_full)
        step_rows = batched("bij,bjk->bik", left_applied.astype(BF16), roots_full)
        weights_new = weights - MATRIX_RATE * step_rows

    place_sum = sum(jnp.sum(got.astype(F32), axis=(0, 1)) for got in dx_got)
    for k in bits_of(seq_count):
        low = place_sum.astype(BF16)
        place_sum = low.astype(F32) + swap(low, "seq", seq_count, k).astype(F32)
    vector_grads = vec_sums[: vec.shape[0]].reshape(-1)
    vector_second_new = DECAY * vector_second + (1.0 - DECAY) * vector_grads * vector_grads
    vectors_new = vectors - VECTOR_RATE * vector_grads / (jnp.sqrt(vector_second_new) + ROOT_EPS)
    position_grads = place_sum
    position_second_new = DECAY * position_second + (1.0 - DECAY) * position_grads * position_grads
    positions_new = positions - VECTOR_RATE * position_grads / (
        jnp.sqrt(position_second_new) + ROOT_EPS
    )
    return (
        layer_out,
        jnp.stack([got.astype(F32).reshape(whole) for got in dx_got], axis=0),
        grad_rows,
        left_new,
        right_new,
        weights_new,
        vector_grads,
        vector_second_new,
        vectors_new,
        position_grads,
        position_second_new,
        positions_new,
    )


def solution(mesh):
    rows = P(None, "seq", "dp", None)
    blocks = P("dp", "seq", None)
    in_specs = (
        rows, rows, P(None, "seq"), blocks, P(), P("dp", None),
        blocks, blocks, blocks, blocks, P(), P("dp", None),
    )
    out_specs = (
        rows, rows, blocks, blocks, blocks, blocks,
        P(), P(), P(), P("dp", None), P("dp", None), P("dp", None),
    )
    return jax.shard_map(body, mesh=mesh, in_specs=in_specs, out_specs=out_specs, check_vma=False)
```
